256 devices in a mesh: dp: 8 (over x, core), expert: 4 (over z_hi), shard: 8 (over y, z_lo).
Axes of the slice: x: 4, y: 4, z: 8 (z_hi: 4, z_lo: 2; z = z_hi * 2 + z_lo), core: 2. Of those that a mesh axis runs over, the one named last changes fastest.
Arguments:
- tokens: bfloat16 [4096, 4096], P(('dp', 'expert'), 'shard'), may hold values from -6 to 6
- expert_ids: int32 [4096, 2], P(('dp', 'expert')), may hold values from 0 to 3, all different within a row; in each aligned block of 128 rows (0 to 127, 128 to 255, ...) at most 80 rows name the same one
- gate_probs: float32 [4096, 2], P(('dp', 'expert')), may hold values from 0.1 to 1
- stacked_weights: bfloat16 [4, 3, 1536, 4096], P('expert', None, 'shard', 'dp'), may hold values from -0.09375 to 0.09375
- out_grad: bfloat16 [4096, 4096], P(('dp', 'expert'), 'shard'), may hold values from -6 to 6
Outputs:
- layer_output: bfloat16 [4096, 4096], P(('dp', 'expert'), 'shard')
- token_grad: bfloat16 [4096, 4096], P(('dp', 'expert'), 'shard')
- prob_grad: float32 [4096, 2], P(('dp', 'expert'))
- weight_grad: float32 [4, 3, 1536, 4096], P('expert', None, 'shard', 'dp')
The draws below stay inside these ranges and needn't reach their ends.
Inputs may be any that keep to these rules, and one draw needn't show every extreme that they name: `expert_ids`: within each aligned block of 128 rows (the tokens of one index of dp and expert) no expert is named by more than 80 rows, a bound that some block reaches; the 2 ids of a row differ.
All inputs are finite; a program needn't handle non-finite values.
Results may differ from the reference program's by a relative error of at most 0.0065.
Values may be sent and summed in bfloat16 or wider, within the bound.
No kernel may reach another device: no remote copies, remote signals or barrier semaphores. Data moves between devices by JAX's collectives and lax.ppermute only.
A program may use at most 128 MiB of HBM per device.

```python
import math
import jax
import jax.numpy as jnp
import numpy as np

D = 4096
H = 1536
TOPK = 2
TOK_DEV = 128
EXPERTS = 4
CAP = 80
TOKENS = 4096


def block_scale(own_key, dims, shards, low, top_value):
    gain, own = 1.0, jax.random.fold_in(own_key, 6)
    for axis_at, parts in shards:
        draws = jnp.exp(jax.random.uniform(jax.random.fold_in(own, axis_at), (parts,), jnp.float32, low / len(shards), top_value / len(shards)))
        gain = gain * jnp.repeat(draws, dims[axis_at] // parts).reshape([-1 if axis == axis_at else 1 for axis in range(len(dims))])
    return gain


def assign_block(key, own, number, rows, count, top, most, lean):
    sequence = jax.random.permutation(key, count)
    crowded, usual = portions_of(count, rows * top, most, lean, True), portions_of(count, rows * top, most, lean, False)
    places = jnp.arange(count)

    def named(tallies, rotation):
        used = int((tallies > 0).sum())
        fixed = max(1, used // 4)
        shifted = fixed + (places - fixed + rotation * (used - fixed)) % max(1, count - fixed)
        return jnp.zeros((count,), jnp.int32).at[sequence[jnp.where(places < fixed, places, shifted)]].set(jnp.asarray(tallies, jnp.int32))

    tallies = jnp.where(number % 4 == 0, named(crowded, number // 4), named(usual, number - number // 4 - 1))
    mixed = jax.random.permutation(jax.random.fold_in(own, 3), count)
    source_of, taker = mixed[0:count // 2 * 2:2], mixed[1:count // 2 * 2:2]
    room = jnp.minimum(tallies[source_of] - 1, most - tallies[taker]) // 2
    room = jnp.where((source_of == sequence[0]) | (taker == sequence[0]) | (tallies[taker] == 0), 0, jnp.maximum(room, 0))
    shifted = jax.random.randint(jax.random.fold_in(own, 4), (count // 2,), 0, 1 << 20) % (room + 1)
    tallies = tallies.at[source_of].add(-shifted).at[taker].add(shifted)
    labels = jnp.searchsorted(jnp.cumsum(tallies), jnp.arange(rows * top), side="right").astype(jnp.int32)
    listing = labels.reshape(top, rows).T
    listing = listing[jax.random.permutation(jax.random.fold_in(own, 1), rows)]
    rotation = jax.random.randint(jax.random.fold_in(own, 2), (rows, 1), 0, top)
    return jnp.take_along_axis(listing, (jnp.arange(top)[None, :] + rotation) % top, axis=1)


def portions_of(count, total, reach, skew, full):
    weights = [(1 << 20) // math.isqrt(grade ** skew) + 1 for grade in range(1, count + 1)]
    largest = reach if full else min(reach, max(-(-total // count), total * weights[0] // sum(weights)))
    least = 1 if total - largest >= count - 1 else 0
    given, rest = [largest] + [least] * (count - 1), total - largest - least * (count - 1)
    while rest > 0:
        free = [i for i in range(1, count) if given[i] < largest] or [i for i in range(1, count) if given[i] < reach]
        whole, budget = sum([weights[i] for i in free]), rest
        for i in free:
            more = min(reach - given[i], max(1, budget * weights[i] // whole), rest)
            given[i] = given[i] + more
            rest = rest - more
    return np.array(given)


def normal_values(rng, shape, spread, reach, pieces=(), kind=jnp.bfloat16):
    gain = block_scale(rng, shape, pieces, -0.22, 0.18) if pieces else 1.0
    entries = jax.random.normal(rng, shape, jnp.float32) * spread * gain
    return jnp.minimum(jnp.maximum(entries, -reach), reach).astype(kind)


def setup_inputs(seed: int = 0) -> dict:
    keys = jax.random.split(jax.random.key(seed), 6)
    tokens = normal_values(keys[0], (TOKENS, D), 1.0, 6.0, ((0, 32), (1, 8)))
    expert_ids_keys = jax.random.split(jax.random.fold_in(keys[1], 1), TOKENS // TOK_DEV)
    expert_ids_turns = jax.random.permutation(jax.random.fold_in(keys[1], 3), TOKENS // TOK_DEV)
    expert_ids = jax.vmap(lambda own, number: assign_block(jax.random.fold_in(keys[1], 2), own, number, TOK_DEV, EXPERTS, TOPK, CAP, 1))(expert_ids_keys, expert_ids_turns).reshape((TOKENS, TOPK))
    gate_probs = jnp.clip(0.1 + 0.9 * jax.random.uniform(keys[2], (TOKENS, TOPK), jnp.float32) ** block_scale(keys[2], (TOKENS, TOPK), ((0, 32),), -0.2, 0.2), 0.1, 1.0)
    stacked_weights = normal_values(keys[3], (EXPERTS, 3, H, D), D ** -0.5, 0.09375, ((0, 4), (2, 8), (3, 8)))
    out_grad = normal_values(keys[4], (TOKENS, D), 1.0, 6.0, ((0, 32), (1, 8)))
    return {"tokens": tokens, "expert_ids": expert_ids, "gate_probs": gate_probs, "stacked_weights": stacked_weights, "out_grad": out_grad}


def expert_pass(token_rows, routed_rows, weights):
    w_gate = weights[0]
    w_up = weights[1]
    w_down = weights[2]
    gate_proj = jnp.dot(token_rows, w_gate.T, preferred_element_type=jnp.float32)
    up_proj = jnp.dot(token_rows, w_up.T, preferred_element_type=jnp.float32)
    sigmoid_gate = jax.nn.sigmoid(gate_proj)
    swish_gate = gate_proj * sigmoid_gate
    activation = (swish_gate * up_proj).astype(jnp.bfloat16)
    output_rows = jnp.dot(activation, w_down, preferred_element_type=jnp.float32).astype(jnp.bfloat16)
    activation_grad = jnp.dot(routed_rows, w_down.T, preferred_element_type=jnp.float32)
    gate_grad = (activation_grad * up_proj * sigmoid_gate * (1.0 + gate_proj * (1.0 - sigmoid_gate))).astype(jnp.bfloat16)
    up_grad = (activation_grad * swish_gate).astype(jnp.bfloat16)
    input_rows = (jnp.dot(gate_grad, w_gate, preferred_element_type=jnp.float32)
                  + jnp.dot(up_grad, w_up, preferred_element_type=jnp.float32)).astype(jnp.bfloat16)
    weight_terms = jnp.stack([
        jnp.dot(gate_grad.T, token_rows, preferred_element_type=jnp.float32),
        jnp.dot(up_grad.T, token_rows, preferred_element_type=jnp.float32),
        jnp.dot(activation.T, routed_rows, preferred_element_type=jnp.float32)])
    return output_rows, input_rows, weight_terms


def reference(tokens, expert_ids, gate_probs, stacked_weights, out_grad):
    blocks = TOKENS // TOK_DEV
    pair_count = TOK_DEV * TOPK
    assign = expert_ids.reshape(blocks, pair_count)
    onehot = (assign[:, :, None] == jnp.arange(EXPERTS, dtype=jnp.int32)[None, None, :]).astype(jnp.int32)
    before = jnp.cumsum(onehot, axis=1, dtype=jnp.int32) - onehot
    position = jnp.sum(before * onehot, axis=2, dtype=jnp.int32)
    block_base = (jnp.arange(blocks, dtype=jnp.int32) * CAP)[:, None]
    slot_index = (block_base + position).reshape(-1).astype(jnp.int32)
    flat_ids = assign.reshape(-1)
    token_pairs = jnp.repeat(tokens, TOPK, axis=0)
    pair_probs = gate_probs.reshape(-1)
    routed = (pair_probs[:, None] * jnp.repeat(out_grad, TOPK, axis=0).astype(jnp.float32)).astype(jnp.bfloat16)
    buffer_rows = blocks * CAP
    out_pairs = jnp.zeros((TOKENS * TOPK, D), jnp.float32)
    input_pairs = jnp.zeros((TOKENS * TOPK, D), jnp.float32)
    weight_list = []
    for expert in range(EXPERTS):
        matched = flat_ids == expert
        target = jnp.where(matched, slot_index, buffer_rows).astype(jnp.int32)
        token_rows = jnp.zeros((buffer_rows, D), jnp.bfloat16).at[target].set(token_pairs, mode="drop")
        routed_rows = jnp.zeros((buffer_rows, D), jnp.bfloat16).at[target].set(routed, mode="drop")
        output_rows, input_rows, weight_terms = expert_pass(token_rows, routed_rows, stacked_weights[expert])
        picked = jnp.minimum(target, buffer_rows - 1).astype(jnp.int32)
        out_pairs = out_pairs + jnp.where(matched[:, None], output_rows[picked].astype(jnp.float32), 0.0)
        input_pairs = input_pairs + jnp.where(matched[:, None], input_rows[picked].astype(jnp.float32), 0.0)
        weight_list.append(weight_terms)
    out_pairs = out_pairs.reshape(TOKENS, TOPK, D)
    layer_output = jnp.sum(gate_probs[:, :, None] * out_pairs, axis=1).astype(jnp.bfloat16)
    prob_grad = jnp.sum(out_grad.astype(jnp.float32)[:, None, :] * out_pairs, axis=2)
    token_grad = jnp.sum(input_pairs.reshape(TOKENS, TOPK, D), axis=1).astype(jnp.bfloat16)
    weight_grad = jnp.stack(weight_list)
    return layer_output, token_grad, prob_grad, weight_grad
```

```python
import jax
import jax.numpy as jnp
from jax import lax
from jax.experimental import pallas as pl
from jax.experimental.pallas import tpu as pltpu
from jax.sharding import Mesh, PartitionSpec as P

F32 = jnp.float32
BF16 = jnp.bfloat16
CAP = 80
PARAMS = pltpu.CompilerParams(vmem_limit_bytes=48 * 1024 * 1024)


def nn(a, b):
    return lax.dot_general(a, b, (((1,), (0,)), ((), ())), preferred_element_type=F32)


def nt(a, b):
    return lax.dot_general(a, b, (((1,), (1,)), ((), ())), preferred_element_type=F32)


def tn(a, b):
    return lax.dot_general(a, b, (((0,), (0,)), ((), ())), preferred_element_type=F32)


def call(kernel, place, args, outs, scratch=()):
    whole = pl.BlockSpec(memory_space=pltpu.VMEM)
    return pl.pallas_call(
        kernel,
        out_shape=[jax.ShapeDtypeStruct(shape, kind) for shape, kind in outs],
        in_specs=[pl.BlockSpec(memory_space=pltpu.SMEM)] + [whole] * len(args),
        out_specs=[whole] * len(outs),
        scratch_shapes=[pltpu.VMEM(shape, kind) for shape, kind in scratch],
        compiler_params=PARAMS,
    )(place, *args)


def slots_kernel(place, ids, probs, tokens, grads, placing, *outs):
    rows = ids.shape[1]
    group = place[0]
    first, second = ids[0:1, :], ids[1:2, :]
    before = (
        lax.broadcasted_iota(jnp.int32, (rows, rows), 0)
        < lax.broadcasted_iota(jnp.int32, (rows, rows), 1)
    ).astype(BF16)
    slot = lax.broadcasted_iota(jnp.int32, (CAP, rows), 0)
    for k in range(4):
        expert = lax.rem(group + k, 4)
        named = jnp.logical_or(first == expert, second == expert)
        marks = jnp.broadcast_to(named, (8, rows)).astype(F32)
        position = nn(marks.astype(BF16), before)[0:1, :].astype(jnp.int32)
        weight = jnp.where(first == expert, probs[0:1, :], probs[1:2, :])
        chosen = jnp.logical_and(
            jnp.broadcast_to(marks[0:1, :] > 0.5, (CAP, rows)),
            slot == jnp.broadcast_to(position, (CAP, rows)),
        )
        hot = chosen.astype(F32).astype(BF16)
        placing[k * CAP : (k + 1) * CAP, :] = hot
        scale = jnp.sum(jnp.where(chosen, weight, 0.0), axis=1, keepdims=True)
        outs[k][...] = nn(hot, tokens[...]).astype(BF16)
        outs[4 + k][...] = (scale * nn(hot, grads[...])).astype(BF16)


def gate_up_kernel(place, *refs):
    rows, own, other = refs[0:4], refs[4:8], refs[8:12]
    keep, send, turned, total = refs[12:16]
    x, y, zl = place[1], place[2], place[3]
    for j in range(4):
        turned[lax.rem(x - y + j + 4, 4)] = rows[j][...]
    for m in range(2):
        for h, half in enumerate((own, other)):
            acc = nt(turned[0], half[0][m])
            for i in range(1, 4):
                acc += nt(turned[i], half[i][m])
            total[2 * m + h] = acc
    part = keep.shape[1]
    mine = pl.multiple_of(zl * part, 32)
    theirs = pl.multiple_of((1 - zl) * part, 32)
    for n in range(keep.shape[0]):
        keep[n] = total[n, pl.ds(mine, part), :]
        send[n] = total[n, pl.ds(theirs, part), :].astype(BF16)


def back_kernel(place, *refs):
    rows, own, other = refs[0:4], refs[4:8], refs[8:12]
    keep, send, turned, total = refs[12:16]
    x, y, zl = place[1], place[2], place[3]
    for j in range(4):
        turned[lax.rem(x - y + j + 4, 4)] = rows[j][...]
    for h, half in enumerate((own, other)):
        acc = nt(turned[0], half[0][...])
        for i in range(1, 4):
            acc += nt(turned[i], half[i][...])
        total[h] = acc
    part = keep.shape[1]
    mine = pl.multiple_of(zl * part, 32)
    theirs = pl.multiple_of((1 - zl) * part, 32)
    for n in range(keep.shape[0]):
        keep[n] = total[n, pl.ds(mine, part), :]
        send[n] = total[n, pl.ds(theirs, part), :].astype(BF16)


def join(target, mine, theirs, zl):
    part = mine.shape[-2]
    target[pl.ds(pl.multiple_of(zl * part, 32), part), :] = mine[...]
    target[pl.ds(pl.multiple_of((1 - zl) * part, 32), part), :] = theirs[...]


def output_kernel(place, *refs):
    act, act_far, own, other = refs[0], refs[1], refs[2:6], refs[6:10]
    outs, joined, turned = refs[10:14], refs[14], refs[15]
    x, y, zl = place[1], place[2], place[3]
    for n in range(2):
        join(joined.at[n], act.at[n], act_far.at[n], zl)
    for i in range(4):
        spot = lax.rem(y - x + i + 4, 4)
        turned[0, spot] = own[i][...]
        turned[1, spot] = other[i][...]
    for j in range(4):
        acc = nn(joined[0], turned[0, j]) + nn(joined[1], turned[1, j])
        outs[j][...] = acc.astype(outs[j].dtype)


def input_kernel(place, *refs):
    grad, grad_far, own, other = refs[0], refs[1], refs[2:6], refs[6:10]
    outs, joined, turned = refs[10:14], refs[14], refs[15]
    x, y, zl = place[1], place[2], place[3]
    for n in range(4):
        join(joined.at[n], grad.at[n], grad_far.at[n], zl)
    for i in range(4):
        spot = lax.rem(y - x + i + 4, 4)
        for m in range(2):
            turned[2 * m, spot] = own[i][m]
            turned[2 * m + 1, spot] = other[i][m]
    for j in range(4):
        acc = nn(joined[0], turned[0, j])
        for n in range(1, 4):
            acc += nn(joined[n], turned[n, j])
        outs[j][...] = acc.astype(outs[j].dtype)


def weight_kernel(place, *refs):
    act, act_far, grad, grad_far = refs[0:4]
    rows, routed = refs[4:8], refs[8:12]
    keeps, sends = refs[12:16], refs[16:20]
    joined, turned = refs[20], refs[21]
    x, y, zl = place[1], place[2], place[3]
    for n in range(4):
        join(joined.at[n], grad.at[n], grad_far.at[n], zl)
    for n in range(2):
        join(joined.at[4 + n], act.at[n], act_far.at[n], zl)
    for j in range(4):
        spot = lax.rem(x - y + j + 4, 4)
        turned[0, spot] = rows[j][...]
        turned[1, spot] = routed[j][...]
    for i in range(4):
        for m in range(3):
            block = turned[1 if m == 2 else 0, i]
            keeps[i][m] = tn(joined[2 * m], block)
            sends[i][m] = tn(joined[2 * m + 1], block).astype(BF16)


def spread_rows(ids, place, placing, blocks):
    for k in range(4):
        dense = tn(placing[k * CAP : (k + 1) * CAP, :], blocks[k][...])
        yield ids == lax.rem(place[0] + k, 4), dense


def layer_kernel(place, ids, probs, grads, placing, *refs):
    blocks, out, part = refs[0:4], refs[4], refs[5]
    total = jnp.zeros(out.shape, F32)
    shares = jnp.zeros(part.shape, F32)
    cotangent = grads[...].astype(F32)
    for named, dense in spread_rows(ids[...], place, placing, blocks):
        weight = jnp.sum(jnp.where(named, probs[...], 0.0), axis=1, keepdims=True)
        total += weight * dense
        share = jnp.sum(cotangent * dense, axis=1, keepdims=True)
        shares += jnp.where(named, share, 0.0)
    out[...] = total.astype(BF16)
    part[...] = shares


def token_kernel(place, placing, *refs):
    blocks, out = refs[0:4], refs[4]
    total = jnp.zeros(out.shape, F32)
    for k in range(4):
        total += tn(placing[k * CAP : (k + 1) * CAP, :], blocks[k][...])
    out[...] = total.astype(BF16)


def shift(value, axis, step):
    return lax.ppermute(value, axis, [(i, (i + step) % 4) for i in range(4)])


def swap(value, axis):
    return lax.ppermute(value, axis, [(0, 1), (1, 0)])


def turn(value):
    return lax.ppermute(value, ("core", "zl"), [(2 * c + z, 2 * z + c) for c in range(2) for z in range(2)])


def body(tokens, expert_ids, gate_probs, stacked_weights, out_grad):
    rows, width = tokens.shape
    hidden = stacked_weights.shape[2]
    slots = 4 * CAP
    part = slots // 2
    place = jnp.stack(
        [lax.axis_index(name) for name in ("expert", "x", "y", "zl")]
    ).astype(jnp.int32)

    turned = turn(stacked_weights[0])
    pair, down = turned[0:2], turned[2]
    pair_own = [pair] + [shift(pair, "x", i) for i in (1, 2, 3)]
    down_own = [down] + [shift(down, "x", i) for i in (1, 2, 3)]
    pair_other = [swap(block, "core") for block in pair_own]
    down_other = [swap(block, "core") for block in down_own]

    placed = call(
        slots_kernel,
        place,
        [expert_ids.T, gate_probs.T, tokens, out_grad],
        [((slots, rows), BF16)] + [((CAP, width), BF16)] * 8,
    )
    placing = placed[0]
    token_rows = jnp.concatenate(
        [placed[1]] + [shift(placed[1 + k], "expert", k) for k in (1, 2, 3)], axis=0
    )
    routed_rows = jnp.concatenate(
        [placed[5]] + [shift(placed[5 + k], "expert", k) for k in (1, 2, 3)], axis=0
    )
    token_rows = [token_rows] + [shift(token_rows, "y", j) for j in (1, 2, 3)]
    routed_rows = [routed_rows] + [shift(routed_rows, "y", j) for j in (1, 2, 3)]

    keep, send = call(
        gate_up_kernel,
        place,
        token_rows + pair_own + pair_other,
        [((4, part, hidden), F32), ((4, part, hidden), BF16)],
        [((4, slots, width), BF16), ((4, slots, hidden), F32)],
    )
    both = keep + swap(send, "zl").astype(F32)
    gate, up = both[0:2], both[2:4]
    sigmoid = jax.nn.sigmoid(gate)
    swish = gate * sigmoid
    activation = (swish * up).astype(BF16)
    activation_far = swap(activation, "zl")
    keep, send = call(
        back_kernel,
        place,
        routed_rows + down_own + down_other,
        [((2, part, hidden), F32), ((2, part, hidden), BF16)],
        [((4, slots, width), BF16), ((2, slots, hidden), F32)],
    )
    activation_grad = keep + swap(send, "zl").astype(F32)
    hidden_grad = jnp.concatenate(
        [
            (activation_grad * up * sigmoid * (1.0 + gate * (1.0 - sigmoid))).astype(BF16),
            (activation_grad * swish).astype(BF16),
        ],
        axis=0,
    )
    hidden_grad_far = swap(hidden_grad, "zl")

    def returned(blocks):
        total = blocks[0]
        for j in (1, 2, 3):
            total = total + shift(blocks[j], "y", -j).astype(F32)
        total = total.astype(BF16)
        parts = [total[k * CAP : (k + 1) * CAP] for k in range(4)]
        return [parts[0]] + [shift(parts[k], "expert", -k) for k in (1, 2, 3)]

    shares = [((slots, width), F32)] + [((slots, width), BF16)] * 3
    output_blocks = returned(
        call(
            output_kernel,
            place,
            [activation, activation_far] + down_own + down_other,
            shares,
            [((2, slots, hidden), BF16), ((2, 4, hidden, width), BF16)],
        )
    )
    input_blocks = returned(
        call(
            input_kernel,
            place,
            [hidden_grad, hidden_grad_far] + pair_own + pair_other,
            shares,
            [((4, slots, hidden), BF16), ((4, 4, hidden, width), BF16)],
        )
    )
    terms = call(
        weight_kernel,
        place,
        [activation, activation_far, hidden_grad, hidden_grad_far] + token_rows + routed_rows,
        [((3, hidden, width), F32)] * 4 + [((3, hidden, width), BF16)] * 4,
        [((6, slots, hidden), BF16), ((2, 4, slots, width), BF16)],
    )
    sums = [terms[i] + swap(terms[4 + i], "core").astype(F32) for i in range(4)]
    weight_total = sums[0]
    for i in (1, 2, 3):
        weight_total = weight_total + shift(sums[i].astype(BF16), "x", -i).astype(F32)
    weight_grad = turn(weight_total.astype(BF16)).astype(F32)[None]

    layer_output, prob_part = call(
        layer_kernel,
        place,
        [expert_ids, gate_probs, out_grad, placing] + output_blocks,
        [((rows, width), BF16), ((rows, 2), F32)],
    )
    near, across, far = [shift(prob_part, "y", j) for j in (1, 2, 3)]
    prob_grad = (prob_part + across) + (near + far)
    prob_grad = prob_grad + swap(prob_grad, "zl")
    token_grad = call(
        token_kernel, place, [placing] + input_blocks, [((rows, width), BF16)]
    )[0]
    return layer_output, token_grad, prob_grad, weight_grad


def solution(mesh):
    split = Mesh(
        mesh.devices.reshape(4, 2, 4, 4, 2), ("x", "core", "expert", "y", "zl")
    )
    rows = P(("x", "core", "expert"), ("y", "zl"))
    pairs = P(("x", "core", "expert"), None)
    weights = P("expert", None, ("y", "zl"), ("x", "core"))
    return jax.shard_map(
        body,
        mesh=split,
        in_specs=(rows, pairs, pairs, weights, rows),
        out_specs=(rows, rows, pairs, weights),
        check_vma=False,
    )
```

```python
import jax
import jax.numpy as jnp
from jax import lax
from jax.experimental import pallas as pl
from jax.experimental.pallas import tpu as pltpu
from jax.sharding import Mesh, PartitionSpec as P

F32 = jnp.float32
BF16 = jnp.bfloat16
CAP = 80
TILE = 16
PARAMS = pltpu.CompilerParams(vmem_limit_bytes=48 * 1024 * 1024)


def nn(a, b):
    return lax.dot_general(a, b, (((1,), (0,)), ((), ())), preferred_element_type=F32)


def nt(a, b):
    return lax.dot_general(a, b, (((1,), (1,)), ((), ())), preferred_element_type=F32)


def tn(a, b):
    return lax.dot_general(a, b, (((0,), (0,)), ((), ())), preferred_element_type=F32)


def call(kernel, place, args, outs, scratch=(), spaces=None):
    whole = pl.BlockSpec(memory_space=pltpu.VMEM)
    return pl.pallas_call(
        kernel,
        out_shape=[jax.ShapeDtypeStruct(shape, kind) for shape, kind in outs],
        in_specs=[pl.BlockSpec(memory_space=pltpu.SMEM)] + (spaces or [whole] * len(args)),
        out_specs=[whole] * len(outs),
        scratch_shapes=list(scratch),
        compiler_params=PARAMS,
    )(place, *args)


def expert_rows(place, ids, k):
    expert = lax.rem(place[0] + k, 4)
    return ids[0:1, :] == expert, ids[1:2, :] == expert


def slots_kernel(place, ids, probs, tokens, grads, placing, *refs):
    outs, token_copy, grad_copy, sems = refs[0:4], refs[4], refs[5], refs[6]
    first = pltpu.make_async_copy(tokens, token_copy, sems.at[0])
    second = pltpu.make_async_copy(grads, grad_copy, sems.at[1])
    first.start()
    second.start()
    rows = ids.shape[1]
    before = (
        lax.broadcasted_iota(jnp.int32, (rows, rows), 0)
        < lax.broadcasted_iota(jnp.int32, (rows, rows), 1)
    ).astype(BF16)
    slot = lax.broadcasted_iota(jnp.int32, (CAP, rows), 0)
    scales = []
    for k in range(4):
        one, two = expert_rows(place, ids, k)
        named = jnp.logical_or(one, two)
        marks = jnp.broadcast_to(named, (8, rows)).astype(F32)
        position = nn(marks.astype(BF16), before)[0:1, :].astype(jnp.int32)
        weight = jnp.where(one, probs[0:1, :], probs[1:2, :])
        chosen = jnp.logical_and(
            jnp.broadcast_to(marks[0:1, :] > 0.5, (CAP, rows)),
            slot == jnp.broadcast_to(position, (CAP, rows)),
        )
        placing[k * CAP : (k + 1) * CAP, :] = chosen.astype(F32).astype(BF16)
        scales.append(jnp.sum(jnp.where(chosen, weight, 0.0), axis=1, keepdims=True))
    first.wait()
    second.wait()
    for k in range(4):
        hot = placing[k * CAP : (k + 1) * CAP, :]
        outs[k][0:CAP, :] = nn(hot, token_copy[...]).astype(BF16)
        outs[k][CAP : 2 * CAP, :] = (scales[k] * nn(hot, grad_copy[...])).astype(BF16)


def split_halves(total, keep, send, zl):
    part = keep.shape[-2]
    mine = pl.multiple_of(zl * part, 32)
    theirs = pl.multiple_of((1 - zl) * part, 32)
    for n in range(keep.shape[0]):
        keep[n] = total[n, pl.ds(mine, part), :]
        send[n] = total[n, pl.ds(theirs, part), :].astype(BF16)


def fetch(weights, joined, sems, names):
    half = weights.shape[3]
    copies = [
        pltpu.make_async_copy(
            weights.at[block, c, m],
            joined.at[n, block, pl.ds(c * half, half)],
            sems.at[n, block, c],
        )
        for n, m in enumerate(names)
        for block in range(4)
        for c in range(2)
    ]
    for copy in copies:
        copy.start()
    return copies


def project(rows, weights, y, total, joined, sems, names):
    for copy in fetch(weights, joined, sems, names):
        copy.wait()
    for n in range(len(names)):
        for j in range(4):
            share = nt(rows[j][...], joined[n, lax.rem(y - j + 4, 4)])
            total[n] = share if j == 0 else total[n] + share


def gate_up_kernel(place, *refs):
    rows, weights, keep, send, total, joined, sems = refs[0:4], *refs[4:10]
    project(rows, weights, place[2], total, joined, sems, (0, 1))
    split_halves(total, keep, send, place[3])


def back_kernel(place, *refs):
    rows, weights, keep, send, total, joined, sems = refs[0:4], *refs[4:10]
    project(rows, weights, place[2], total, joined, sems, (2,))
    split_halves(total, keep, send, place[3])


def pieces(values):
    high = values.astype(BF16)
    rest = values - high.astype(F32)
    middle = rest.astype(BF16)
    low = (rest - middle.astype(F32)).astype(BF16)
    return high, middle, low


def marked_rows(row):
    spot = lax.broadcasted_iota(jnp.int32, (TILE, row.shape[1]), 0)
    parts = [part.astype(F32) for part in pieces(row)]
    total = jnp.where(spot == 0, parts[0], 0.0)
    total += jnp.where(spot == 1, parts[1], 0.0)
    return (total + jnp.where(spot == 2, parts[2], 0.0)).astype(BF16)


def hidden_kernel(place, both, act, keep, far, out):
    gate, up = both[0], both[1]
    sigmoid = 1.0 / (1.0 + jnp.exp(-gate))
    swish = gate * sigmoid
    grad = keep[0] + far[0].astype(F32)
    part = grad.shape[0]
    out[0:part, :] = (grad * up * sigmoid * (1.0 + gate * (1.0 - sigmoid))).astype(BF16)
    out[part : 2 * part, :] = (grad * swish).astype(BF16)
    share = jnp.sum(act[0].astype(F32) * grad, axis=1, keepdims=True)
    out[2 * part :, :] = jnp.zeros((2 * TILE, out.shape[1]), BF16)
    shape = (CAP, 128)
    same = lax.broadcasted_iota(jnp.int32, shape, 0) == lax.broadcasted_iota(jnp.int32, shape, 1)
    for n in range(2):
        row = jnp.sum(
            jnp.where(same, share[n * CAP : (n + 1) * CAP, :], 0.0), axis=0, keepdims=True
        )
        out[2 * part + n * TILE : 2 * part + (n + 1) * TILE, 0:128] = marked_rows(row)


def join(target, mine, theirs, zl):
    part = mine.shape[-2]
    target[pl.ds(pl.multiple_of(zl * part, 32), part), :] = mine[...]
    target[pl.ds(pl.multiple_of((1 - zl) * part, 32), part), :] = theirs[...]


def join_hidden(joined, act, act_far, grad, grad_far, zl):
    part = act.shape[1]
    join(joined.at[2], act.at[0], act_far.at[0], zl)
    for n in range(2):
        span = pl.ds(n * part, part)
        join(joined.at[n], grad.at[span], grad_far.at[span], zl)


def share_kernel(place, act, act_far, grad, grad_far, weights, *refs):
    outs, joined, blocks, marks, sems = refs[0:4], *refs[4:8]
    copies = fetch(weights, blocks, sems, (2, 0, 1))
    part = act.shape[1]
    join_hidden(joined, act, act_far, grad, grad_far, place[3])
    marks[place[3]] = grad[2 * part :, 0:128]
    marks[1 - place[3]] = grad_far[2 * part :, 0:128]
    unit = 2 * CAP + TILE
    for n in range(3):
        for copy in copies[8 * n : 8 * n + 8]:
            copy.wait()
        if n == 1:
            continue
        for j in range(4):
            spot = lax.rem(place[2] - j + 4, 4)
            kind = outs[j].dtype
            if n == 0:
                acc = nn(joined[2], blocks[0, spot])
            else:
                acc = nn(joined[0], blocks[1, spot]) + nn(joined[1], blocks[2, spot])
            first = 0 if n == 0 else CAP
            for k in range(4):
                start = k * unit + first
                outs[j][start : start + CAP, :] = acc[k * CAP : (k + 1) * CAP, :].astype(kind)
    for j in range(4):
        for k in range(4):
            start = k * unit + 2 * CAP
            kind = outs[j].dtype
            rows = marks[k // 2, (k % 2) * TILE : (k % 2 + 1) * TILE, :]
            outs[j][start : start + TILE, :] = jnp.zeros((TILE, outs[j].shape[1]), kind)
            outs[j][start : start + TILE, 0:128] = rows.astype(kind)


def total_kernel(place, own, one, three, two, *outs):
    unit = 2 * CAP + TILE
    for k in range(4):
        span = pl.ds(k * unit, unit)
        total = own[span, :] + one[span, :].astype(F32)
        total += three[span, :].astype(F32) + two[span, :].astype(F32)
        outs[k][...] = total.astype(BF16)
        row = jnp.sum(total[2 * CAP :, 0:128], axis=0, keepdims=True)
        outs[k][2 * CAP :, 0:128] = marked_rows(row)


def weight_kernel(place, after, *refs):
    act, act_far, grad, grad_far = refs[0:4]
    rows, routed = refs[4:8], refs[8:12]
    out, joined, turned = refs[12:15]
    y, zl = place[2], place[3]
    half = out.shape[3]
    join_hidden(joined, act, act_far, grad, grad_far, zl)
    for j in range(4):
        spot = lax.rem(y - j + 4, 4)
        turned[0, spot] = rows[j][...]
        turned[1, spot] = routed[j][...]
    for i in range(4):
        for m in range(3):
            total = tn(joined[m], turned[1 if m == 2 else 0, i])
            for c in range(2):
                out[i, c, m] = total[c * half : (c + 1) * half, :].astype(BF16)


def column(row):
    rows = row.shape[1]
    shape = (rows, rows)
    same = lax.broadcasted_iota(jnp.int32, shape, 0) == lax.broadcasted_iota(jnp.int32, shape, 1)
    return jnp.sum(jnp.where(same, row, 0.0), axis=1, keepdims=True)


def owner_kernel(place, ids, probs, placing, *refs):
    blocks, layer, token, prob = refs[0:4], *refs[4:7]
    total = jnp.zeros(layer.shape, F32)
    grads = jnp.zeros(token.shape, F32)
    shares = [jnp.zeros((1, ids.shape[1]), F32) for _ in range(2)]
    for k in range(4):
        one, two = expert_rows(place, ids, k)
        hot = placing[k * CAP : (k + 1) * CAP, :]
        weight = jnp.where(one, probs[0:1, :], 0.0) + jnp.where(two, probs[1:2, :], 0.0)
        total += column(weight) * tn(hot, blocks[k][0:CAP, :])
        grads += tn(hot, blocks[k][CAP : 2 * CAP, :])
        found = nn(blocks[k][2 * CAP :, 0:128][:, 0:CAP], hot)
        share = jnp.sum(found, axis=0, keepdims=True)
        shares[0] += jnp.where(one, share, 0.0)
        shares[1] += jnp.where(two, share, 0.0)
    layer[...] = total.astype(BF16)
    token[...] = grads.astype(BF16)
    prob[...] = jnp.zeros(prob.shape, F32)
    for n in range(2):
        prob[n : n + 1, :] = shares[n] / probs[n : n + 1, :]


def shift(value, axis, step):
    return lax.ppermute(value, axis, [(i, (i + step) % 4) for i in range(4)])


def swap(value, axis):
    return lax.ppermute(value, axis, [(0, 1), (1, 0)])


def turn(value):
    return lax.ppermute(value, ("core", "zl"), [(2 * c + z, 2 * z + c) for c in range(2) for z in range(2)])


def body(tokens, expert_ids, gate_probs, stacked_weights, out_grad):
    rows, width = tokens.shape
    half = stacked_weights.shape[2]
    hidden = 2 * half
    slots = 4 * CAP
    part = slots // 2
    place = jnp.stack(
        [lax.axis_index(name) for name in ("expert", "x", "y", "zl")]
    ).astype(jnp.int32)
    ids, probs = expert_ids.T, gate_probs.T
    vmem = pl.BlockSpec(memory_space=pltpu.VMEM)
    hbm = pl.BlockSpec(memory_space=pl.ANY)

    weights = lax.all_gather(turn(stacked_weights[0]), ("x", "core"), axis=0, tiled=False)
    weights = weights.reshape(4, 2, 3, half, width)

    placing, *blocks = call(
        slots_kernel,
        place,
        [ids, probs, tokens, out_grad],
        [((slots, rows), BF16)] + [((2 * CAP, width), BF16)] * 4,
        [pltpu.VMEM((rows, width), BF16)] * 2 + [pltpu.SemaphoreType.DMA((2,))],
        [vmem, vmem, hbm, hbm],
    )
    blocks = [blocks[0]] + [shift(blocks[k], "expert", k) for k in (1, 2, 3)]
    token_rows = jnp.concatenate([block[:CAP] for block in blocks], axis=0)
    routed_rows = jnp.concatenate([block[CAP:] for block in blocks], axis=0)
    token_rows = [token_rows] + [shift(token_rows, "y", j) for j in (1, 3, 2)]
    routed_rows = [routed_rows] + [shift(routed_rows, "y", j) for j in (1, 3, 2)]
    token_rows[2:] = token_rows[:1:-1]
    routed_rows[2:] = routed_rows[:1:-1]

    def project_call(kernel, blocks, count):
        return call(
            kernel,
            place,
            blocks + [weights],
            [((count, part, hidden), F32), ((count, part, hidden), BF16)],
            [
                pltpu.VMEM((count, slots, hidden), F32),
                pltpu.VMEM((count, 4, hidden, width), BF16),
                pltpu.SemaphoreType.DMA((count, 4, 2)),
            ],
            [vmem] * 4 + [hbm],
        )

    keep, send = project_call(gate_up_kernel, token_rows, 2)
    both = keep + swap(send, "zl").astype(F32)
    gate, up = both[0:1], both[1:2]
    activation = (gate * jax.nn.sigmoid(gate) * up).astype(BF16)
    activation_far = swap(activation, "zl")
    keep, send = project_call(back_kernel, routed_rows, 1)
    hidden_grad = call(
        hidden_kernel,
        place,
        [both, activation, keep, swap(send, "zl")],
        [((2 * part + 2 * TILE, hidden), BF16)],
    )[0]
    pairs = [activation, activation_far, hidden_grad, swap(hidden_grad, "zl")]

    unit = 2 * CAP + TILE
    shares = call(
        share_kernel,
        place,
        pairs + [weights],
        [((4 * unit, width), F32)] + [((4 * unit, width), BF16)] * 3,
        [
            pltpu.VMEM((3, slots, hidden), BF16),
            pltpu.VMEM((3, 4, hidden, width), BF16),
            pltpu.VMEM((2, 2 * TILE, 128), BF16),
            pltpu.SemaphoreType.DMA((3, 4, 2)),
        ],
        [vmem] * 4 + [hbm],
    )
    arrived = [shift(shares[j], "y", -j) for j in (1, 3, 2)]
    terms = call(
        weight_kernel,
        place,
        [shares[3]] + pairs + token_rows + routed_rows,
        [((4, 2, 3, half, width), BF16)],
        [pltpu.VMEM((3, slots, hidden), BF16), pltpu.VMEM((2, 4, slots, width), BF16)],
        [hbm] + [vmem] * 12,
    )[0]
    weight_total = lax.psum_scatter(
        terms.reshape(8, 3, half, width), ("x", "core"), scatter_dimension=0, tiled=False
    )
    totals = call(total_kernel, place, [shares[0]] + arrived, [((unit, width), BF16)] * 4)
    returned = [totals[0]] + [shift(totals[k], "expert", -k) for k in (1, 2, 3)]
    weight_total, returned[1] = lax.optimization_barrier((weight_total, returned[1]))
    layer_output, token_grad, prob_grad = call(
        owner_kernel,
        place,
        [ids, probs, placing] + returned,
        [((rows, width), BF16), ((rows, width), BF16), ((8, rows), F32)],
    )
    weight_grad = turn(weight_total).astype(F32)[None]
    return layer_output, token_grad, prob_grad[0:2].T, weight_grad


def solution(mesh):
    split = Mesh(
        mesh.devices.reshape(4, 2, 4, 4, 2), ("x", "core", "expert", "y", "zl")
    )
    rows = P(("x", "core", "expert"), ("y", "zl"))
    pairs = P(("x", "core", "expert"), None)
    weights = P("expert", None, ("y", "zl"), ("x", "core"))
    return jax.shard_map(
        body,
        mesh=split,
        in_specs=(rows, pairs, pairs, weights, rows),
        out_specs=(rows, rows, pairs, weights),
        check_vma=False,
    )
```

```python
import functools

import jax
import jax.numpy as jnp
from jax import lax
from jax.experimental import pallas as pl
from jax.experimental.pallas import tpu as pltpu
from jax.sharding import Mesh, PartitionSpec as P

F32 = jnp.float32
BF16 = jnp.bfloat16
CAP = 80
TILE = 16
PARAMS = pltpu.CompilerParams(vmem_limit_bytes=48 * 1024 * 1024)


def nn(a, b):
    return lax.dot_general(a, b, (((1,), (0,)), ((), ())), preferred_element_type=F32)


def nt(a, b):
    return lax.dot_general(a, b, (((1,), (1,)), ((), ())), preferred_element_type=F32)


def tn(a, b):
    return lax.dot_general(a, b, (((0,), (0,)), ((), ())), preferred_element_type=F32)


def call(kernel, place, args, outs, scratch=(), spaces=None):
    whole = pl.BlockSpec(memory_space=pltpu.VMEM)
    return list(pl.pallas_call(
        kernel,
        out_shape=[jax.ShapeDtypeStruct(shape, kind) for shape, kind in outs],
        in_specs=[pl.BlockSpec(memory_space=pltpu.SMEM)] + (spaces or [whole] * len(args)),
        out_specs=[whole] * len(outs),
        scratch_shapes=list(scratch),
        compiler_params=PARAMS,
    )(place, *args))


def expert_rows(place, ids, k):
    expert = lax.rem(place[0] + k, 4)
    return ids[0:1, :] == expert, ids[1:2, :] == expert


def slots_kernel(place, ids_far, probs_far, tokens, grads, placing, *refs):
    outs, ids, probs, token_copy, grad_copy, sems = refs[0:4], *refs[4:9]
    copies = [
        pltpu.make_async_copy(source, target, sems.at[n])
        for n, (source, target) in enumerate(
            [(ids_far, ids), (probs_far, probs), (tokens, token_copy), (grads, grad_copy)]
        )
    ]
    for copy in copies:
        copy.start()
    copies[0].wait()
    copies[1].wait()
    rows = ids.shape[1]
    before = (
        lax.broadcasted_iota(jnp.int32, (rows, rows), 0)
        < lax.broadcasted_iota(jnp.int32, (rows, rows), 1)
    ).astype(BF16)
    slot = lax.broadcasted_iota(jnp.int32, (CAP, rows), 0)
    scales = []
    for k in range(4):
        one, two = expert_rows(place, ids, k)
        named = jnp.logical_or(one, two)
        marks = jnp.broadcast_to(named, (8, rows)).astype(F32)
        position = nn(marks.astype(BF16), before)[0:1, :].astype(jnp.int32)
        weight = jnp.where(one, probs[0:1, :], probs[1:2, :])
        chosen = jnp.logical_and(
            jnp.broadcast_to(marks[0:1, :] > 0.5, (CAP, rows)),
            slot == jnp.broadcast_to(position, (CAP, rows)),
        )
        placing[k * CAP : (k + 1) * CAP, :] = chosen.astype(F32).astype(BF16)
        scales.append(jnp.sum(jnp.where(chosen, weight, 0.0), axis=1, keepdims=True))
    copies[2].wait()
    copies[3].wait()
    for k in range(4):
        hot = placing[k * CAP : (k + 1) * CAP, :]
        outs[k][0:CAP, :] = nn(hot, token_copy[...]).astype(BF16)
        outs[k][CAP : 2 * CAP, :] = (scales[k] * nn(hot, grad_copy[...])).astype(BF16)


def fetch(own, other, joined, sems, names, place):
    half, width = own[0].shape[1:]
    copies = []
    for i in range(4):
        spot = lax.rem(place[2] - place[1] + i + 4, 4)
        columns = pl.ds(pl.multiple_of(spot * width, width), width)
        for n, m in enumerate(names):
            for h, source in enumerate((own[i], other[i])):
                copies.append(
                    pltpu.make_async_copy(
                        source.at[m],
                        joined.at[pl.ds((2 * n + h) * half, half), columns],
                        sems.at[i, n, h],
                    )
                )
    for copy in copies:
        copy.start()
    return copies


def project_kernel(names, place, *refs):
    rows, own, other = refs[0:4], refs[4:8], refs[8:12]
    keep, send, joined, wide, total, sems = refs[12:18]
    width = rows[0].shape[1]
    copies = fetch(own, other, joined, sems, names, place)
    for j in range(4):
        wide[:, j * width : (j + 1) * width] = rows[j][...]
    for copy in copies:
        copy.wait()
    total[...] = nt(wide[...], joined[...])
    part = keep.shape[0]
    keep[...] = total[pl.ds(pl.multiple_of(place[3] * part, 32), part), :]
    send[...] = total[pl.ds(pl.multiple_of((1 - place[3]) * part, 32), part), :].astype(BF16)


def pieces(values):
    high = values.astype(BF16)
    rest = values - high.astype(F32)
    middle = rest.astype(BF16)
    low = (rest - middle.astype(F32)).astype(BF16)
    return high, middle, low


def marked_rows(row):
    spot = lax.broadcasted_iota(jnp.int32, (TILE, row.shape[1]), 0)
    parts = [part.astype(F32) for part in pieces(row)]
    total = jnp.where(spot == 0, parts[0], 0.0)
    total += jnp.where(spot == 1, parts[1], 0.0)
    return (total + jnp.where(spot == 2, parts[2], 0.0)).astype(BF16)


def hidden_kernel(place, both, act, keep, far, out):
    part, width = keep.shape
    gate, up = both[:, 0:width], both[:, width : 2 * width]
    sigmoid = 1.0 / (1.0 + jnp.exp(-gate))
    swish = gate * sigmoid
    grad = keep[...] + far[...].astype(F32)
    out[0:part, 0:width] = (
        grad * up * sigmoid * (1.0 + gate * (1.0 - sigmoid))
    ).astype(BF16)
    out[0:part, width : 2 * width] = (grad * swish).astype(BF16)
    share = jnp.sum(act[...].astype(F32) * grad, axis=1, keepdims=True)
    out[part:, :] = jnp.zeros((2 * TILE, out.shape[1]), BF16)
    shape = (CAP, 128)
    same = lax.broadcasted_iota(jnp.int32, shape, 0) == lax.broadcasted_iota(jnp.int32, shape, 1)
    for n in range(2):
        row = jnp.sum(
            jnp.where(same, share[n * CAP : (n + 1) * CAP, :], 0.0), axis=0, keepdims=True
        )
        out[part + n * TILE : part + (n + 1) * TILE, 0:128] = marked_rows(row)


def join(target, mine, theirs, zl):
    part = target.shape[0] // 2
    target[pl.ds(pl.multiple_of(zl * part, 32), part), :] = mine[0:part, :]
    target[pl.ds(pl.multiple_of((1 - zl) * part, 32), part), :] = theirs[0:part, :]


def share_kernel(place, act, act_far, grad, grad_far, pair, down, *refs):
    outs, acts, grads, marks = refs[0:4], *refs[4:7]
    part, width = act.shape[0], outs[0].shape[1]
    zl = place[3]
    join(acts, act, act_far, zl)
    join(grads, grad, grad_far, zl)
    marks[zl] = grad[part:, 0:128]
    marks[1 - zl] = grad_far[part:, 0:128]
    unit = 2 * CAP + TILE
    for j in (1, 3, 2, 0):
        kind = outs[j].dtype
        columns = slice(j * width, (j + 1) * width)
        out = nn(acts[...], down[:, columns])
        back = nn(grads[...], pair[:, columns])
        for k in range(4):
            start, rows = k * unit, slice(k * CAP, (k + 1) * CAP)
            outs[j][start : start + CAP, :] = out[rows, :].astype(kind)
            outs[j][start + CAP : start + 2 * CAP, :] = back[rows, :].astype(kind)
    for j in range(4):
        for k in range(4):
            start = k * unit + 2 * CAP
            kind = outs[j].dtype
            rows = marks[k // 2, (k % 2) * TILE : (k % 2 + 1) * TILE, :]
            outs[j][start : start + TILE, :] = jnp.zeros((TILE, outs[j].shape[1]), kind)
            outs[j][start : start + TILE, 0:128] = rows.astype(kind)


def total_kernel(place, own, one, three, two, *outs):
    unit = 2 * CAP + TILE
    for k in range(4):
        span = pl.ds(k * unit, unit)
        total = own[span, :] + one[span, :].astype(F32)
        total += three[span, :].astype(F32) + two[span, :].astype(F32)
        outs[k][...] = total.astype(BF16)
        row = jnp.sum(total[2 * CAP :, 0:128], axis=0, keepdims=True)
        outs[k][2 * CAP :, 0:128] = marked_rows(row)


def weight_kernel(place, act, act_far, grad, grad_far, *refs):
    rows, routed = refs[0:4], refs[4:8]
    keep, send, acts, grads, turned = refs[8:13]
    half = keep.shape[2]
    join(acts, act, act_far, place[3])
    join(grads, grad, grad_far, place[3])
    for j in range(4):
        spot = lax.rem(place[1] - place[2] + j + 4, 4)
        turned[0, spot] = rows[j][...]
        turned[1, spot] = routed[j][...]
    for i in range(4):
        pair = tn(grads[...], turned[0, i])
        down = tn(acts[...], turned[1, i])
        for m, total in enumerate((pair[0 : 2 * half], pair[2 * half :], down)):
            keep[i, m] = total[0:half, :]
            send[i, m] = total[half:, :].astype(BF16)


def sum_kernel(place, keep, far, *outs):
    for i in range(4):
        outs[i][...] = (keep[i] + far[i].astype(F32)).astype(outs[i].dtype)


def column(row):
    rows = row.shape[1]
    shape = (rows, rows)
    same = lax.broadcasted_iota(jnp.int32, shape, 0) == lax.broadcasted_iota(jnp.int32, shape, 1)
    return jnp.sum(jnp.where(same, row, 0.0), axis=1, keepdims=True)


def owner_kernel(place, ids, probs, placing, *refs):
    blocks, layer, token, prob = refs[0:4], *refs[4:7]
    total = jnp.zeros(layer.shape, F32)
    grads = jnp.zeros(token.shape, F32)
    shares = [jnp.zeros((1, ids.shape[1]), F32) for _ in range(2)]
    for k in range(4):
        one, two = expert_rows(place, ids, k)
        hot = placing[k * CAP : (k + 1) * CAP, :]
        weight = jnp.where(one, probs[0:1, :], 0.0) + jnp.where(two, probs[1:2, :], 0.0)
        total += column(weight) * tn(hot, blocks[k][0:CAP, :])
        grads += tn(hot, blocks[k][CAP : 2 * CAP, :])
        found = nn(blocks[k][2 * CAP :, 0:128][:, 0:CAP], hot)
        share = jnp.sum(found, axis=0, keepdims=True)
        shares[0] += jnp.where(one, share, 0.0)
        shares[1] += jnp.where(two, share, 0.0)
    layer[...] = total.astype(BF16)
    token[...] = grads.astype(BF16)
    prob[...] = jnp.zeros(prob.shape, F32)
    for n in range(2):
        prob[n : n + 1, :] = shares[n] / probs[n : n + 1, :]


def shift(value, axis, step):
    return lax.ppermute(value, axis, [(i, (i + step) % 4) for i in range(4)])


def swap(value, axis):
    return lax.ppermute(value, axis, [(0, 1), (1, 0)])


def turn(value):
    return lax.ppermute(value, ("core", "zl"), [(2 * c + z, 2 * z + c) for c in range(2) for z in range(2)])


def body(tokens, expert_ids, gate_probs, stacked_weights, out_grad):
    rows, width = tokens.shape
    half = stacked_weights.shape[2]
    hidden = 2 * half
    slots = 4 * CAP
    part = slots // 2
    place = jnp.stack(
        [lax.axis_index(name) for name in ("expert", "x", "y", "zl")]
    ).astype(jnp.int32)
    ids, probs = expert_ids.T, gate_probs.T
    vmem = pl.BlockSpec(memory_space=pltpu.VMEM)
    hbm = pl.BlockSpec(memory_space=pl.ANY)
    far = pl.BlockSpec(memory_space=pltpu.HBM)

    placing, *blocks = call(
        slots_kernel,
        place,
        [ids, probs, tokens, out_grad],
        [((slots, rows), BF16)] + [((2 * CAP, width), BF16)] * 4,
        [
            pltpu.VMEM(ids.shape, jnp.int32),
            pltpu.VMEM(probs.shape, F32),
            pltpu.VMEM((rows, width), BF16),
            pltpu.VMEM((rows, width), BF16),
            pltpu.SemaphoreType.DMA((4,)),
        ],
        [far, far, far, far],
    )

    own, placing = lax.optimization_barrier((turn(stacked_weights[0]), placing))
    own = [own] + [shift(own, "x", i) for i in (1, 3, 2)]
    own[2:] = own[:1:-1]
    other = [swap(block, "core") for block in own]
    blocks = [blocks[0]] + [shift(blocks[k], "expert", k) for k in (1, 2, 3)]
    token_rows = jnp.concatenate([block[:CAP] for block in blocks], axis=0)
    routed_rows = jnp.concatenate([block[CAP:] for block in blocks], axis=0)
    token_rows, other[1], other[3] = lax.optimization_barrier((token_rows, other[1], other[3]))
    token_rows = [token_rows] + [shift(token_rows, "y", j) for j in (1, 3, 2)]
    routed_rows = [routed_rows] + [shift(routed_rows, "y", j) for j in (1, 3, 2)]
    token_rows[2:] = token_rows[:1:-1]
    routed_rows[2:] = routed_rows[:1:-1]

    def project(names, blocks):
        wide = len(names) * hidden
        return call(
            functools.partial(project_kernel, names),
            place,
            blocks + own + other,
            [((part, wide), F32), ((part, wide), BF16), ((wide, 4 * width), BF16)],
            [
                pltpu.VMEM((slots, 4 * width), BF16),
                pltpu.VMEM((slots, wide), F32),
                pltpu.SemaphoreType.DMA((4, 2, 2)),
            ],
            [vmem] * 4 + [hbm] * 8,
        )

    keep, send, pair_weights = project((0, 1), token_rows)
    both = keep + swap(send, "zl").astype(F32)
    gate, up = both[:, :hidden], both[:, hidden:]
    activation = (gate * jax.nn.sigmoid(gate) * up).astype(BF16)
    activation_far = swap(activation, "zl")
    keep, send, down_weights = project((2,), routed_rows)
    send, activation_far = lax.optimization_barrier((swap(send, "zl"), activation_far))
    hidden_grad = call(
        hidden_kernel,
        place,
        [both, activation, keep, send],
        [((part + 2 * TILE, 2 * hidden), BF16)],
    )[0]
    pairs = [activation, activation_far, hidden_grad, swap(hidden_grad, "zl")]

    unit = 2 * CAP + TILE
    joined = [pltpu.VMEM((slots, hidden), BF16), pltpu.VMEM((slots, 2 * hidden), BF16)]
    shares = call(
        share_kernel,
        place,
        pairs + [pair_weights, down_weights],
        [((4 * unit, width), F32)] + [((4 * unit, width), BF16)] * 3,
        joined + [pltpu.VMEM((2, 2 * TILE, 128), BF16)],
    )
    arrived = [shift(shares[j], "y", -j) for j in (1, 3, 2)]
    shares[0], pairs[0] = lax.optimization_barrier((shares[0], pairs[0]))
    keep, send = call(
        weight_kernel,
        place,
        pairs + token_rows + routed_rows,
        [((4, 3, half, width), F32), ((4, 3, half, width), BF16)],
        joined + [pltpu.VMEM((2, 4, slots, width), BF16)],
    )
    sums = call(
        sum_kernel,
        place,
        [keep, swap(send, "core")],
        [((3, half, width), F32)] + [((3, half, width), BF16)] * 3,
    )
    sums = list(sums)
    sums[1], sums[3], arrived[0], arrived[1] = lax.optimization_barrier(
        (sums[1], sums[3], arrived[0], arrived[1])
    )
    sums[2], arrived[2] = lax.optimization_barrier((sums[2], arrived[2]))
    far_sums = [shift(sums[i], "x", -i) for i in (1, 3, 2)]
    totals = call(total_kernel, place, [shares[0]] + arrived, [((unit, width), BF16)] * 4)
    returned = [totals[0]] + [shift(totals[k], "expert", -k) for k in (1, 2, 3)]
    far_sums[2], returned[1], returned[3] = lax.optimization_barrier(
        (far_sums[2], returned[1], returned[3])
    )
    layer_output, token_grad, prob_grad = call(
        owner_kernel,
        place,
        [ids, probs, placing] + returned,
        [((rows, width), BF16), ((rows, width), BF16), ((8, rows), F32)],
    )
    weight_total = sums[0]
    for block in far_sums:
        weight_total = weight_total + block.astype(F32)
    weight_grad = turn(weight_total.astype(BF16)).astype(F32)[None]
    return layer_output, token_grad, prob_grad[0:2].T, weight_grad


def solution(mesh):
    split = Mesh(
        mesh.devices.reshape(4, 2, 4, 4, 2), ("x", "core", "expert", "y", "zl")
    )
    rows = P(("x", "core", "expert"), ("y", "zl"))
    pairs = P(("x", "core", "expert"), None)
    weights = P("expert", None, ("y", "zl"), ("x", "core"))
    return jax.shard_map(
        body,
        mesh=split,
        in_specs=(rows, pairs, pairs, weights, rows),
        out_specs=(rows, rows, pairs, weights),
        check_vma=False,
    )
```

```python
import functools

import jax
import jax.numpy as jnp
from jax import lax
from jax.experimental import pallas as pl
from jax.experimental.pallas import tpu as pltpu
from jax.sharding import Mesh, PartitionSpec as P

F32 = jnp.float32
BF16 = jnp.bfloat16
CAP = 80
TILE = 16
PARAMS = pltpu.CompilerParams(vmem_limit_bytes=48 * 1024 * 1024)


def nn(a, b):
    return lax.dot_general(a, b, (((1,), (0,)), ((), ())), preferred_element_type=F32)


def nt(a, b):
    return lax.dot_general(a, b, (((1,), (1,)), ((), ())), preferred_element_type=F32)


def tn(a, b):
    return lax.dot_general(a, b, (((0,), (0,)), ((), ())), preferred_element_type=F32)


def call(kernel, place, args, outs, scratch=(), spaces=None):
    whole = pl.BlockSpec(memory_space=pltpu.VMEM)
    return list(pl.pallas_call(
        kernel,
        out_shape=[jax.ShapeDtypeStruct(shape, kind) for shape, kind in outs],
        in_specs=[pl.BlockSpec(memory_space=pltpu.SMEM)] + (spaces or [whole] * len(args)),
        out_specs=[whole] * len(outs),
        scratch_shapes=list(scratch),
        compiler_params=PARAMS,
    )(place, *args))


def expert_rows(place, ids, k):
    expert = lax.rem(place[0] + k, 4)
    return ids[0:1, :] == expert, ids[1:2, :] == expert


def slots_kernel(place, ids_far, probs_far, tokens, grads, placing, *refs):
    outs, ids, probs, token_copy, grad_copy, sems = refs[0:4], *refs[4:9]
    copies = [
        pltpu.make_async_copy(source, target, sems.at[n])
        for n, (source, target) in enumerate(
            [(ids_far, ids), (probs_far, probs), (tokens, token_copy), (grads, grad_copy)]
        )
    ]
    for copy in copies:
        copy.start()
    copies[0].wait()
    copies[1].wait()
    rows = ids.shape[1]
    before = (
        lax.broadcasted_iota(jnp.int32, (rows, rows), 0)
        < lax.broadcasted_iota(jnp.int32, (rows, rows), 1)
    ).astype(BF16)
    slot = lax.broadcasted_iota(jnp.int32, (CAP, rows), 0)
    scales = []
    for k in range(4):
        one, two = expert_rows(place, ids, k)
        named = jnp.logical_or(one, two)
        marks = jnp.broadcast_to(named, (8, rows)).astype(F32)
        position = nn(marks.astype(BF16), before)[0:1, :].astype(jnp.int32)
        weight = jnp.where(one, probs[0:1, :], probs[1:2, :])
        chosen = jnp.logical_and(
            jnp.broadcast_to(marks[0:1, :] > 0.5, (CAP, rows)),
            slot == jnp.broadcast_to(position, (CAP, rows)),
        )
        placing[k * CAP : (k + 1) * CAP, :] = chosen.astype(F32).astype(BF16)
        scales.append(jnp.sum(jnp.where(chosen, weight, 0.0), axis=1, keepdims=True))
    copies[2].wait()
    copies[3].wait()
    for k in range(4):
        hot = placing[k * CAP : (k + 1) * CAP, :]
        outs[k][0:CAP, :] = nn(hot, token_copy[...]).astype(BF16)
        outs[k][CAP : 2 * CAP, :] = (scales[k] * nn(hot, grad_copy[...])).astype(BF16)


def fetch(own, other, joined, sems, names, place):
    half, width = own.shape[2:]
    copies = []
    for block in range(4):
        spot = lax.rem(place[2] - place[1] + block + 4, 4)
        columns = pl.ds(pl.multiple_of(spot * width, width), width)
        for n, m in enumerate(names):
            for h, source in enumerate((own, other)):
                copies.append(
                    pltpu.make_async_copy(
                        source.at[block, m],
                        joined.at[pl.ds((2 * n + h) * half, half), columns],
                        sems.at[block, n, h],
                    )
                )
    for copy in copies:
        copy.start()
    return copies


def take_rows(target, source, second):
    for k in range(4):
        first = (2 * k + second) * CAP
        target[k * CAP : (k + 1) * CAP, :] = source[first : first + CAP, :]


def project_kernel(names, second, place, *refs):
    rows, own, other = refs[0:4], refs[4], refs[5]
    keep, send, joined, wide, total, sems = refs[6:12]
    width = rows[0].shape[1]
    copies = fetch(own, other, joined, sems, names, place)
    for j in range(4):
        take_rows(wide.at[:, pl.ds(j * width, width)], rows[j], second)
    for copy in copies:
        copy.wait()
    total[...] = nt(wide[...], joined[...])
    part = keep.shape[0]
    keep[...] = total[pl.ds(pl.multiple_of(place[3] * part, 32), part), :]
    send[...] = total[pl.ds(pl.multiple_of((1 - place[3]) * part, 32), part), :].astype(BF16)


def pieces(values):
    high = values.astype(BF16)
    rest = values - high.astype(F32)
    middle = rest.astype(BF16)
    low = (rest - middle.astype(F32)).astype(BF16)
    return high, middle, low


def marked_rows(row, first):
    spot = lax.broadcasted_iota(jnp.int32, (TILE, row.shape[1]), 0)
    total = jnp.zeros(spot.shape, F32)
    for n, part in enumerate(pieces(row)):
        total += jnp.where(spot == first + n, part.astype(F32), 0.0)
    return total


def hidden_kernel(place, both, act, keep, far, out):
    part, width = keep.shape
    gate, up = both[:, 0:width], both[:, width : 2 * width]
    sigmoid = 1.0 / (1.0 + jnp.exp(-gate))
    swish = gate * sigmoid
    grad = keep[...] + far[...].astype(F32)
    out[0:part, 0:width] = (
        grad * up * sigmoid * (1.0 + gate * (1.0 - sigmoid))
    ).astype(BF16)
    out[0:part, width : 2 * width] = (grad * swish).astype(BF16)
    share = jnp.sum(act[...].astype(F32) * grad, axis=1, keepdims=True)
    out[part:, :] = jnp.zeros((TILE, out.shape[1]), BF16)
    marks = jnp.zeros((TILE, 128), F32)
    shape = (CAP, 128)
    same = lax.broadcasted_iota(jnp.int32, shape, 0) == lax.broadcasted_iota(jnp.int32, shape, 1)
    for n in range(2):
        row = jnp.sum(
            jnp.where(same, share[n * CAP : (n + 1) * CAP, :], 0.0), axis=0, keepdims=True
        )
        marks += marked_rows(row, 6 * place[3] + 3 * n)
    out[part:, 0:128] = marks.astype(BF16)


def join(target, mine, theirs, zl):
    part = target.shape[0] // 2
    target[pl.ds(pl.multiple_of(zl * part, 32), part), :] = mine[0:part, :]
    target[pl.ds(pl.multiple_of((1 - zl) * part, 32), part), :] = theirs[0:part, :]


def share_kernel(place, act, act_far, grad, grad_far, pair, down, *refs):
    outs, acts, grads = refs[0:4], *refs[4:6]
    part, width = act.shape[0], outs[0].shape[1]
    zl = place[3]
    join(acts, act, act_far, zl)
    join(grads, grad, grad_far, zl)
    marks = grad[part:, 0:128].astype(F32) + grad_far[part:, 0:128].astype(F32)
    unit = 2 * CAP
    for j in (1, 3, 2, 0):
        kind = outs[j].dtype
        columns = slice(j * width, (j + 1) * width)
        out = nn(acts[...], down[:, columns])
        back = nn(grads[...], pair[:, columns])
        for k in range(4):
            start, rows = k * unit, slice(k * CAP, (k + 1) * CAP)
            outs[j][start : start + CAP, :] = out[rows, :].astype(kind)
            outs[j][start + CAP : start + 2 * CAP, :] = back[rows, :].astype(kind)
    for j in range(4):
        kind = outs[j].dtype
        outs[j][4 * unit :, :] = jnp.zeros((TILE, width), kind)
        outs[j][4 * unit :, 0:128] = marks.astype(kind)


def total_kernel(place, own, one, three, two, *outs):
    unit = 2 * CAP

    def total(span, columns):
        value = own[span, columns] + one[span, columns].astype(F32)
        return value + three[span, columns].astype(F32) + two[span, columns].astype(F32)

    marks = total(slice(4 * unit, 4 * unit + TILE), slice(0, 128))
    width = own.shape[1]
    for k in range(4):
        outs[k][0:unit, :] = total(slice(k * unit, (k + 1) * unit), slice(0, width)).astype(BF16)
        row = jnp.sum(marks[3 * k : 3 * k + 3, :], axis=0, keepdims=True)
        outs[k][unit:, :] = jnp.zeros((TILE, width), BF16)
        outs[k][unit:, 0:128] = marked_rows(row, 0).astype(BF16)


def weight_kernel(second, place, near, far, *refs):
    rows, keep, send, joined, chosen = refs[0:4], *refs[4:8]
    half = keep.shape[2]
    join(joined, near, far, place[3])
    for j in range(4):
        block = lax.rem(place[1] - place[2] + j + 4, 4)
        take_rows(chosen, rows[j], second)
        total = tn(joined[...], chosen[...])
        for m in range(keep.shape[1]):
            keep[block, m] = total[2 * m * half : (2 * m + 1) * half, :]
            send[block, m] = total[(2 * m + 1) * half : (2 * m + 2) * half, :].astype(BF16)


def sum_kernel(place, pair, pair_far, down, down_far, *outs):
    for i in range(4):
        kind = outs[i].dtype
        for m in range(2):
            outs[i][m] = (pair[i, m] + pair_far[i, m].astype(F32)).astype(kind)
        outs[i][2] = (down[i, 0] + down_far[i, 0].astype(F32)).astype(kind)


def column(row):
    rows = row.shape[1]
    shape = (rows, rows)
    same = lax.broadcasted_iota(jnp.int32, shape, 0) == lax.broadcasted_iota(jnp.int32, shape, 1)
    return jnp.sum(jnp.where(same, row, 0.0), axis=1, keepdims=True)


def owner_kernel(place, ids, probs, placing, *refs):
    blocks, layer, token, prob = refs[0:4], *refs[4:7]
    total = jnp.zeros(layer.shape, F32)
    grads = jnp.zeros(token.shape, F32)
    shares = [jnp.zeros((1, ids.shape[1]), F32) for _ in range(2)]
    for k in range(4):
        one, two = expert_rows(place, ids, k)
        hot = placing[k * CAP : (k + 1) * CAP, :]
        weight = jnp.where(one, probs[0:1, :], 0.0) + jnp.where(two, probs[1:2, :], 0.0)
        total += column(weight) * tn(hot, blocks[k][0:CAP, :])
        grads += tn(hot, blocks[k][CAP : 2 * CAP, :])
        found = nn(blocks[k][2 * CAP :, 0:128][:, 0:CAP], hot)
        share = jnp.sum(found, axis=0, keepdims=True)
        shares[0] += jnp.where(one, share, 0.0)
        shares[1] += jnp.where(two, share, 0.0)
    layer[...] = total.astype(BF16)
    token[...] = grads.astype(BF16)
    prob[...] = jnp.zeros(prob.shape, F32)
    for n in range(2):
        prob[n : n + 1, :] = shares[n] / probs[n : n + 1, :]


def shift(value, axis, step):
    return lax.ppermute(value, axis, [(i, (i + step) % 4) for i in range(4)])


def swap(value, axis):
    return lax.ppermute(value, axis, [(0, 1), (1, 0)])


def turn(value):
    return lax.ppermute(value, ("core", "zl"), [(2 * c + z, 2 * z + c) for c in range(2) for z in range(2)])


def body(tokens, expert_ids, gate_probs, stacked_weights, out_grad):
    rows, width = tokens.shape
    half = stacked_weights.shape[2]
    hidden = 2 * half
    slots = 4 * CAP
    part = slots // 2
    place = jnp.stack(
        [lax.axis_index(name) for name in ("expert", "x", "y", "zl")]
    ).astype(jnp.int32)
    ids, probs = expert_ids.T, gate_probs.T
    vmem = pl.BlockSpec(memory_space=pltpu.VMEM)
    hbm = pl.BlockSpec(memory_space=pl.ANY)
    far = pl.BlockSpec(memory_space=pltpu.HBM)

    placing, *blocks = call(
        slots_kernel,
        place,
        [ids, probs, tokens, out_grad],
        [((slots, rows), BF16)] + [((2 * CAP, width), BF16)] * 4,
        [
            pltpu.VMEM(ids.shape, jnp.int32),
            pltpu.VMEM(probs.shape, F32),
            pltpu.VMEM((rows, width), BF16),
            pltpu.VMEM((rows, width), BF16),
            pltpu.SemaphoreType.DMA((4,)),
        ],
        [far, far, far, far],
    )

    own, placing = lax.optimization_barrier((turn(stacked_weights[0]), placing))
    near, back, across = [shift(own, "x", i) for i in (1, 3, 2)]
    blocks = [blocks[0]] + [shift(blocks[k], "expert", k) for k in (1, 2, 3)]
    blocks[2], near, back = lax.optimization_barrier((blocks[2], near, back))
    own = jnp.stack([own, near, across, back])
    blocks = [jnp.concatenate(blocks, axis=0)]
    blocks += [shift(blocks[0], "y", j) for j in (1, 3, 2)]
    own, *blocks[1:] = lax.optimization_barrier((own, *blocks[1:]))
    other = swap(own, "core")
    blocks[2:] = blocks[:1:-1]

    def project(names, second):
        wide = len(names) * hidden
        return call(
            functools.partial(project_kernel, names, second),
            place,
            blocks + [own, other],
            [((part, wide), F32), ((part, wide), BF16), ((wide, 4 * width), BF16)],
            [
                pltpu.VMEM((slots, 4 * width), BF16),
                pltpu.VMEM((slots, wide), F32),
                pltpu.SemaphoreType.DMA((4, 2, 2)),
            ],
            [vmem] * 4 + [hbm] * 2,
        )

    keep, send, pair_weights = project((0, 1), 0)
    both = keep + swap(send, "zl").astype(F32)
    gate, up = both[:, :hidden], both[:, hidden:]
    activation = (gate * jax.nn.sigmoid(gate) * up).astype(BF16)
    activation_far = swap(activation, "zl")
    keep, send, down_weights = project((2,), 1)
    send, activation_far = lax.optimization_barrier((swap(send, "zl"), activation_far))
    hidden_grad = call(
        hidden_kernel,
        place,
        [both, activation, keep, send],
        [((part + TILE, 2 * hidden), BF16)],
    )[0]
    hidden_far = swap(hidden_grad, "zl")

    def weight_terms(near, far, second):
        count = near.shape[1] // hidden
        shape = (4, count, half, width)
        return call(
            functools.partial(weight_kernel, second),
            place,
            [near, far] + blocks,
            [(shape, F32), (shape, BF16)],
            [pltpu.VMEM((slots, near.shape[1]), BF16), pltpu.VMEM((slots, width), BF16)],
        )

    down_keep, down_send = weight_terms(activation, activation_far, 1)
    hidden_far, down_keep = lax.optimization_barrier((hidden_far, down_keep))

    unit = 2 * CAP + TILE
    shares = call(
        share_kernel,
        place,
        [activation, activation_far, hidden_grad, hidden_far, pair_weights, down_weights],
        [((8 * CAP + TILE, width), F32)] + [((8 * CAP + TILE, width), BF16)] * 3,
        [pltpu.VMEM((slots, hidden), BF16), pltpu.VMEM((slots, 2 * hidden), BF16)],
    )
    arrived = [shift(shares[j], "y", -j) for j in (1, 3, 2)]
    shares[0], hidden_grad = lax.optimization_barrier((shares[0], hidden_grad))
    pair_keep, pair_send = weight_terms(hidden_grad, hidden_far, 0)
    sums = call(
        sum_kernel,
        place,
        [pair_keep, swap(pair_send, "core"), down_keep, swap(down_send, "core")],
        [((3, half, width), F32)] + [((3, half, width), BF16)] * 3,
    )
    sums[2], *arrived[:2] = lax.optimization_barrier((sums[2], *arrived[:2]))
    far_sums = [shift(sums[i], "x", -i) for i in (1, 3, 2)]
    *far_sums, arrived[2] = lax.optimization_barrier((*far_sums, arrived[2]))
    totals = call(total_kernel, place, [shares[0]] + arrived, [((unit, width), BF16)] * 4)
    returned = [totals[0]] + [shift(totals[k], "expert", -k) for k in (1, 2, 3)]
    layer_output, token_grad, prob_grad = call(
        owner_kernel,
        place,
        [ids, probs, placing] + returned,
        [((rows, width), BF16), ((rows, width), BF16), ((8, rows), F32)],
    )
    weight_total = sums[0]
    for block in far_sums:
        weight_total = weight_total + block.astype(F32)
    weight_grad = turn(weight_total.astype(BF16)).astype(F32)[None]
    return layer_output, token_grad, prob_grad[0:2].T, weight_grad


def solution(mesh):
    split = Mesh(
        mesh.devices.reshape(4, 2, 4, 4, 2), ("x", "core", "expert", "y", "zl")
    )
    rows = P(("x", "core", "expert"), ("y", "zl"))
    pairs = P(("x", "core", "expert"), None)
    weights = P("expert", None, ("y", "zl"), ("x", "core"))
    return jax.shard_map(
        body,
        mesh=split,
        in_specs=(rows, pairs, pairs, weights, rows),
        out_specs=(rows, rows, pairs, weights),
        check_vma=False,
    )
```

```python
import functools

import jax
import jax.numpy as jnp
from jax import lax
from jax.experimental import pallas as pl
from jax.experimental.pallas import tpu as pltpu
from jax.sharding import Mesh, PartitionSpec as P

F32 = jnp.float32
BF16 = jnp.bfloat16
CAP = 80
TILE = 16
PARAMS = pltpu.CompilerParams(vmem_limit_bytes=48 * 1024 * 1024)


def nn(a, b):
    return lax.dot_general(a, b, (((1,), (0,)), ((), ())), preferred_element_type=F32)


def nt(a, b):
    return lax.dot_general(a, b, (((1,), (1,)), ((), ())), preferred_element_type=F32)


def tn(a, b):
    return lax.dot_general(a, b, (((0,), (0,)), ((), ())), preferred_element_type=F32)


def call(kernel, place, args, outs, scratch=(), spaces=None):
    whole = pl.BlockSpec(memory_space=pltpu.VMEM)
    return list(pl.pallas_call(
        kernel,
        out_shape=[jax.ShapeDtypeStruct(shape, kind) for shape, kind in outs],
        in_specs=[pl.BlockSpec(memory_space=pltpu.SMEM)] + (spaces or [whole] * len(args)),
        out_specs=[whole] * len(outs),
        scratch_shapes=list(scratch),
        compiler_params=PARAMS,
    )(place, *args))


def expert_rows(place, ids, k):
    expert = lax.rem(place[0] + k, 4)
    return ids[0:1, :] == expert, ids[1:2, :] == expert


def slots_kernel(place, ids_far, probs_far, tokens, grads, placing, *refs):
    outs, ids, probs, token_copy, grad_copy, sems = refs[0:4], *refs[4:9]
    copies = [
        pltpu.make_async_copy(source, target, sems.at[n])
        for n, (source, target) in enumerate(
            [(ids_far, ids), (probs_far, probs), (tokens, token_copy), (grads, grad_copy)]
        )
    ]
    for copy in copies:
        copy.start()
    copies[0].wait()
    copies[1].wait()
    rows = ids.shape[1]
    before = (
        lax.broadcasted_iota(jnp.int32, (rows, rows), 0)
        < lax.broadcasted_iota(jnp.int32, (rows, rows), 1)
    ).astype(BF16)
    slot = lax.broadcasted_iota(jnp.int32, (CAP, rows), 0)
    scales = []
    for k in range(4):
        one, two = expert_rows(place, ids, k)
        named = jnp.logical_or(one, two)
        marks = jnp.broadcast_to(named, (8, rows)).astype(F32)
        position = nn(marks.astype(BF16), before)[0:1, :].astype(jnp.int32)
        weight = jnp.where(one, probs[0:1, :], probs[1:2, :])
        chosen = jnp.logical_and(
            jnp.broadcast_to(marks[0:1, :] > 0.5, (CAP, rows)),
            slot == jnp.broadcast_to(position, (CAP, rows)),
        )
        placing[k * CAP : (k + 1) * CAP, :] = chosen.astype(F32).astype(BF16)
        scales.append(jnp.sum(jnp.where(chosen, weight, 0.0), axis=1, keepdims=True))
    copies[2].wait()
    copies[3].wait()
    for k in range(4):
        hot = placing[k * CAP : (k + 1) * CAP, :]
        outs[k][0:CAP, :] = nn(hot, token_copy[...]).astype(BF16)
        outs[k][CAP : 2 * CAP, :] = (scales[k] * nn(hot, grad_copy[...])).astype(BF16)


def fetch(own, other, joined, sems, names, place):
    half, width = own.shape[2:]
    copies = []
    for block in range(4):
        spot = lax.rem(place[2] - place[1] + block + 4, 4)
        columns = pl.ds(pl.multiple_of(spot * width, width), width)
        for n, m in enumerate(names):
            for h, source in enumerate((own, other)):
                copies.append(
                    pltpu.make_async_copy(
                        source.at[block, m],
                        joined.at[pl.ds((2 * n + h) * half, half), columns],
                        sems.at[block, n, h],
                    )
                )
    for copy in copies:
        copy.start()
    return copies


def take_rows(target, source, second):
    for k in range(4):
        first = (2 * k + second) * CAP
        target[k * CAP : (k + 1) * CAP, :] = source[first : first + CAP, :]


def project_kernel(names, second, place, *refs):
    rows, own, other = refs[0:4], refs[4], refs[5]
    keep, send, joined, wide, total, sems = refs[6:12]
    width = rows[0].shape[1]
    copies = fetch(own, other, joined, sems, names, place)
    for j in range(4):
        take_rows(wide.at[:, pl.ds(j * width, width)], rows[j], second)
    for copy in copies:
        copy.wait()
    total[...] = nt(wide[...], joined[...])
    part = keep.shape[0]
    keep[...] = total[pl.ds(pl.multiple_of(place[3] * part, 32), part), :]
    send[...] = total[pl.ds(pl.multiple_of((1 - place[3]) * part, 32), part), :].astype(BF16)


def pieces(values):
    high = values.astype(BF16)
    rest = values - high.astype(F32)
    middle = rest.astype(BF16)
    low = (rest - middle.astype(F32)).astype(BF16)
    return high, middle, low


def marked_rows(row, first):
    spot = lax.broadcasted_iota(jnp.int32, (TILE, row.shape[1]), 0)
    total = jnp.zeros(spot.shape, F32)
    for n, part in enumerate(pieces(row)):
        total += jnp.where(spot == first + n, part.astype(F32), 0.0)
    return total


def hidden_kernel(place, both, act, keep, far, out):
    part, width = keep.shape
    gate, up = both[:, 0:width], both[:, width : 2 * width]
    sigmoid = 1.0 / (1.0 + jnp.exp(-gate))
    swish = gate * sigmoid
    grad = keep[...] + far[...].astype(F32)
    out[0:part, 0:width] = (
        grad * up * sigmoid * (1.0 + gate * (1.0 - sigmoid))
    ).astype(BF16)
    out[0:part, width : 2 * width] = (grad * swish).astype(BF16)
    share = jnp.sum(act[...].astype(F32) * grad, axis=1, keepdims=True)
    out[part:, :] = jnp.zeros((TILE, out.shape[1]), BF16)
    marks = jnp.zeros((TILE, 128), F32)
    shape = (CAP, 128)
    same = lax.broadcasted_iota(jnp.int32, shape, 0) == lax.broadcasted_iota(jnp.int32, shape, 1)
    for n in range(2):
        row = jnp.sum(
            jnp.where(same, share[n * CAP : (n + 1) * CAP, :], 0.0), axis=0, keepdims=True
        )
        marks += marked_rows(row, 6 * place[3] + 3 * n)
    out[part:, 0:128] = marks.astype(BF16)


def join(target, mine, theirs, zl):
    part = target.shape[0] // 2
    target[pl.ds(pl.multiple_of(zl * part, 32), part), :] = mine[0:part, :]
    target[pl.ds(pl.multiple_of((1 - zl) * part, 32), part), :] = theirs[0:part, :]


def share_kernel(place, act, act_far, grad, grad_far, pair, down, *refs):
    outs, acts, grads = refs[0:4], *refs[4:6]
    part, width = act.shape[0], outs[0].shape[1]
    zl = place[3]
    join(acts, act, act_far, zl)
    join(grads, grad, grad_far, zl)
    marks = grad[part:, 0:128].astype(F32) + grad_far[part:, 0:128].astype(F32)
    unit = 2 * CAP
    for j in (1, 3, 2, 0):
        kind = outs[j].dtype
        columns = slice(j * width, (j + 1) * width)
        out = nn(acts[...], down[:, columns])
        back = nn(grads[...], pair[:, columns])
        for k in range(4):
            start, rows = k * unit, slice(k * CAP, (k + 1) * CAP)
            outs[j][start : start + CAP, :] = out[rows, :].astype(kind)
            outs[j][start + CAP : start + 2 * CAP, :] = back[rows, :].astype(kind)
    for j in range(4):
        kind = outs[j].dtype
        outs[j][4 * unit :, :] = jnp.zeros((TILE, width), kind)
        outs[j][4 * unit :, 0:128] = marks.astype(kind)


def total_kernel(place, own, one, three, *outs):
    unit = 2 * CAP

    def total(span, columns):
        value = own[span, columns] + one[span, columns].astype(F32)
        return value + three[span, columns].astype(F32)

    marks = total(slice(4 * unit, 4 * unit + TILE), slice(0, 128))
    width = own.shape[1]
    for k in range(4):
        outs[k][0:unit, :] = total(slice(k * unit, (k + 1) * unit), slice(0, width)).astype(BF16)
        row = jnp.sum(marks[3 * k : 3 * k + 3, :], axis=0, keepdims=True)
        outs[k][unit:, :] = jnp.zeros((TILE, width), BF16)
        outs[k][unit:, 0:128] = marked_rows(row, 0).astype(BF16)


def weight_kernel(second, place, near, far, *refs):
    rows, keep, send, joined, chosen = refs[0:4], *refs[4:8]
    half = keep.shape[2]
    join(joined, near, far, place[3])
    for j in range(4):
        block = lax.rem(place[1] - place[2] + j + 4, 4)
        take_rows(chosen, rows[j], second)
        total = tn(joined[...], chosen[...])
        for m in range(keep.shape[1]):
            keep[block, m] = total[2 * m * half : (2 * m + 1) * half, :]
            send[block, m] = total[(2 * m + 1) * half : (2 * m + 2) * half, :].astype(BF16)


def sum_kernel(place, pair, pair_far, down, down_far, own, one, two, three):
    def total(i, m):
        if m == 2:
            return down[i, 0] + down_far[i, 0].astype(F32)
        return pair[i, m] + pair_far[i, m].astype(F32)

    for m in range(3):
        for i, out in enumerate((own, one, two, three)):
            out[m] = total(i, m).astype(out.dtype)


def column(row):
    rows = row.shape[1]
    shape = (rows, rows)
    same = lax.broadcasted_iota(jnp.int32, shape, 0) == lax.broadcasted_iota(jnp.int32, shape, 1)
    return jnp.sum(jnp.where(same, row, 0.0), axis=1, keepdims=True)


def owner_kernel(place, ids, probs, placing, *refs):
    blocks, layer, token, prob = refs[0:4], *refs[4:7]
    total = jnp.zeros(layer.shape, F32)
    grads = jnp.zeros(token.shape, F32)
    shares = [jnp.zeros((1, ids.shape[1]), F32) for _ in range(2)]
    for k in range(4):
        one, two = expert_rows(place, ids, k)
        hot = placing[k * CAP : (k + 1) * CAP, :]
        weight = jnp.where(one, probs[0:1, :], 0.0) + jnp.where(two, probs[1:2, :], 0.0)
        total += column(weight) * tn(hot, blocks[k][0:CAP, :])
        grads += tn(hot, blocks[k][CAP : 2 * CAP, :])
        found = nn(blocks[k][2 * CAP :, 0:128][:, 0:CAP], hot)
        share = jnp.sum(found, axis=0, keepdims=True)
        shares[0] += jnp.where(one, share, 0.0)
        shares[1] += jnp.where(two, share, 0.0)
    layer[...] = total.astype(BF16)
    token[...] = grads.astype(BF16)
    prob[...] = jnp.zeros(prob.shape, F32)
    for n in range(2):
        prob[n : n + 1, :] = shares[n] / probs[n : n + 1, :]


def shift(value, axis, step):
    return lax.ppermute(value, axis, [(i, (i + step) % 4) for i in range(4)])


def relay(value, axis):
    steps = [(c, i, (i + (3 if c else 1)) % 4) for c in range(2) for i in range(4)]
    if axis == "x":
        return lax.ppermute(value, ("x", "core"), [(2 * i + c, 2 * j + c) for c, i, j in steps])
    return lax.ppermute(value, ("core", axis), [(4 * c + i, 4 * c + j) for c, i, j in steps])


def swap(value, axis):
    return lax.ppermute(value, axis, [(0, 1), (1, 0)])


def turn(value):
    return lax.ppermute(value, ("core", "zl"), [(2 * c + z, 2 * z + c) for c in range(2) for z in range(2)])


def body(tokens, expert_ids, gate_probs, stacked_weights, out_grad):
    rows, width = tokens.shape
    half = stacked_weights.shape[2]
    hidden = 2 * half
    slots = 4 * CAP
    part = slots // 2
    place = jnp.stack(
        [lax.axis_index(name) for name in ("expert", "x", "y", "zl")]
    ).astype(jnp.int32)
    ids, probs = expert_ids.T, gate_probs.T
    vmem = pl.BlockSpec(memory_space=pltpu.VMEM)
    hbm = pl.BlockSpec(memory_space=pl.ANY)
    far = pl.BlockSpec(memory_space=pltpu.HBM)

    placing, *blocks = call(
        slots_kernel,
        place,
        [ids, probs, tokens, out_grad],
        [((slots, rows), BF16)] + [((2 * CAP, width), BF16)] * 4,
        [
            pltpu.VMEM(ids.shape, jnp.int32),
            pltpu.VMEM(probs.shape, F32),
            pltpu.VMEM((rows, width), BF16),
            pltpu.VMEM((rows, width), BF16),
            pltpu.SemaphoreType.DMA((4,)),
        ],
        [far, far, far, far],
    )

    own, placing = lax.optimization_barrier((turn(stacked_weights[0]), placing))
    first = lax.axis_index("core") == 0
    near, back = shift(own, "x", 1), shift(own, "x", 3)
    blocks = [blocks[0]] + [shift(blocks[k], "expert", k) for k in (1, 2, 3)]
    blocks[2], near, back = lax.optimization_barrier((blocks[2], near, back))
    across = relay(jnp.where(first, near, back), "x")
    own = jnp.stack([own, near, across, back])
    blocks = [jnp.concatenate(blocks, axis=0)]
    near, back = shift(blocks[0], "y", 1), shift(blocks[0], "y", 3)
    own, near, back = lax.optimization_barrier((own, near, back))
    other = swap(own, "core")
    blocks += [near, relay(jnp.where(first, near, back), "y"), back]

    def project(names, second):
        wide = len(names) * hidden
        return call(
            functools.partial(project_kernel, names, second),
            place,
            blocks + [own, other],
            [((part, wide), F32), ((part, wide), BF16), ((wide, 4 * width), BF16)],
            [
                pltpu.VMEM((slots, 4 * width), BF16),
                pltpu.VMEM((slots, wide), F32),
                pltpu.SemaphoreType.DMA((4, 2, 2)),
            ],
            [vmem] * 4 + [hbm] * 2,
        )

    keep, send, pair_weights = project((0, 1), 0)
    both = keep + swap(send, "zl").astype(F32)
    gate, up = both[:, :hidden], both[:, hidden:]
    activation = (gate * jax.nn.sigmoid(gate) * up).astype(BF16)
    activation_far = swap(activation, "zl")
    keep, send, down_weights = project((2,), 1)
    send, activation_far = lax.optimization_barrier((swap(send, "zl"), activation_far))
    hidden_grad = call(
        hidden_kernel,
        place,
        [both, activation, keep, send],
        [((part + TILE, 2 * hidden), BF16)],
    )[0]
    hidden_far = swap(hidden_grad, "zl")

    def weight_terms(near, far, second):
        count = near.shape[1] // hidden
        shape = (4, count, half, width)
        return call(
            functools.partial(weight_kernel, second),
            place,
            [near, far] + blocks,
            [(shape, F32), (shape, BF16)],
            [pltpu.VMEM((slots, near.shape[1]), BF16), pltpu.VMEM((slots, width), BF16)],
        )

    down_keep, down_send = weight_terms(activation, activation_far, 1)
    hidden_far, down_keep = lax.optimization_barrier((hidden_far, down_keep))

    def halfway(passed, near, back):
        passed = passed.astype(F32)
        near = (near + jnp.where(first, 0.0, passed)).astype(BF16)
        return near, (back + jnp.where(first, passed, 0.0)).astype(BF16)

    unit = 2 * CAP + TILE
    shares = call(
        share_kernel,
        place,
        [activation, activation_far, hidden_grad, hidden_far, pair_weights, down_weights],
        [((8 * CAP + TILE, width), kind) for kind in (F32, F32, BF16, F32)],
        [pltpu.VMEM((slots, hidden), BF16), pltpu.VMEM((slots, 2 * hidden), BF16)],
    )
    passed = relay(shares[2], "y")
    shares[0], hidden_grad = lax.optimization_barrier((shares[0], hidden_grad))
    pair_keep, pair_send = weight_terms(hidden_grad, hidden_far, 0)
    pair_far = swap(pair_send, "core")
    passed, pair_far = lax.optimization_barrier((passed, pair_far))
    near, back = halfway(passed, shares[1], shares[3])
    arrived = [shift(near, "y", -1), shift(back, "y", 1)]
    mine, near, across, back = call(
        sum_kernel,
        place,
        [pair_keep, pair_far, down_keep, swap(down_send, "core")],
        [((3, half, width), kind) for kind in (F32, F32, BF16, F32)],
    )
    near, back = halfway(relay(across, "x"), near, back)
    near, back, *arrived = lax.optimization_barrier((near, back, *arrived))
    far_sums = [shift(near, "x", -1), shift(back, "x", 1)]
    totals = call(total_kernel, place, [shares[0]] + arrived, [((unit, width), BF16)] * 4)
    returned = [totals[0]] + [shift(totals[k], "expert", -k) for k in (1, 2, 3)]
    *far_sums, returned[1], returned[2], returned[3] = lax.optimization_barrier(
        (*far_sums, *returned[1:])
    )
    layer_output, token_grad, prob_grad = call(
        owner_kernel,
        place,
        [ids, probs, placing] + returned,
        [((rows, width), BF16), ((rows, width), BF16), ((8, rows), F32)],
    )
    weight_total = mine
    for block in far_sums:
        weight_total = weight_total + block.astype(F32)
    weight_grad = turn(weight_total.astype(BF16)).astype(F32)[None]
    return layer_output, token_grad, prob_grad[0:2].T, weight_grad


def solution(mesh):
    split = Mesh(
        mesh.devices.reshape(4, 2, 4, 4, 2), ("x", "core", "expert", "y", "zl")
    )
    rows = P(("x", "core", "expert"), ("y", "zl"))
    pairs = P(("x", "core", "expert"), None)
    weights = P("expert", None, ("y", "zl"), ("x", "core"))
    return jax.shard_map(
        body,
        mesh=split,
        in_specs=(rows, pairs, pairs, weights, rows),
        out_specs=(rows, rows, pairs, weights),
        check_vma=False,
    )
```

```python
import functools

import jax
import jax.numpy as jnp
from jax import lax
from jax.experimental import pallas as pl
from jax.experimental.pallas import tpu as pltpu
from jax.sharding import Mesh, PartitionSpec as P

F32 = jnp.float32
BF16 = jnp.bfloat16
CAP = 80
TILE = 16
PARAMS = pltpu.CompilerParams(vmem_limit_bytes=48 * 1024 * 1024)


def nn(a, b):
    return lax.dot_general(a, b, (((1,), (0,)), ((), ())), preferred_element_type=F32)


def nt(a, b):
    return lax.dot_general(a, b, (((1,), (1,)), ((), ())), preferred_element_type=F32)


def tn(a, b):
    return lax.dot_general(a, b, (((0,), (0,)), ((), ())), preferred_element_type=F32)


def call(kernel, place, args, outs, scratch=(), spaces=None):
    whole = pl.BlockSpec(memory_space=pltpu.VMEM)
    return list(pl.pallas_call(
        kernel,
        out_shape=[jax.ShapeDtypeStruct(shape, kind) for shape, kind in outs],
        in_specs=[pl.BlockSpec(memory_space=pltpu.SMEM)] + (spaces or [whole] * len(args)),
        out_specs=[whole] * len(outs),
        scratch_shapes=list(scratch),
        compiler_params=PARAMS,
    )(place, *args))


def expert_rows(place, ids, k):
    expert = lax.rem(place[0] + k, 4)
    return ids[0:1, :] == expert, ids[1:2, :] == expert


def slots_kernel(place, ids_far, probs_far, tokens, grads, placing, *refs):
    outs, ids, probs, token_copy, grad_copy, sems = refs[0:4], *refs[4:9]
    copies = [
        pltpu.make_async_copy(source, target, sems.at[n])
        for n, (source, target) in enumerate(
            [(ids_far, ids), (probs_far, probs), (tokens, token_copy), (grads, grad_copy)]
        )
    ]
    for copy in copies:
        copy.start()
    copies[0].wait()
    copies[1].wait()
    rows = ids.shape[1]
    before = (
        lax.broadcasted_iota(jnp.int32, (rows, rows), 0)
        < lax.broadcasted_iota(jnp.int32, (rows, rows), 1)
    ).astype(BF16)
    slot = lax.broadcasted_iota(jnp.int32, (CAP, rows), 0)
    scales = []
    for k in range(4):
        one, two = expert_rows(place, ids, k)
        named = jnp.logical_or(one, two)
        marks = jnp.broadcast_to(named, (8, rows)).astype(F32)
        position = nn(marks.astype(BF16), before)[0:1, :].astype(jnp.int32)
        weight = jnp.where(one, probs[0:1, :], probs[1:2, :])
        chosen = jnp.logical_and(
            jnp.broadcast_to(marks[0:1, :] > 0.5, (CAP, rows)),
            slot == jnp.broadcast_to(position, (CAP, rows)),
        )
        placing[k * CAP : (k + 1) * CAP, :] = chosen.astype(F32).astype(BF16)
        scales.append(jnp.sum(jnp.where(chosen, weight, 0.0), axis=1, keepdims=True))
    copies[2].wait()
    copies[3].wait()
    for k in range(4):
        hot = placing[k * CAP : (k + 1) * CAP, :]
        outs[k][0:CAP, :] = nn(hot, token_copy[...]).astype(BF16)
        outs[k][CAP : 2 * CAP, :] = (scales[k] * nn(hot, grad_copy[...])).astype(BF16)


def fetch(own, other, joined, sems, names, place):
    half, width = own[0].shape[1:]
    copies = []
    for block in range(4):
        spot = lax.rem(place[2] - place[1] + block + 4, 4)
        columns = pl.ds(pl.multiple_of(spot * width, width), width)
        for n, m in enumerate(names):
            for h, source in enumerate((own[block], other[block])):
                copies.append(
                    pltpu.make_async_copy(
                        source.at[m],
                        joined.at[pl.ds((2 * n + h) * half, half), columns],
                        sems.at[block, n, h],
                    )
                )
    for copy in copies:
        copy.start()
    return copies


def take_rows(target, source, second):
    for k in range(4):
        first = (2 * k + second) * CAP
        target[k * CAP : (k + 1) * CAP, :] = source[first : first + CAP, :]


def project_kernel(names, second, place, *refs):
    rows, own, other = refs[0:4], refs[4:8], refs[8:12]
    keep, send, joined, wide, total, sems = refs[12:18]
    width = rows[0].shape[1]
    copies = fetch(own, other, joined, sems, names, place)
    for j in range(4):
        take_rows(wide.at[:, pl.ds(j * width, width)], rows[j], second)
    for copy in copies:
        copy.wait()
    total[...] = nt(wide[...], joined[...])
    part = keep.shape[0]
    keep[...] = total[pl.ds(pl.multiple_of(place[3] * part, 32), part), :]
    send[...] = total[pl.ds(pl.multiple_of((1 - place[3]) * part, 32), part), :].astype(BF16)


def pieces(values):
    high = values.astype(BF16)
    rest = values - high.astype(F32)
    middle = rest.astype(BF16)
    low = (rest - middle.astype(F32)).astype(BF16)
    return high, middle, low


def marked_rows(row, first):
    spot = lax.broadcasted_iota(jnp.int32, (TILE, row.shape[1]), 0)
    total = jnp.zeros(spot.shape, F32)
    for n, part in enumerate(pieces(row)):
        total += jnp.where(spot == first + n, part.astype(F32), 0.0)
    return total


def hidden_kernel(place, both, act, keep, far, out):
    part, width = keep.shape
    gate, up = both[:, 0:width], both[:, width : 2 * width]
    sigmoid = 1.0 / (1.0 + jnp.exp(-gate))
    swish = gate * sigmoid
    grad = keep[...] + far[...].astype(F32)
    out[0:part, 0:width] = (
        grad * up * sigmoid * (1.0 + gate * (1.0 - sigmoid))
    ).astype(BF16)
    out[0:part, width : 2 * width] = (grad * swish).astype(BF16)
    share = jnp.sum(act[...].astype(F32) * grad, axis=1, keepdims=True)
    out[part:, :] = jnp.zeros((TILE, out.shape[1]), BF16)
    marks = jnp.zeros((TILE, 128), F32)
    shape = (CAP, 128)
    same = lax.broadcasted_iota(jnp.int32, shape, 0) == lax.broadcasted_iota(jnp.int32, shape, 1)
    for n in range(2):
        row = jnp.sum(
            jnp.where(same, share[n * CAP : (n + 1) * CAP, :], 0.0), axis=0, keepdims=True
        )
        marks += marked_rows(row, 6 * place[3] + 3 * n)
    out[part:, 0:128] = marks.astype(BF16)


def join(target, mine, theirs, zl):
    part = target.shape[0] // 2
    target[pl.ds(pl.multiple_of(zl * part, 32), part), :] = mine[0:part, :]
    target[pl.ds(pl.multiple_of((1 - zl) * part, 32), part), :] = theirs[0:part, :]


def share_kernel(place, act, act_far, grad, grad_far, pair, down, *refs):
    outs, acts, grads = refs[0:4], *refs[4:6]
    part, width = act.shape[0], outs[0].shape[1]
    zl = place[3]
    join(acts, act, act_far, zl)
    join(grads, grad, grad_far, zl)
    marks = grad[part:, 0:128].astype(F32) + grad_far[part:, 0:128].astype(F32)
    unit = 2 * CAP
    for j in (1, 3, 2, 0):
        kind = outs[j].dtype
        columns = slice(j * width, (j + 1) * width)
        out = nn(acts[...], down[:, columns])
        back = nn(grads[...], pair[:, columns])
        for k in range(4):
            start, rows = k * unit, slice(k * CAP, (k + 1) * CAP)
            outs[j][start : start + CAP, :] = out[rows, :].astype(kind)
            outs[j][start + CAP : start + 2 * CAP, :] = back[rows, :].astype(kind)
    for j in range(4):
        kind = outs[j].dtype
        outs[j][4 * unit :, :] = jnp.zeros((TILE, width), kind)
        outs[j][4 * unit :, 0:128] = marks.astype(kind)


def total_kernel(place, own, one, three, *outs):
    unit = 2 * CAP

    def total(span, columns):
        value = own[span, columns] + one[span, columns].astype(F32)
        return value + three[span, columns].astype(F32)

    marks = total(slice(4 * unit, 4 * unit + TILE), slice(0, 128))
    width = own.shape[1]
    for k in range(4):
        outs[k][0:unit, :] = total(slice(k * unit, (k + 1) * unit), slice(0, width)).astype(BF16)
        row = jnp.sum(marks[3 * k : 3 * k + 3, :], axis=0, keepdims=True)
        outs[k][unit:, :] = jnp.zeros((TILE, width), BF16)
        outs[k][unit:, 0:128] = marked_rows(row, 0).astype(BF16)


def weight_kernel(second, place, near, far, *refs):
    rows, keep, joined, chosen = refs[0:4], refs[4], *refs[-2:]
    sends = refs[5:-2]
    half = keep.shape[2]
    join(joined, near, far, place[3])
    for j in range(4):
        block = lax.rem(place[1] - place[2] + j + 4, 4)
        take_rows(chosen, rows[j], second)
        total = tn(joined[...], chosen[...])
        for m in range(keep.shape[1]):
            keep[block, m] = total[2 * m * half : (2 * m + 1) * half, :]
            sends[m][block] = total[(2 * m + 1) * half : (2 * m + 2) * half, :].astype(BF16)


def column(row):
    rows = row.shape[1]
    shape = (rows, rows)
    same = lax.broadcasted_iota(jnp.int32, shape, 0) == lax.broadcasted_iota(jnp.int32, shape, 1)
    return jnp.sum(jnp.where(same, row, 0.0), axis=1, keepdims=True)


def owner_kernel(place, ids, probs, placing, *refs):
    blocks, layer, token, prob = refs[0:4], *refs[4:7]
    total = jnp.zeros(layer.shape, F32)
    grads = jnp.zeros(token.shape, F32)
    shares = [jnp.zeros((1, ids.shape[1]), F32) for _ in range(2)]
    for k in range(4):
        one, two = expert_rows(place, ids, k)
        hot = placing[k * CAP : (k + 1) * CAP, :]
        weight = jnp.where(one, probs[0:1, :], 0.0) + jnp.where(two, probs[1:2, :], 0.0)
        total += column(weight) * tn(hot, blocks[k][0:CAP, :])
        grads += tn(hot, blocks[k][CAP : 2 * CAP, :])
        found = nn(blocks[k][2 * CAP :, 0:128][:, 0:CAP], hot)
        share = jnp.sum(found, axis=0, keepdims=True)
        shares[0] += jnp.where(one, share, 0.0)
        shares[1] += jnp.where(two, share, 0.0)
    layer[...] = total.astype(BF16)
    token[...] = grads.astype(BF16)
    prob[...] = jnp.zeros(prob.shape, F32)
    for n in range(2):
        prob[n : n + 1, :] = shares[n] / probs[n : n + 1, :]


def shift(value, axis, step):
    return lax.ppermute(value, axis, [(i, (i + step) % 4) for i in range(4)])


def relay(value, axis):
    steps = [(c, i, (i + (3 if c else 1)) % 4) for c in range(2) for i in range(4)]
    if axis == "x":
        return lax.ppermute(value, ("x", "core"), [(2 * i + c, 2 * j + c) for c, i, j in steps])
    return lax.ppermute(value, ("core", axis), [(4 * c + i, 4 * c + j) for c, i, j in steps])


def swap(value, axis):
    return lax.ppermute(value, axis, [(0, 1), (1, 0)])


def turn(value):
    return lax.ppermute(value, ("core", "zl"), [(2 * c + z, 2 * z + c) for c in range(2) for z in range(2)])


def body(tokens, expert_ids, gate_probs, stacked_weights, out_grad):
    rows, width = tokens.shape
    half = stacked_weights.shape[2]
    hidden = 2 * half
    slots = 4 * CAP
    part = slots // 2
    place = jnp.stack(
        [lax.axis_index(name) for name in ("expert", "x", "y", "zl")]
    ).astype(jnp.int32)
    ids, probs = expert_ids.T, gate_probs.T
    vmem = pl.BlockSpec(memory_space=pltpu.VMEM)
    hbm = pl.BlockSpec(memory_space=pl.ANY)
    far = pl.BlockSpec(memory_space=pltpu.HBM)

    placing, *blocks = call(
        slots_kernel,
        place,
        [ids, probs, tokens, out_grad],
        [((slots, rows), BF16)] + [((2 * CAP, width), BF16)] * 4,
        [
            pltpu.VMEM(ids.shape, jnp.int32),
            pltpu.VMEM(probs.shape, F32),
            pltpu.VMEM((rows, width), BF16),
            pltpu.VMEM((rows, width), BF16),
            pltpu.SemaphoreType.DMA((4,)),
        ],
        [far, far, far, far],
    )

    blocks = [blocks[0]] + [shift(blocks[k], "expert", k) for k in (1, 2, 3)]
    own, *blocks[1:] = lax.optimization_barrier((turn(stacked_weights[0]), *blocks[1:]))
    first = lax.axis_index("core") == 0
    near, back = shift(own, "x", 1), shift(own, "x", 3)
    own = [own, near, relay(jnp.where(first, near, back), "x"), back]
    blocks = [jnp.concatenate(blocks, axis=0)]
    near, back = shift(blocks[0], "y", 1), shift(blocks[0], "y", 3)
    own[0], own[1], own[3], near, back = lax.optimization_barrier(
        (own[0], own[1], own[3], near, back)
    )
    other = [swap(block, "core") for block in own]
    blocks += [near, relay(jnp.where(first, near, back), "y"), back]

    def project(names, second):
        wide = len(names) * hidden
        return call(
            functools.partial(project_kernel, names, second),
            place,
            blocks + own + other,
            [((part, wide), F32), ((part, wide), BF16), ((wide, 4 * width), BF16)],
            [
                pltpu.VMEM((slots, 4 * width), BF16),
                pltpu.VMEM((slots, wide), F32),
                pltpu.SemaphoreType.DMA((4, 2, 2)),
            ],
            [vmem] * 4 + [hbm] * 8,
        )

    keep, send, pair_weights = project((0, 1), 0)
    both = keep + swap(send, "zl").astype(F32)
    gate, up = both[:, :hidden], both[:, hidden:]
    activation = (gate * jax.nn.sigmoid(gate) * up).astype(BF16)
    activation_far = swap(activation, "zl")
    keep, send, down_weights = project((2,), 1)
    send, activation_far = lax.optimization_barrier((swap(send, "zl"), activation_far))
    hidden_grad = call(
        hidden_kernel,
        place,
        [both, activation, keep, send],
        [((part + TILE, 2 * hidden), BF16)],
    )[0]
    hidden_far = swap(hidden_grad, "zl")

    def weight_terms(near, far, second):
        count = near.shape[1] // hidden
        shape = (4, count, half, width)
        return call(
            functools.partial(weight_kernel, second),
            place,
            [near, far] + blocks,
            [(shape, F32)] + [((4, half, width), BF16)] * count,
            [pltpu.VMEM((slots, near.shape[1]), BF16), pltpu.VMEM((slots, width), BF16)],
        )

    down_keep, down_send = weight_terms(activation, activation_far, 1)
    hidden_far, down_keep = lax.optimization_barrier((hidden_far, down_keep))

    def halfway(passed, near, back):
        passed = passed.astype(F32)
        near = (near + jnp.where(first, 0.0, passed)).astype(BF16)
        return near, (back + jnp.where(first, passed, 0.0)).astype(BF16)

    unit = 2 * CAP + TILE
    shares = call(
        share_kernel,
        place,
        [activation, activation_far, hidden_grad, hidden_far, pair_weights, down_weights],
        [((8 * CAP + TILE, width), kind) for kind in (F32, F32, BF16, F32)],
        [pltpu.VMEM((slots, hidden), BF16), pltpu.VMEM((slots, 2 * hidden), BF16)],
    )
    passed = relay(shares[2], "y")
    shares[0], hidden_grad = lax.optimization_barrier((shares[0], hidden_grad))
    pair_keep, *pair_send = weight_terms(hidden_grad, hidden_far, 0)
    pair_far = [swap(send, "core") for send in pair_send]
    near, back = halfway(passed, shares[1], shares[3])
    near, back, *pair_far = lax.optimization_barrier((near, back, *pair_far))
    arrived = [shift(near, "y", -1), shift(back, "y", 1)]
    down_far = swap(down_send, "core")

    def both_cores(i):
        kept = (pair_keep[i, 0], pair_keep[i, 1], down_keep[i, 0])
        moved = (*pair_far, down_far)
        return jnp.stack([near + far[i].astype(F32) for near, far in zip(kept, moved)])

    passed = relay(both_cores(2).astype(BF16), "x")
    totals = call(total_kernel, place, [shares[0]] + arrived, [((unit, width), BF16)] * 4)
    passed, totals[0] = lax.optimization_barrier((passed, totals[0]))
    near, back = halfway(passed, both_cores(1), both_cores(3))
    far_sums = [shift(near, "x", -1), shift(back, "x", 1)]
    returned = [totals[0]] + [shift(totals[k], "expert", -k) for k in (1, 2, 3)]
    *far_sums, returned[1], returned[2], returned[3] = lax.optimization_barrier(
        (*far_sums, *returned[1:])
    )
    layer_output, token_grad, prob_grad = call(
        owner_kernel,
        place,
        [ids, probs, placing] + returned,
        [((rows, width), BF16), ((rows, width), BF16), ((8, rows), F32)],
    )
    weight_total = both_cores(0)
    for block in far_sums:
        weight_total = weight_total + block.astype(F32)
    weight_grad = turn(weight_total.astype(BF16)).astype(F32)[None]
    return layer_output, token_grad, prob_grad[0:2].T, weight_grad


def solution(mesh):
    split = Mesh(
        mesh.devices.reshape(4, 2, 4, 4, 2), ("x", "core", "expert", "y", "zl")
    )
    rows = P(("x", "core", "expert"), ("y", "zl"))
    pairs = P(("x", "core", "expert"), None)
    weights = P("expert", None, ("y", "zl"), ("x", "core"))
    return jax.shard_map(
        body,
        mesh=split,
        in_specs=(rows, pairs, pairs, weights, rows),
        out_specs=(rows, rows, pairs, weights),
        check_vma=False,
    )
```

```python
import functools

import jax
import jax.numpy as jnp
from jax import lax
from jax.experimental import pallas as pl
from jax.experimental.pallas import tpu as pltpu
from jax.sharding import Mesh, PartitionSpec as P

F32 = jnp.float32
BF16 = jnp.bfloat16
CAP = 80
TILE = 16
PARAMS = pltpu.CompilerParams(vmem_limit_bytes=48 * 1024 * 1024)


def nn(a, b):
    return lax.dot_general(a, b, (((1,), (0,)), ((), ())), preferred_element_type=F32)


def nt(a, b):
    return lax.dot_general(a, b, (((1,), (1,)), ((), ())), preferred_element_type=F32)


def tn(a, b):
    return lax.dot_general(a, b, (((0,), (0,)), ((), ())), preferred_element_type=F32)


def call(kernel, place, args, outs, scratch=(), spaces=None):
    whole = pl.BlockSpec(memory_space=pltpu.VMEM)
    return list(pl.pallas_call(
        kernel,
        out_shape=[jax.ShapeDtypeStruct(shape, kind) for shape, kind in outs],
        in_specs=[pl.BlockSpec(memory_space=pltpu.SMEM)] + (spaces or [whole] * len(args)),
        out_specs=[whole] * len(outs),
        scratch_shapes=list(scratch),
        compiler_params=PARAMS,
    )(place, *args))


def expert_rows(place, ids, k):
    expert = lax.rem(place[0] + k, 4)
    return ids[0:1, :] == expert, ids[1:2, :] == expert


def slots_kernel(place, ids_far, probs_far, tokens, grads, placing, *refs):
    outs, ids, probs, token_copy, grad_copy, sems = refs[0:4], *refs[4:9]
    copies = [
        pltpu.make_async_copy(source, target, sems.at[n])
        for n, (source, target) in enumerate(
            [(ids_far, ids), (probs_far, probs), (tokens, token_copy), (grads, grad_copy)]
        )
    ]
    for copy in copies:
        copy.start()
    copies[0].wait()
    copies[1].wait()
    rows = ids.shape[1]
    before = (
        lax.broadcasted_iota(jnp.int32, (rows, rows), 0)
        < lax.broadcasted_iota(jnp.int32, (rows, rows), 1)
    ).astype(BF16)
    slot = lax.broadcasted_iota(jnp.int32, (CAP, rows), 0)
    scales = []
    for k in range(4):
        one, two = expert_rows(place, ids, k)
        named = jnp.logical_or(one, two)
        marks = jnp.broadcast_to(named, (8, rows)).astype(F32)
        position = nn(marks.astype(BF16), before)[0:1, :].astype(jnp.int32)
        weight = jnp.where(one, probs[0:1, :], probs[1:2, :])
        chosen = jnp.logical_and(
            jnp.broadcast_to(marks[0:1, :] > 0.5, (CAP, rows)),
            slot == jnp.broadcast_to(position, (CAP, rows)),
        )
        placing[k * CAP : (k + 1) * CAP, :] = chosen.astype(F32).astype(BF16)
        scales.append(jnp.sum(jnp.where(chosen, weight, 0.0), axis=1, keepdims=True))
    copies[2].wait()
    copies[3].wait()
    for k in range(4):
        hot = placing[k * CAP : (k + 1) * CAP, :]
        outs[k][0:CAP, :] = nn(hot, token_copy[...]).astype(BF16)
        outs[k][CAP : 2 * CAP, :] = (scales[k] * nn(hot, grad_copy[...])).astype(BF16)


def fetch(own, other, joined, sems, names, place):
    half, width = own[0].shape[1:]
    copies = []
    for block in range(4):
        spot = lax.rem(place[2] - place[1] + block + 4, 4)
        columns = pl.ds(pl.multiple_of(spot * width, width), width)
        for n, m in enumerate(names):
            for h, source in enumerate((own[block], other[block])):
                copies.append(
                    pltpu.make_async_copy(
                        source.at[m],
                        joined.at[pl.ds((2 * n + h) * half, half), columns],
                        sems.at[block, n, h],
                    )
                )
    for copy in copies:
        copy.start()
    return copies


def take_rows(target, source, second):
    for k in range(4):
        first = (2 * k + second) * CAP
        target[k * CAP : (k + 1) * CAP, :] = source[first : first + CAP, :]


def project_kernel(names, second, place, *refs):
    rows, own, other = refs[0:4], refs[4:8], refs[8:12]
    keep, send, joined, wide, total, sems = refs[12:18]
    width = rows[0].shape[1]
    copies = fetch(own, other, joined, sems, names, place)
    for j in range(4):
        take_rows(wide.at[:, pl.ds(j * width, width)], rows[j], second)
    for copy in copies:
        copy.wait()
    total[...] = nt(wide[...], joined[...])
    part = keep.shape[0]
    keep[...] = total[pl.ds(pl.multiple_of(place[3] * part, 32), part), :]
    send[...] = total[pl.ds(pl.multiple_of((1 - place[3]) * part, 32), part), :].astype(BF16)


def pieces(values):
    high = values.astype(BF16)
    rest = values - high.astype(F32)
    middle = rest.astype(BF16)
    low = (rest - middle.astype(F32)).astype(BF16)
    return high, middle, low


def marked_rows(row, first):
    spot = lax.broadcasted_iota(jnp.int32, (TILE, row.shape[1]), 0)
    total = jnp.zeros(spot.shape, F32)
    for n, part in enumerate(pieces(row)):
        total += jnp.where(spot == first + n, part.astype(F32), 0.0)
    return total


def hidden_kernel(place, both, act, keep, far, out):
    part, width = keep.shape
    gate, up = both[:, 0:width], both[:, width : 2 * width]
    sigmoid = 1.0 / (1.0 + jnp.exp(-gate))
    swish = gate * sigmoid
    grad = keep[...] + far[...].astype(F32)
    out[0:part, 0:width] = (
        grad * up * sigmoid * (1.0 + gate * (1.0 - sigmoid))
    ).astype(BF16)
    out[0:part, width : 2 * width] = (grad * swish).astype(BF16)
    share = jnp.sum(act[...].astype(F32) * grad, axis=1, keepdims=True)
    out[part:, :] = jnp.zeros((TILE, out.shape[1]), BF16)
    marks = jnp.zeros((TILE, 128), F32)
    shape = (CAP, 128)
    same = lax.broadcasted_iota(jnp.int32, shape, 0) == lax.broadcasted_iota(jnp.int32, shape, 1)
    for n in range(2):
        row = jnp.sum(
            jnp.where(same, share[n * CAP : (n + 1) * CAP, :], 0.0), axis=0, keepdims=True
        )
        marks += marked_rows(row, 6 * place[3] + 3 * n)
    out[part:, 0:128] = marks.astype(BF16)


def join(target, mine, theirs, zl):
    part = target.shape[0] // 2
    target[pl.ds(pl.multiple_of(zl * part, 32), part), :] = mine[0:part, :]
    target[pl.ds(pl.multiple_of((1 - zl) * part, 32), part), :] = theirs[0:part, :]


def share_kernel(place, act, act_far, grad, grad_far, pair, down, *refs):
    outs, acts, grads = refs[0:4], *refs[4:6]
    part, width = act.shape[0], outs[0].shape[1]
    zl = place[3]
    join(acts, act, act_far, zl)
    join(grads, grad, grad_far, zl)
    marks = grad[part:, 0:128].astype(F32) + grad_far[part:, 0:128].astype(F32)
    unit = 2 * CAP
    for j in (1, 3, 2, 0):
        kind = outs[j].dtype
        columns = slice(j * width, (j + 1) * width)
        out = nn(acts[...], down[:, columns])
        back = nn(grads[...], pair[:, columns])
        for k in range(4):
            start, rows = k * unit, slice(k * CAP, (k + 1) * CAP)
            outs[j][start : start + CAP, :] = out[rows, :].astype(kind)
            outs[j][start + CAP : start + 2 * CAP, :] = back[rows, :].astype(kind)
    for j in range(4):
        kind = outs[j].dtype
        outs[j][4 * unit :, :] = jnp.zeros((TILE, width), kind)
        outs[j][4 * unit :, 0:128] = marks.astype(kind)


def total_kernel(place, own, one, three, *outs):
    unit = 2 * CAP

    def total(span, columns):
        value = own[span, columns] + one[span, columns].astype(F32)
        return value + three[span, columns].astype(F32)

    marks = total(slice(4 * unit, 4 * unit + TILE), slice(0, 128))
    width = own.shape[1]
    for k in range(4):
        outs[k][0:unit, :] = total(slice(k * unit, (k + 1) * unit), slice(0, width)).astype(BF16)
        row = jnp.sum(marks[3 * k : 3 * k + 3, :], axis=0, keepdims=True)
        outs[k][unit:, :] = jnp.zeros((TILE, width), BF16)
        outs[k][unit:, 0:128] = marked_rows(row, 0).astype(BF16)


def weight_kernel(second, place, near, far, *refs):
    rows, keep, joined, chosen = refs[0:4], refs[4], *refs[-2:]
    sends = refs[5:-2]
    half = keep.shape[2]
    join(joined, near, far, place[3])
    for j in range(4):
        block = lax.rem(place[1] - place[2] + j + 4, 4)
        take_rows(chosen, rows[j], second)
        total = tn(joined[...], chosen[...])
        for m in range(keep.shape[1]):
            keep[block, m] = total[2 * m * half : (2 * m + 1) * half, :]
            sends[m][block] = total[(2 * m + 1) * half : (2 * m + 2) * half, :].astype(BF16)


def column(row):
    rows = row.shape[1]
    shape = (rows, rows)
    same = lax.broadcasted_iota(jnp.int32, shape, 0) == lax.broadcasted_iota(jnp.int32, shape, 1)
    return jnp.sum(jnp.where(same, row, 0.0), axis=1, keepdims=True)


def owner_kernel(place, ids, probs, placing, *refs):
    blocks, layer, token, prob = refs[0:4], *refs[4:7]
    total = jnp.zeros(layer.shape, F32)
    grads = jnp.zeros(token.shape, F32)
    shares = [jnp.zeros((1, ids.shape[1]), F32) for _ in range(2)]
    for k in range(4):
        one, two = expert_rows(place, ids, k)
        hot = placing[k * CAP : (k + 1) * CAP, :]
        weight = jnp.where(one, probs[0:1, :], 0.0) + jnp.where(two, probs[1:2, :], 0.0)
        total += column(weight) * tn(hot, blocks[k][0:CAP, :])
        grads += tn(hot, blocks[k][CAP : 2 * CAP, :])
        found = nn(blocks[k][2 * CAP :, 0:128][:, 0:CAP], hot)
        share = jnp.sum(found, axis=0, keepdims=True)
        shares[0] += jnp.where(one, share, 0.0)
        shares[1] += jnp.where(two, share, 0.0)
    layer[...] = total.astype(BF16)
    token[...] = grads.astype(BF16)
    prob[...] = jnp.zeros(prob.shape, F32)
    for n in range(2):
        prob[n : n + 1, :] = shares[n] / probs[n : n + 1, :]


def shift(value, axis, step):
    return lax.ppermute(value, axis, [(i, (i + step) % 4) for i in range(4)])


def relay(value, axis):
    steps = [(c, i, (i + (3 if c else 1)) % 4) for c in range(2) for i in range(4)]
    if axis == "x":
        return lax.ppermute(value, ("x", "core"), [(2 * i + c, 2 * j + c) for c, i, j in steps])
    return lax.ppermute(value, ("core", axis), [(4 * c + i, 4 * c + j) for c, i, j in steps])


def swap(value, axis):
    return lax.ppermute(value, axis, [(0, 1), (1, 0)])


def turn(value):
    return lax.ppermute(value, ("core", "zl"), [(2 * c + z, 2 * z + c) for c in range(2) for z in range(2)])


def body(tokens, expert_ids, gate_probs, stacked_weights, out_grad):
    rows, width = tokens.shape
    half = stacked_weights.shape[2]
    hidden = 2 * half
    slots = 4 * CAP
    part = slots // 2
    place = jnp.stack(
        [lax.axis_index(name) for name in ("expert", "x", "y", "zl")]
    ).astype(jnp.int32)
    ids, probs = expert_ids.T, gate_probs.T
    vmem = pl.BlockSpec(memory_space=pltpu.VMEM)
    hbm = pl.BlockSpec(memory_space=pl.ANY)
    far = pl.BlockSpec(memory_space=pltpu.HBM)

    placing, *blocks = call(
        slots_kernel,
        place,
        [ids, probs, tokens, out_grad],
        [((slots, rows), BF16)] + [((2 * CAP, width), BF16)] * 4,
        [
            pltpu.VMEM(ids.shape, jnp.int32),
            pltpu.VMEM(probs.shape, F32),
            pltpu.VMEM((rows, width), BF16),
            pltpu.VMEM((rows, width), BF16),
            pltpu.SemaphoreType.DMA((4,)),
        ],
        [far, far, far, far],
    )

    blocks = [blocks[0]] + [shift(blocks[k], "expert", k) for k in (1, 2, 3)]
    own, blocks[0] = lax.optimization_barrier((stacked_weights[0], blocks[0]))
    own = turn(own)
    first = lax.axis_index("core") == 0
    near, back = shift(own, "x", 1), shift(own, "x", 3)
    own = [own, near, relay(jnp.where(first, near, back), "x"), back]
    blocks = [jnp.concatenate(blocks, axis=0)]
    near, back = shift(blocks[0], "y", 1), shift(blocks[0], "y", 3)
    own[0], own[1], own[3], near, back = lax.optimization_barrier(
        (own[0], own[1], own[3], near, back)
    )
    other = [swap(block, "core") for block in own]
    blocks += [near, relay(jnp.where(first, near, back), "y"), back]

    def project(names, second):
        wide = len(names) * hidden
        return call(
            functools.partial(project_kernel, names, second),
            place,
            blocks + own + other,
            [((part, wide), F32), ((part, wide), BF16), ((wide, 4 * width), BF16)],
            [
                pltpu.VMEM((slots, 4 * width), BF16),
                pltpu.VMEM((slots, wide), F32),
                pltpu.SemaphoreType.DMA((4, 2, 2)),
            ],
            [vmem] * 4 + [hbm] * 8,
        )

    keep, send, pair_weights = project((0, 1), 0)
    both = keep + swap(send, "zl").astype(F32)
    gate, up = both[:, :hidden], both[:, hidden:]
    activation = (gate * jax.nn.sigmoid(gate) * up).astype(BF16)
    activation_far = swap(activation, "zl")
    keep, send, down_weights = project((2,), 1)
    send, activation_far = lax.optimization_barrier((swap(send, "zl"), activation_far))
    hidden_grad = call(
        hidden_kernel,
        place,
        [both, activation, keep, send],
        [((part + TILE, 2 * hidden), BF16)],
    )[0]
    hidden_far = swap(hidden_grad, "zl")

    def weight_terms(near, far, second):
        count = near.shape[1] // hidden
        shape = (4, count, half, width)
        return call(
            functools.partial(weight_kernel, second),
            place,
            [near, far] + blocks,
            [(shape, F32)] + [((4, half, width), BF16)] * count,
            [pltpu.VMEM((slots, near.shape[1]), BF16), pltpu.VMEM((slots, width), BF16)],
        )

    down_keep, down_send = weight_terms(activation, activation_far, 1)
    hidden_far, down_keep = lax.optimization_barrier((hidden_far, down_keep))

    def halfway(passed, near, back):
        passed = passed.astype(F32)
        near = (near + jnp.where(first, 0.0, passed)).astype(BF16)
        return near, (back + jnp.where(first, passed, 0.0)).astype(BF16)

    unit = 2 * CAP + TILE
    shares = call(
        share_kernel,
        place,
        [activation, activation_far, hidden_grad, hidden_far, pair_weights, down_weights],
        [((8 * CAP + TILE, width), kind) for kind in (F32, F32, BF16, F32)],
        [pltpu.VMEM((slots, hidden), BF16), pltpu.VMEM((slots, 2 * hidden), BF16)],
    )
    passed = relay(shares[2], "y")
    shares[0], hidden_grad = lax.optimization_barrier((shares[0], hidden_grad))
    pair_keep, *pair_send = weight_terms(hidden_grad, hidden_far, 0)
    pair_far = [swap(send, "core") for send in pair_send]
    near, back = halfway(passed, shares[1], shares[3])
    near, back, *pair_far = lax.optimization_barrier((near, back, *pair_far))
    arrived = [shift(near, "y", -1), shift(back, "y", 1)]
    down_far = swap(down_send, "core")

    def both_cores(i):
        kept = (pair_keep[i, 0], pair_keep[i, 1], down_keep[i, 0])
        moved = (*pair_far, down_far)
        return jnp.stack([near + far[i].astype(F32) for near, far in zip(kept, moved)])

    passed = relay(both_cores(2).astype(BF16), "x")
    passed, arrived[0] = lax.optimization_barrier((passed, arrived[0]))
    near, back = halfway(passed, both_cores(1), both_cores(3))
    far_sums = [shift(near, "x", -1), shift(back, "x", 1)]
    totals = call(total_kernel, place, [shares[0]] + arrived, [((unit, width), BF16)] * 4)
    returned = [totals[0]] + [shift(totals[k], "expert", -k) for k in (1, 2, 3)]
    layer_output, token_grad, prob_grad = call(
        owner_kernel,
        place,
        [ids, probs, placing] + returned,
        [((rows, width), BF16), ((rows, width), BF16), ((8, rows), F32)],
    )
    weight_total = both_cores(0)
    for block in far_sums:
        weight_total = weight_total + block.astype(F32)
    weight_total = weight_total.astype(BF16).reshape(2, 3 * half // 2, width)
    parts = [turn(weight_total[n]) for n in range(2)]
    *parts, layer_output = lax.optimization_barrier((*parts, layer_output))
    weight_grad = jnp.concatenate([part.astype(F32) for part in parts])
    weight_grad = weight_grad.reshape(stacked_weights.shape)
    return layer_output, token_grad, prob_grad[0:2].T, weight_grad


def solution(mesh):
    split = Mesh(
        mesh.devices.reshape(4, 2, 4, 4, 2), ("x", "core", "expert", "y", "zl")
    )
    rows = P(("x", "core", "expert"), ("y", "zl"))
    pairs = P(("x", "core", "expert"), None)
    weights = P("expert", None, ("y", "zl"), ("x", "core"))
    return jax.shard_map(
        body,
        mesh=split,
        in_specs=(rows, pairs, pairs, weights, rows),
        out_specs=(rows, rows, pairs, weights),
        check_vma=False,
    )
```

```python
import functools

import jax
import jax.numpy as jnp
from jax import lax
from jax.experimental import pallas as pl
from jax.experimental.pallas import tpu as pltpu
from jax.sharding import Mesh, PartitionSpec as P

F32 = jnp.float32
BF16 = jnp.bfloat16
CAP = 80
TILE = 16
PARAMS = pltpu.CompilerParams(vmem_limit_bytes=48 * 1024 * 1024)


def nn(a, b):
    return lax.dot_general(a, b, (((1,), (0,)), ((), ())), preferred_element_type=F32)


def nt(a, b):
    return lax.dot_general(a, b, (((1,), (1,)), ((), ())), preferred_element_type=F32)


def tn(a, b):
    return lax.dot_general(a, b, (((0,), (0,)), ((), ())), preferred_element_type=F32)


def call(kernel, place, args, outs, scratch=(), spaces=None):
    whole = pl.BlockSpec(memory_space=pltpu.VMEM)
    return list(pl.pallas_call(
        kernel,
        out_shape=[jax.ShapeDtypeStruct(shape, kind) for shape, kind in outs],
        in_specs=[pl.BlockSpec(memory_space=pltpu.SMEM)] + (spaces or [whole] * len(args)),
        out_specs=[whole] * len(outs),
        scratch_shapes=list(scratch),
        compiler_params=PARAMS,
    )(place, *args))


def expert_rows(place, ids, k):
    expert = lax.rem(place[0] + k, 4).astype(F32)
    return ids[0:1, :] == expert, ids[1:2, :] == expert


def slots_kernel(place, small, wide, placing, *outs):
    ids, probs = small.at[0:2], small.at[2:4]
    width = wide.shape[1] // 2
    rows = ids.shape[1]
    before = (
        lax.broadcasted_iota(jnp.int32, (rows, rows), 0)
        < lax.broadcasted_iota(jnp.int32, (rows, rows), 1)
    ).astype(BF16)
    slot = lax.broadcasted_iota(jnp.int32, (CAP, rows), 0)
    scales = []
    for k in range(4):
        one, two = expert_rows(place, ids, k)
        named = jnp.logical_or(one, two)
        marks = jnp.broadcast_to(named, (8, rows)).astype(F32)
        position = nn(marks.astype(BF16), before)[0:1, :].astype(jnp.int32)
        weight = jnp.where(one, probs[0:1, :], probs[1:2, :])
        chosen = jnp.logical_and(
            jnp.broadcast_to(marks[0:1, :] > 0.5, (CAP, rows)),
            slot == jnp.broadcast_to(position, (CAP, rows)),
        )
        placing[k * CAP : (k + 1) * CAP, :] = chosen.astype(F32).astype(BF16)
        scales.append(jnp.sum(jnp.where(chosen, weight, 0.0), axis=1, keepdims=True))
    for k in range(4):
        hot = placing[k * CAP : (k + 1) * CAP, :]
        outs[k][0:CAP, :] = nn(hot, wide[:, 0:width]).astype(BF16)
        outs[k][CAP : 2 * CAP, :] = (scales[k] * nn(hot, wide[:, width:])).astype(BF16)


def fetch(own, other, joined, sems, place):
    half, width = own[0].shape[1:]
    copies = []
    for block in range(4):
        spot = lax.rem(place[2] - place[1] + block + 4, 4)
        columns = pl.ds(pl.multiple_of(spot * width, width), width)
        for m in range(3):
            for h, source in enumerate((own[block], other[block])):
                copies.append(
                    pltpu.make_async_copy(
                        source.at[m],
                        joined.at[pl.ds((2 * m + h) * half, half), columns],
                        sems.at[block, m, h],
                    )
                )
    for copy in copies:
        copy.start()
    return copies


def take_rows(target, source, second):
    for k in range(4):
        first = (2 * k + second) * CAP
        target[k * CAP : (k + 1) * CAP, :] = source[first : first + CAP, :]


def project_kernel(place, *refs):
    rows, own, other = refs[0:4], refs[4:8], refs[8:12]
    keep, send, joined, wide, total, sems = refs[12:18]
    width = rows[0].shape[1]
    hidden = keep.shape[1] // 3
    copies = fetch(own, other, joined, sems, place)
    for second in range(2):
        for j in range(4):
            take_rows(wide.at[second, :, pl.ds(j * width, width)], rows[j], second)
    for copy in copies:
        copy.wait()
    total[:, 0 : 2 * hidden] = nt(wide[0], joined[0 : 2 * hidden, :])
    total[:, 2 * hidden :] = nt(wide[1], joined[2 * hidden :, :])
    part = keep.shape[0]
    keep[...] = total[pl.ds(pl.multiple_of(place[3] * part, 32), part), :]
    send[...] = total[pl.ds(pl.multiple_of((1 - place[3]) * part, 32), part), :].astype(BF16)


def pieces(values):
    high = values.astype(BF16)
    rest = values - high.astype(F32)
    middle = rest.astype(BF16)
    low = (rest - middle.astype(F32)).astype(BF16)
    return high, middle, low


def marked_rows(row, first):
    spot = lax.broadcasted_iota(jnp.int32, (TILE, row.shape[1]), 0)
    total = jnp.zeros(spot.shape, F32)
    for n, part in enumerate(pieces(row)):
        total += jnp.where(spot == first + n, part.astype(F32), 0.0)
    return total


def hidden_kernel(place, keep, far, out):
    part, width = keep.shape[0], keep.shape[1] // 3
    gate, up, grad = [
        keep[:, n * width : (n + 1) * width] + far[:, n * width : (n + 1) * width].astype(F32)
        for n in range(3)
    ]
    sigmoid = 1.0 / (1.0 + jnp.exp(-gate))
    swish = gate * sigmoid
    act = (swish * up).astype(BF16)
    out[0:part, 0:width] = (
        grad * up * sigmoid * (1.0 + gate * (1.0 - sigmoid))
    ).astype(BF16)
    out[0:part, width : 2 * width] = (grad * swish).astype(BF16)
    out[0:part, 2 * width :] = act
    share = jnp.sum(act.astype(F32) * grad, axis=1, keepdims=True)
    out[part:, :] = jnp.zeros((TILE, out.shape[1]), BF16)
    marks = jnp.zeros((TILE, 128), F32)
    shape = (CAP, 128)
    same = lax.broadcasted_iota(jnp.int32, shape, 0) == lax.broadcasted_iota(jnp.int32, shape, 1)
    for n in range(2):
        row = jnp.sum(
            jnp.where(same, share[n * CAP : (n + 1) * CAP, :], 0.0), axis=0, keepdims=True
        )
        marks += marked_rows(row, 6 * place[3] + 3 * n)
    out[part:, 0:128] = marks.astype(BF16)


def join(target, mine, theirs, zl):
    part = target.shape[0] // 2
    target[pl.ds(pl.multiple_of(zl * part, 32), part), :] = mine[0:part, :]
    target[pl.ds(pl.multiple_of((1 - zl) * part, 32), part), :] = theirs[0:part, :]


def share_kernel(place, near, far, weights, *refs):
    outs, joined = refs[0:4], refs[4]
    part, width = joined.shape[0] // 2, outs[0].shape[1]
    hidden = near.shape[1] // 3
    join(joined, near, far, place[3])
    marks = near[part:, 0:128].astype(F32) + far[part:, 0:128].astype(F32)
    unit = 2 * CAP
    for j in (1, 3, 2, 0):
        kind = outs[j].dtype
        columns = slice(j * width, (j + 1) * width)
        out = nn(joined[:, 2 * hidden :], weights[2 * hidden :, columns])
        back = nn(joined[:, 0 : 2 * hidden], weights[0 : 2 * hidden, columns])
        for k in range(4):
            start, rows = k * unit, slice(k * CAP, (k + 1) * CAP)
            outs[j][start : start + CAP, :] = out[rows, :].astype(kind)
            outs[j][start + CAP : start + 2 * CAP, :] = back[rows, :].astype(kind)
    for j in range(4):
        kind = outs[j].dtype
        outs[j][4 * unit :, :] = jnp.zeros((TILE, width), kind)
        outs[j][4 * unit :, 0:128] = marks.astype(kind)


def total_kernel(place, own, one, three, *outs):
    unit = 2 * CAP

    def total(span, columns):
        value = own[span, columns] + one[span, columns].astype(F32)
        return value + three[span, columns].astype(F32)

    marks = total(slice(4 * unit, 4 * unit + TILE), slice(0, 128))
    width = own.shape[1]
    for k in range(4):
        outs[k][0:unit, :] = total(slice(k * unit, (k + 1) * unit), slice(0, width)).astype(BF16)
        row = jnp.sum(marks[3 * k : 3 * k + 3, :], axis=0, keepdims=True)
        outs[k][unit:, :] = jnp.zeros((TILE, width), BF16)
        outs[k][unit:, 0:128] = marked_rows(row, 0).astype(BF16)


def weight_kernel(place, near, far, *refs):
    rows, keep, sends = refs[0:4], refs[4], refs[5:8]
    joined, chosen = refs[8:10]
    half = keep.shape[2]
    join(joined, near, far, place[3])
    for j in range(4):
        block = lax.rem(place[1] - place[2] + j + 4, 4)
        for m, second in ((2, 1), (0, 0), (1, 0)):
            if m != 1:
                take_rows(chosen, rows[j], second)
            total = tn(joined[:, 2 * m * half : 2 * (m + 1) * half], chosen[...])
            keep[block, m] = total[0:half, :]
            sends[m][block] = total[half:, :].astype(BF16)


def column(row):
    rows = row.shape[1]
    shape = (rows, rows)
    same = lax.broadcasted_iota(jnp.int32, shape, 0) == lax.broadcasted_iota(jnp.int32, shape, 1)
    return jnp.sum(jnp.where(same, row, 0.0), axis=1, keepdims=True)


def owner_kernel(place, small, placing, *refs):
    ids, probs = small.at[0:2], small.at[2:4]
    blocks, layer, token, prob = refs[0:4], *refs[4:7]
    total = jnp.zeros(layer.shape, F32)
    grads = jnp.zeros(token.shape, F32)
    shares = [jnp.zeros((1, ids.shape[1]), F32) for _ in range(2)]
    for k in range(4):
        one, two = expert_rows(place, ids, k)
        hot = placing[k * CAP : (k + 1) * CAP, :]
        weight = jnp.where(one, probs[0:1, :], 0.0) + jnp.where(two, probs[1:2, :], 0.0)
        total += column(weight) * tn(hot, blocks[k][0:CAP, :])
        grads += tn(hot, blocks[k][CAP : 2 * CAP, :])
        found = nn(blocks[k][2 * CAP :, 0:128][:, 0:CAP], hot)
        share = jnp.sum(found, axis=0, keepdims=True)
        shares[0] += jnp.where(one, share, 0.0)
        shares[1] += jnp.where(two, share, 0.0)
    layer[...] = total.astype(BF16)
    token[...] = grads.astype(BF16)
    prob[...] = jnp.zeros(prob.shape, F32)
    for n in range(2):
        prob[n : n + 1, :] = shares[n] / probs[n : n + 1, :]


def shift(value, axis, step):
    return lax.ppermute(value, axis, [(i, (i + step) % 4) for i in range(4)])


def relay(value, axis):
    steps = [(c, i, (i + (3 if c else 1)) % 4) for c in range(2) for i in range(4)]
    if axis == "x":
        return lax.ppermute(value, ("x", "core"), [(2 * i + c, 2 * j + c) for c, i, j in steps])
    return lax.ppermute(value, ("core", axis), [(4 * c + i, 4 * c + j) for c, i, j in steps])


def swap(value, axis):
    return lax.ppermute(value, axis, [(0, 1), (1, 0)])


def turn(value):
    return lax.ppermute(value, ("core", "zl"), [(2 * c + z, 2 * z + c) for c in range(2) for z in range(2)])


def body(tokens, expert_ids, gate_probs, stacked_weights, out_grad):
    rows, width = tokens.shape
    half = stacked_weights.shape[2]
    hidden = 2 * half
    slots = 4 * CAP
    part = slots // 2
    place = jnp.stack(
        [lax.axis_index(name) for name in ("expert", "x", "y", "zl", "core")]
    ).astype(jnp.int32)
    small = jnp.concatenate([expert_ids.T.astype(F32), gate_probs.T])
    wide = jnp.concatenate([tokens, out_grad], axis=1)
    vmem = pl.BlockSpec(memory_space=pltpu.VMEM)
    hbm = pl.BlockSpec(memory_space=pl.ANY)

    placing, *blocks = call(
        slots_kernel,
        place,
        [small, wide],
        [((slots, rows), BF16)] + [((2 * CAP, width), BF16)] * 4,
    )

    blocks = [blocks[0]] + [shift(blocks[k], "expert", k) for k in (1, 2, 3)]
    own, blocks[0] = lax.optimization_barrier((stacked_weights[0], blocks[0]))
    turned = lax.ppermute(own, ("core", "zl"), [(1, 2), (2, 1)])
    own = jnp.where(place[4] == place[3], own, turned)
    first = lax.axis_index("core") == 0
    near, back = shift(own, "x", 1), shift(own, "x", 3)
    own = [own, near, relay(jnp.where(first, near, back), "x"), back]
    blocks = [jnp.concatenate(blocks, axis=0)]
    near, back = shift(blocks[0], "y", 1), shift(blocks[0], "y", 3)
    own[0], own[1], own[3], near, back = lax.optimization_barrier(
        (own[0], own[1], own[3], near, back)
    )
    other = [swap(block, "core") for block in own]
    blocks += [near, relay(jnp.where(first, near, back), "y"), back]

    keep, send, weights = call(
        project_kernel,
        place,
        blocks + own + other,
        [((part, 3 * hidden), F32), ((part, 3 * hidden), BF16), ((3 * hidden, 4 * width), BF16)],
        [
            pltpu.VMEM((2, slots, 4 * width), BF16),
            pltpu.VMEM((slots, 3 * hidden), F32),
            pltpu.SemaphoreType.DMA((4, 3, 2)),
        ],
        [vmem] * 4 + [hbm] * 8,
    )
    hidden_near = call(
        hidden_kernel,
        place,
        [keep, swap(send, "zl")],
        [((part + TILE, 3 * hidden), BF16)],
    )[0]
    hidden_far = swap(hidden_near, "zl")

    def halfway(passed, near, back):
        passed = passed.astype(F32)
        near = (near + jnp.where(first, 0.0, passed)).astype(BF16)
        return near, (back + jnp.where(first, passed, 0.0)).astype(BF16)

    unit = 2 * CAP + TILE
    shares = call(
        share_kernel,
        place,
        [hidden_near, hidden_far, weights],
        [((8 * CAP + TILE, width), F32)] + [((8 * CAP + TILE, width), BF16)] * 3,
        [pltpu.VMEM((slots, 3 * hidden), BF16)],
    )
    passed = relay(shares[2], "y")
    shares[0], hidden_near = lax.optimization_barrier((shares[0], hidden_near))
    keep, *sends = call(
        weight_kernel,
        place,
        [hidden_near, hidden_far] + blocks,
        [((4, 3, half, width), F32)] + [((4, half, width), BF16)] * 3,
        [pltpu.VMEM((slots, 3 * hidden), BF16), pltpu.VMEM((slots, width), BF16)],
    )
    moved = [swap(send, "core") for send in sends]
    near, back = halfway(passed, shares[1], shares[3])
    near, back, *moved = lax.optimization_barrier((near, back, *moved))
    arrived = [shift(near, "y", -1), shift(back, "y", 1)]

    def both_cores(i):
        return jnp.stack([keep[i, m] + moved[m][i].astype(F32) for m in range(3)])

    passed = relay(both_cores(2).astype(BF16), "x")
    passed, *arrived = lax.optimization_barrier((passed, *arrived))
    near, back = halfway(passed, both_cores(1), both_cores(3))
    far_sums = [shift(near, "x", -1), shift(back, "x", 1)]
    totals = call(total_kernel, place, [shares[0]] + arrived, [((unit, width), BF16)] * 4)
    returned = [totals[0]] + [shift(totals[k], "expert", -k) for k in (1, 2, 3)]
    layer_output, token_grad, prob_grad = call(
        owner_kernel,
        place,
        [small, placing] + returned,
        [((rows, width), BF16), ((rows, width), BF16), ((8, rows), F32)],
    )
    weight_total = both_cores(0)
    for block in far_sums:
        weight_total = weight_total + block.astype(F32)
    weight_total = weight_total.astype(BF16).reshape(2, 3 * half // 2, width)
    parts = [turn(weight_total[n]) for n in range(2)]
    *parts, layer_output = lax.optimization_barrier((*parts, layer_output))
    weight_grad = jnp.concatenate([part.astype(F32) for part in parts])
    weight_grad = weight_grad.reshape(stacked_weights.shape)
    return layer_output, token_grad, prob_grad[0:2].T, weight_grad


def solution(mesh):
    split = Mesh(
        mesh.devices.reshape(4, 2, 4, 4, 2), ("x", "core", "expert", "y", "zl")
    )
    rows = P(("x", "core", "expert"), ("y", "zl"))
    pairs = P(("x", "core", "expert"), None)
    weights = P("expert", None, ("y", "zl"), ("x", "core"))
    return jax.shard_map(
        body,
        mesh=split,
        in_specs=(rows, pairs, pairs, weights, rows),
        out_specs=(rows, rows, pairs, weights),
        check_vma=False,
    )
```

```python
import functools

import functools

import jax
import jax.numpy as jnp
from jax import lax
from jax.experimental import pallas as pl
from jax.experimental.pallas import tpu as pltpu
from jax.sharding import Mesh, PartitionSpec as P

F32 = jnp.float32
BF16 = jnp.bfloat16
CAP = 80
TILE = 16
PARAMS = pltpu.CompilerParams(vmem_limit_bytes=48 * 1024 * 1024)


def nn(a, b):
    return lax.dot_general(a, b, (((1,), (0,)), ((), ())), preferred_element_type=F32)


def nt(a, b):
    return lax.dot_general(a, b, (((1,), (1,)), ((), ())), preferred_element_type=F32)


def tn(a, b):
    return lax.dot_general(a, b, (((0,), (0,)), ((), ())), preferred_element_type=F32)


def call(kernel, place, args, outs, scratch=(), spaces=None):
    whole = pl.BlockSpec(memory_space=pltpu.VMEM)
    return list(pl.pallas_call(
        kernel,
        out_shape=[jax.ShapeDtypeStruct(shape, kind) for shape, kind in outs],
        in_specs=[pl.BlockSpec(memory_space=pltpu.SMEM)] + (spaces or [whole] * len(args)),
        out_specs=[whole] * len(outs),
        scratch_shapes=list(scratch),
        compiler_params=PARAMS,
    )(place, *args))


def expert_rows(place, ids, k):
    expert = lax.rem(place[0] + k, 4).astype(F32)
    return ids[0:1, :] == expert, ids[1:2, :] == expert


def slots_kernel(place, small, wide, placing, *outs):
    ids, probs = small.at[0:2], small.at[2:4]
    width = wide.shape[1] // 2
    rows = ids.shape[1]
    before = (
        lax.broadcasted_iota(jnp.int32, (rows, rows), 0)
        < lax.broadcasted_iota(jnp.int32, (rows, rows), 1)
    ).astype(BF16)
    slot = lax.broadcasted_iota(jnp.int32, (CAP, rows), 0)
    scales = []
    for k in range(4):
        one, two = expert_rows(place, ids, k)
        named = jnp.logical_or(one, two)
        marks = jnp.broadcast_to(named, (8, rows)).astype(F32)
        position = nn(marks.astype(BF16), before)[0:1, :].astype(jnp.int32)
        weight = jnp.where(one, probs[0:1, :], probs[1:2, :])
        chosen = jnp.logical_and(
            jnp.broadcast_to(marks[0:1, :] > 0.5, (CAP, rows)),
            slot == jnp.broadcast_to(position, (CAP, rows)),
        )
        placing[k * CAP : (k + 1) * CAP, :] = chosen.astype(F32).astype(BF16)
        scales.append(jnp.sum(jnp.where(chosen, weight, 0.0), axis=1, keepdims=True))
    for k in range(4):
        hot = placing[k * CAP : (k + 1) * CAP, :]
        outs[k][0:CAP, :] = nn(hot, wide[:, 0:width]).astype(BF16)
        outs[k][CAP : 2 * CAP, :] = (scales[k] * nn(hot, wide[:, width:])).astype(BF16)


def fetch(own, other, joined, sems, names, place):
    half, width = own[0].shape[1:]
    copies = []
    for block in range(4):
        spot = lax.rem(place[2] - place[1] + block + 4, 4)
        columns = pl.ds(pl.multiple_of(spot * width, width), width)
        for n, m in enumerate(names):
            for h, source in enumerate((own[block], other[block])):
                copies.append(
                    pltpu.make_async_copy(
                        source.at[m],
                        joined.at[pl.ds((2 * n + h) * half, half), columns],
                        sems.at[block, n, h],
                    )
                )
    for copy in copies:
        copy.start()
    return copies


def take_rows(target, source, second):
    for k in range(4):
        first = (2 * k + second) * CAP
        target[k * CAP : (k + 1) * CAP, :] = source[first : first + CAP, :]


def project_kernel(names, second, place, *refs):
    rows, own, other = refs[0:4], refs[4:8], refs[8:12]
    out, joined, wide, sems = refs[12:16]
    width = rows[0].shape[1]
    copies = fetch(own, other, joined, sems, names, place)
    for j in range(4):
        take_rows(wide.at[:, pl.ds(j * width, width)], rows[j], second)
    for copy in copies:
        copy.wait()
    out[...] = nt(wide[...], joined[...]).astype(BF16)


def pieces(values):
    high = values.astype(BF16)
    rest = values - high.astype(F32)
    middle = rest.astype(BF16)
    low = (rest - middle.astype(F32)).astype(BF16)
    return high, middle, low


def marked_rows(row, first):
    spot = lax.broadcasted_iota(jnp.int32, (TILE, row.shape[1]), 0)
    total = jnp.zeros(spot.shape, F32)
    for n, part in enumerate(pieces(row)):
        total += jnp.where(spot == first + n, part.astype(F32), 0.0)
    return total


def share_kernel(place, pair, pair_far, down, down_far, pair_weights, down_weights, *refs):
    outs, hidden = refs[0:4], refs[4]
    width, step = down.shape[1], outs[0].shape[1]

    def both(near, far, n):
        columns = slice(n * width, (n + 1) * width)
        return near[:, columns].astype(F32) + far[:, columns].astype(F32)

    gate, up, grad = both(pair, pair_far, 0), both(pair, pair_far, 1), both(down, down_far, 0)
    sigmoid = 1.0 / (1.0 + jnp.exp(-gate))
    swish = gate * sigmoid
    act = (swish * up).astype(BF16)
    hidden[:, 2 * width :] = act
    hidden[:, 0:width] = (grad * up * sigmoid * (1.0 + gate * (1.0 - sigmoid))).astype(BF16)
    hidden[:, width : 2 * width] = (grad * swish).astype(BF16)
    share = jnp.sum(act.astype(F32) * grad, axis=1, keepdims=True)
    shape = (CAP, 128)
    same = lax.broadcasted_iota(jnp.int32, shape, 0) == lax.broadcasted_iota(jnp.int32, shape, 1)
    marks = jnp.zeros((TILE, 128), F32)
    for k in range(4):
        row = jnp.sum(
            jnp.where(same, share[k * CAP : (k + 1) * CAP, :], 0.0), axis=0, keepdims=True
        )
        marks += marked_rows(row, 3 * k)
    unit = 2 * CAP
    for j in (2, 1, 3, 0):
        kind = outs[j].dtype
        columns = slice(j * step, (j + 1) * step)
        out = nn(hidden[:, 2 * width :], down_weights[:, columns])
        back = nn(hidden[:, 0 : 2 * width], pair_weights[:, columns])
        for k in range(4):
            start, rows = k * unit, slice(k * CAP, (k + 1) * CAP)
            outs[j][start : start + CAP, :] = out[rows, :].astype(kind)
            outs[j][start + CAP : start + 2 * CAP, :] = back[rows, :].astype(kind)
        outs[j][4 * unit :, :] = jnp.zeros((TILE, step), kind)
        outs[j][4 * unit :, 0:128] = marks.astype(kind)


def total_kernel(place, own, one, three, *outs):
    unit = 2 * CAP

    def total(span, columns):
        value = own[span, columns] + one[span, columns].astype(F32)
        return value + three[span, columns].astype(F32)

    marks = total(slice(4 * unit, 4 * unit + TILE), slice(0, 128))
    width = own.shape[1]
    for k in range(4):
        outs[k][0:unit, :] = total(slice(k * unit, (k + 1) * unit), slice(0, width)).astype(BF16)
        row = jnp.sum(marks[3 * k : 3 * k + 3, :], axis=0, keepdims=True)
        outs[k][unit:, :] = jnp.zeros((TILE, width), BF16)
        outs[k][unit:, 0:128] = marked_rows(row, 0).astype(BF16)


def weight_kernel(place, joined, *refs):
    rows, keep, sends, chosen = refs[0:4], refs[4], refs[5:8], refs[8]
    half = keep.shape[2]
    for j in range(4):
        block = lax.rem(place[1] - place[2] + j + 4, 4)
        for m, second in ((2, 1), (0, 0), (1, 0)):
            if m != 1:
                take_rows(chosen, rows[j], second)
            total = tn(joined[:, 2 * m * half : 2 * (m + 1) * half], chosen[...])
            keep[block, m] = total[0:half, :]
            sends[m][block] = total[half:, :].astype(BF16)


def column(row):
    rows = row.shape[1]
    shape = (rows, rows)
    same = lax.broadcasted_iota(jnp.int32, shape, 0) == lax.broadcasted_iota(jnp.int32, shape, 1)
    return jnp.sum(jnp.where(same, row, 0.0), axis=1, keepdims=True)


def owner_kernel(place, small, placing, *refs):
    ids, probs = small.at[0:2], small.at[2:4]
    blocks, layer, token, prob = refs[0:4], *refs[4:7]
    total = jnp.zeros(layer.shape, F32)
    grads = jnp.zeros(token.shape, F32)
    shares = [jnp.zeros((1, ids.shape[1]), F32) for _ in range(2)]
    for k in range(4):
        one, two = expert_rows(place, ids, k)
        hot = placing[k * CAP : (k + 1) * CAP, :]
        weight = jnp.where(one, probs[0:1, :], 0.0) + jnp.where(two, probs[1:2, :], 0.0)
        total += column(weight) * tn(hot, blocks[k][0:CAP, :])
        grads += tn(hot, blocks[k][CAP : 2 * CAP, :])
        found = nn(blocks[k][2 * CAP :, 0:128][:, 0:CAP], hot)
        share = jnp.sum(found, axis=0, keepdims=True)
        shares[0] += jnp.where(one, share, 0.0)
        shares[1] += jnp.where(two, share, 0.0)
    layer[...] = total.astype(BF16)
    token[...] = grads.astype(BF16)
    prob[...] = jnp.zeros(prob.shape, F32)
    for n in range(2):
        prob[n : n + 1, :] = shares[n] / probs[n : n + 1, :]


def shift(value, axis, step):
    return lax.ppermute(value, axis, [(i, (i + step) % 4) for i in range(4)])


def relay(value, axis):
    steps = [(c, i, (i + (3 if c else 1)) % 4) for c in range(2) for i in range(4)]
    if axis == "x":
        return lax.ppermute(value, ("x", "core"), [(2 * i + c, 2 * j + c) for c, i, j in steps])
    return lax.ppermute(value, ("core", axis), [(4 * c + i, 4 * c + j) for c, i, j in steps])


def swap(value, axis):
    return lax.ppermute(value, axis, [(0, 1), (1, 0)])


def turn(value):
    return lax.ppermute(value, ("core", "zl"), [(2 * c + z, 2 * z + c) for c in range(2) for z in range(2)])


def body(tokens, expert_ids, gate_probs, stacked_weights, out_grad):
    rows, width = tokens.shape
    half = stacked_weights.shape[2]
    hidden = 2 * half
    slots = 4 * CAP
    place = jnp.stack(
        [lax.axis_index(name) for name in ("expert", "x", "y", "zl", "core")]
    ).astype(jnp.int32)
    small = jnp.concatenate([expert_ids.T.astype(F32), gate_probs.T])
    wide = jnp.concatenate([tokens, out_grad], axis=1)
    vmem = pl.BlockSpec(memory_space=pltpu.VMEM)
    hbm = pl.BlockSpec(memory_space=pl.ANY)

    placing, *blocks = call(
        slots_kernel,
        place,
        [small, wide],
        [((slots, rows), BF16)] + [((2 * CAP, width), BF16)] * 4,
    )

    blocks = [blocks[0]] + [shift(blocks[k], "expert", k) for k in (1, 2, 3)]
    own, blocks[0] = lax.optimization_barrier((stacked_weights[0], blocks[0]))
    turned = lax.ppermute(own, ("core", "zl"), [(1, 2), (2, 1)])
    own = jnp.where(place[4] == place[3], own, turned)
    first = lax.axis_index("core") == 0
    near, back = shift(own, "x", 1), shift(own, "x", 3)
    own = [own, near, relay(jnp.where(first, near, back), "x"), back]
    blocks = [jnp.concatenate(blocks, axis=0)]
    near, back = shift(blocks[0], "y", 1), shift(blocks[0], "y", 3)
    own[0], own[1], own[3], near, back = lax.optimization_barrier(
        (own[0], own[1], own[3], near, back)
    )
    other = [swap(block, "core") for block in own]
    blocks += [near, relay(jnp.where(first, near, back), "y"), back]

    def project(names, second):
        tall = len(names) * hidden
        return call(
            functools.partial(project_kernel, names, second),
            place,
            blocks + own + other,
            [((slots, tall), BF16), ((tall, 4 * width), BF16)],
            [pltpu.VMEM((slots, 4 * width), BF16), pltpu.SemaphoreType.DMA((4, 2, 2))],
            [vmem] * 4 + [hbm] * 8,
        )

    pair, pair_weights = project((0, 1), 0)
    pair_far = swap(pair, "zl")
    down, down_weights = project((2,), 1)
    down_far = swap(down, "zl")

    def halfway(passed, near, back):
        passed = passed.astype(F32)
        near = (near + jnp.where(first, 0.0, passed)).astype(BF16)
        return near, (back + jnp.where(first, passed, 0.0)).astype(BF16)

    unit = 2 * CAP + TILE
    shares = call(
        share_kernel,
        place,
        [pair, pair_far, down, down_far, pair_weights, down_weights],
        [((8 * CAP + TILE, width), F32)]
        + [((8 * CAP + TILE, width), BF16)] * 3
        + [((slots, 3 * hidden), BF16)],
    )
    passed = relay(shares[2], "y")
    keep, *sends = call(
        weight_kernel,
        place,
        [shares[4]] + blocks,
        [((4, 3, half, width), F32)] + [((4, half, width), BF16)] * 3,
        [pltpu.VMEM((slots, width), BF16)],
    )
    moved = [swap(send, "core") for send in sends]
    near, back = halfway(passed, shares[1], shares[3])
    near, back, *moved = lax.optimization_barrier((near, back, *moved))
    arrived = [shift(near, "y", -1), shift(back, "y", 1)]

    def both_cores(i):
        return jnp.stack([keep[i, m] + moved[m][i].astype(F32) for m in range(3)])

    passed = relay(both_cores(2).astype(BF16), "x")
    passed, *arrived = lax.optimization_barrier((passed, *arrived))
    near, back = halfway(passed, both_cores(1), both_cores(3))
    far_sums = [shift(near, "x", -1), shift(back, "x", 1)]
    totals = call(total_kernel, place, [shares[0]] + arrived, [((unit, width), BF16)] * 4)
    returned = [totals[0]] + [shift(totals[k], "expert", -k) for k in (1, 2, 3)]
    layer_output, token_grad, prob_grad = call(
        owner_kernel,
        place,
        [small, placing] + returned,
        [((rows, width), BF16), ((rows, width), BF16), ((8, rows), F32)],
    )
    weight_total = both_cores(0)
    for block in far_sums:
        weight_total = weight_total + block.astype(F32)
    weight_total = weight_total.astype(BF16).reshape(2, 3 * half // 2, width)
    parts = [turn(weight_total[n]) for n in range(2)]
    *parts, layer_output = lax.optimization_barrier((*parts, layer_output))
    weight_grad = jnp.concatenate([part.astype(F32) for part in parts])
    weight_grad = weight_grad.reshape(stacked_weights.shape)
    return layer_output, token_grad, prob_grad[0:2].T, weight_grad


def solution(mesh):
    split = Mesh(
        mesh.devices.reshape(4, 2, 4, 4, 2), ("x", "core", "expert", "y", "zl")
    )
    rows = P(("x", "core", "expert"), ("y", "zl"))
    pairs = P(("x", "core", "expert"), None)
    weights = P("expert", None, ("y", "zl"), ("x", "core"))
    return jax.shard_map(
        body,
        mesh=split,
        in_specs=(rows, pairs, pairs, weights, rows),
        out_specs=(rows, rows, pairs, weights),
        check_vma=False,
    )
```

```python
import functools

import functools

import jax
import jax.numpy as jnp
from jax import lax
from jax.experimental import pallas as pl
from jax.experimental.pallas import tpu as pltpu
from jax.sharding import Mesh, PartitionSpec as P

F32 = jnp.float32
BF16 = jnp.bfloat16
CAP = 80
TILE = 16
PARAMS = pltpu.CompilerParams(vmem_limit_bytes=48 * 1024 * 1024)


def nn(a, b):
    return lax.dot_general(a, b, (((1,), (0,)), ((), ())), preferred_element_type=F32)


def nt(a, b):
    return lax.dot_general(a, b, (((1,), (1,)), ((), ())), preferred_element_type=F32)


def tn(a, b):
    return lax.dot_general(a, b, (((0,), (0,)), ((), ())), preferred_element_type=F32)


def call(kernel, place, args, outs, scratch=(), spaces=None):
    whole = pl.BlockSpec(memory_space=pltpu.VMEM)
    return list(pl.pallas_call(
        kernel,
        out_shape=[jax.ShapeDtypeStruct(shape, kind) for shape, kind in outs],
        in_specs=[pl.BlockSpec(memory_space=pltpu.SMEM)] + (spaces or [whole] * len(args)),
        out_specs=[whole] * len(outs),
        scratch_shapes=list(scratch),
        compiler_params=PARAMS,
    )(place, *args))


def expert_rows(place, ids, k):
    expert = lax.rem(place[0] + k, 4).astype(F32)
    return ids[0:1, :] == expert, ids[1:2, :] == expert


def slots_kernel(place, small, wide, placing, *outs):
    ids, probs = small.at[0:2], small.at[2:4]
    width = wide.shape[1] // 2
    rows = ids.shape[1]
    before = (
        lax.broadcasted_iota(jnp.int32, (rows, rows), 0)
        < lax.broadcasted_iota(jnp.int32, (rows, rows), 1)
    ).astype(BF16)
    slot = lax.broadcasted_iota(jnp.int32, (CAP, rows), 0)
    scales = []
    for k in range(4):
        one, two = expert_rows(place, ids, k)
        named = jnp.logical_or(one, two)
        marks = jnp.broadcast_to(named, (8, rows)).astype(F32)
        position = nn(marks.astype(BF16), before)[0:1, :].astype(jnp.int32)
        weight = jnp.where(one, probs[0:1, :], probs[1:2, :])
        chosen = jnp.logical_and(
            jnp.broadcast_to(marks[0:1, :] > 0.5, (CAP, rows)),
            slot == jnp.broadcast_to(position, (CAP, rows)),
        )
        placing[k * CAP : (k + 1) * CAP, :] = chosen.astype(F32).astype(BF16)
        scales.append(jnp.sum(jnp.where(chosen, weight, 0.0), axis=1, keepdims=True))
    for k in range(4):
        hot = placing[k * CAP : (k + 1) * CAP, :]
        outs[k][0:CAP, :] = nn(hot, wide[:, 0:width]).astype(BF16)
        outs[k][CAP : 2 * CAP, :] = (scales[k] * nn(hot, wide[:, width:])).astype(BF16)


def fetch(own, other, joined, sems, names, place):
    half, width = own[0].shape[1:]
    copies = []
    for block in range(4):
        spot = lax.rem(place[2] - place[1] + block + 4, 4)
        columns = pl.ds(pl.multiple_of(spot * width, width), width)
        for n, m in enumerate(names):
            for h, source in enumerate((own[block], other[block])):
                copies.append(
                    pltpu.make_async_copy(
                        source.at[m],
                        joined.at[pl.ds((2 * n + h) * half, half), columns],
                        sems.at[block, n, h],
                    )
                )
    for copy in copies:
        copy.start()
    return copies


def take_rows(target, source, second):
    for k in range(4):
        first = (2 * k + second) * CAP
        target[k * CAP : (k + 1) * CAP, :] = source[first : first + CAP, :]


def project_kernel(names, second, place, *refs):
    rows, own, other = refs[0:4], refs[4:8], refs[8:12]
    out, joined, wide, sems = refs[12:16]
    width = rows[0].shape[1]
    copies = fetch(own, other, joined, sems, names, place)
    for j in range(4):
        take_rows(wide.at[:, pl.ds(j * width, width)], rows[j], second)
    for copy in copies:
        copy.wait()
    out[...] = nt(wide[...], joined[...]).astype(BF16)


def pieces(values):
    high = values.astype(BF16)
    rest = values - high.astype(F32)
    middle = rest.astype(BF16)
    low = (rest - middle.astype(F32)).astype(BF16)
    return high, middle, low


def marked_rows(row, first):
    spot = lax.broadcasted_iota(jnp.int32, (TILE, row.shape[1]), 0)
    total = jnp.zeros(spot.shape, F32)
    for n, part in enumerate(pieces(row)):
        total += jnp.where(spot == first + n, part.astype(F32), 0.0)
    return total


def share_kernel(place, pair, pair_far, down, down_far, pair_weights, down_weights, *refs):
    outs, hidden = refs[0:4], refs[4]
    width, step = down.shape[1], outs[0].shape[1]

    def both(near, far, n):
        columns = slice(n * width, (n + 1) * width)
        return near[:, columns].astype(F32) + far[:, columns].astype(F32)

    gate, up, grad = both(pair, pair_far, 0), both(pair, pair_far, 1), both(down, down_far, 0)
    sigmoid = 1.0 / (1.0 + jnp.exp(-gate))
    swish = gate * sigmoid
    act = (swish * up).astype(BF16)
    hidden[:, 2 * width :] = act
    hidden[:, 0:width] = (grad * up * sigmoid * (1.0 + gate * (1.0 - sigmoid))).astype(BF16)
    hidden[:, width : 2 * width] = (grad * swish).astype(BF16)
    share = jnp.sum(act.astype(F32) * grad, axis=1, keepdims=True)
    shape = (CAP, 128)
    same = lax.broadcasted_iota(jnp.int32, shape, 0) == lax.broadcasted_iota(jnp.int32, shape, 1)
    marks = jnp.zeros((TILE, 128), F32)
    for k in range(4):
        row = jnp.sum(
            jnp.where(same, share[k * CAP : (k + 1) * CAP, :], 0.0), axis=0, keepdims=True
        )
        marks += marked_rows(row, 3 * k)
    unit = 2 * CAP
    for j in (2, 1, 3, 0):
        kind = outs[j].dtype
        columns = slice(j * step, (j + 1) * step)
        out = nn(hidden[:, 2 * width :], down_weights[:, columns])
        back = nn(hidden[:, 0 : 2 * width], pair_weights[:, columns])
        for k in range(4):
            start, rows = k * unit, slice(k * CAP, (k + 1) * CAP)
            outs[j][start : start + CAP, :] = out[rows, :].astype(kind)
            outs[j][start + CAP : start + 2 * CAP, :] = back[rows, :].astype(kind)
        outs[j][4 * unit :, :] = jnp.zeros((TILE, step), kind)
        outs[j][4 * unit :, 0:128] = marks.astype(kind)


def total_kernel(place, own, one, three, *outs):
    unit = 2 * CAP

    def total(span, columns):
        value = own[span, columns] + one[span, columns].astype(F32)
        return value + three[span, columns].astype(F32)

    marks = total(slice(4 * unit, 4 * unit + TILE), slice(0, 128))
    width = own.shape[1]
    for k in range(4):
        outs[k][0:unit, :] = total(slice(k * unit, (k + 1) * unit), slice(0, width)).astype(BF16)
        row = jnp.sum(marks[3 * k : 3 * k + 3, :], axis=0, keepdims=True)
        outs[k][unit:, :] = jnp.zeros((TILE, width), BF16)
        outs[k][unit:, 0:128] = marked_rows(row, 0).astype(BF16)


def weight_kernel(place, joined, *refs):
    rows, keeps, sends, chosen = refs[0:4], refs[4:8], refs[8:12], refs[12]
    half = keeps[0].shape[1]
    for j in range(4):
        spot = lax.rem(place[1] - place[2] + j + 4, 4)
        for second in range(2):
            take_rows(chosen.at[second, spot], rows[j], second)
    for i in (2, 1, 3, 0):
        for m in range(3):
            columns = slice(2 * m * half, 2 * (m + 1) * half)
            total = tn(joined[:, columns], chosen[1 if m == 2 else 0, i])
            keeps[i][m] = total[0:half, :]
            sends[i][m] = total[half:, :].astype(BF16)


def column(row):
    rows = row.shape[1]
    shape = (rows, rows)
    same = lax.broadcasted_iota(jnp.int32, shape, 0) == lax.broadcasted_iota(jnp.int32, shape, 1)
    return jnp.sum(jnp.where(same, row, 0.0), axis=1, keepdims=True)


def owner_kernel(place, small, placing, *refs):
    ids, probs = small.at[0:2], small.at[2:4]
    blocks, layer, token, prob = refs[0:4], *refs[4:7]
    total = jnp.zeros(layer.shape, F32)
    grads = jnp.zeros(token.shape, F32)
    shares = [jnp.zeros((1, ids.shape[1]), F32) for _ in range(2)]
    for k in range(4):
        one, two = expert_rows(place, ids, k)
        hot = placing[k * CAP : (k + 1) * CAP, :]
        weight = jnp.where(one, probs[0:1, :], 0.0) + jnp.where(two, probs[1:2, :], 0.0)
        total += column(weight) * tn(hot, blocks[k][0:CAP, :])
        grads += tn(hot, blocks[k][CAP : 2 * CAP, :])
        found = nn(blocks[k][2 * CAP :, 0:128][:, 0:CAP], hot)
        share = jnp.sum(found, axis=0, keepdims=True)
        shares[0] += jnp.where(one, share, 0.0)
        shares[1] += jnp.where(two, share, 0.0)
    layer[...] = total.astype(BF16)
    token[...] = grads.astype(BF16)
    prob[...] = jnp.zeros(prob.shape, F32)
    for n in range(2):
        prob[n : n + 1, :] = shares[n] / probs[n : n + 1, :]


def shift(value, axis, step):
    return lax.ppermute(value, axis, [(i, (i + step) % 4) for i in range(4)])


def relay(value, axis):
    steps = [(c, i, (i + (3 if c else 1)) % 4) for c in range(2) for i in range(4)]
    if axis == "x":
        return lax.ppermute(value, ("x", "core"), [(2 * i + c, 2 * j + c) for c, i, j in steps])
    return lax.ppermute(value, ("core", axis), [(4 * c + i, 4 * c + j) for c, i, j in steps])


def swap(value, axis):
    return lax.ppermute(value, axis, [(0, 1), (1, 0)])


def turn(value):
    return lax.ppermute(value, ("core", "zl"), [(2 * c + z, 2 * z + c) for c in range(2) for z in range(2)])


def body(tokens, expert_ids, gate_probs, stacked_weights, out_grad):
    rows, width = tokens.shape
    half = stacked_weights.shape[2]
    hidden = 2 * half
    slots = 4 * CAP
    place = jnp.stack(
        [lax.axis_index(name) for name in ("expert", "x", "y", "zl", "core")]
    ).astype(jnp.int32)
    small = jnp.concatenate([expert_ids.T.astype(F32), gate_probs.T])
    wide = jnp.concatenate([tokens, out_grad], axis=1)
    vmem = pl.BlockSpec(memory_space=pltpu.VMEM)
    hbm = pl.BlockSpec(memory_space=pl.ANY)

    placing, *blocks = call(
        slots_kernel,
        place,
        [small, wide],
        [((slots, rows), BF16)] + [((2 * CAP, width), BF16)] * 4,
    )

    blocks = [blocks[0]] + [shift(blocks[k], "expert", k) for k in (1, 2, 3)]
    own, blocks[0] = lax.optimization_barrier((stacked_weights[0], blocks[0]))
    turned = lax.ppermute(own, ("core", "zl"), [(1, 2), (2, 1)])
    own = jnp.where(place[4] == place[3], own, turned)
    first = lax.axis_index("core") == 0
    near, back = shift(own, "x", 1), shift(own, "x", 3)
    own = [own, near, relay(jnp.where(first, near, back), "x"), back]
    blocks = [jnp.concatenate(blocks, axis=0)]
    near, back = shift(blocks[0], "y", 1), shift(blocks[0], "y", 3)
    own[0], own[1], own[3], near, back = lax.optimization_barrier(
        (own[0], own[1], own[3], near, back)
    )
    other = [swap(block, "core") for block in own]
    blocks += [near, relay(jnp.where(first, near, back), "y"), back]

    def project(names, second):
        tall = len(names) * hidden
        return call(
            functools.partial(project_kernel, names, second),
            place,
            blocks + own + other,
            [((slots, tall), BF16), ((tall, 4 * width), BF16)],
            [pltpu.VMEM((slots, 4 * width), BF16), pltpu.SemaphoreType.DMA((4, 2, 2))],
            [vmem] * 4 + [hbm] * 8,
        )

    pair, pair_weights = project((0, 1), 0)
    pair_far = swap(pair, "zl")
    down, down_weights = project((2,), 1)
    down_far = swap(down, "zl")

    def halfway(passed, near, back):
        passed = passed.astype(F32)
        near = (near + jnp.where(first, 0.0, passed)).astype(BF16)
        return near, (back + jnp.where(first, passed, 0.0)).astype(BF16)

    unit = 2 * CAP + TILE
    shares = call(
        share_kernel,
        place,
        [pair, pair_far, down, down_far, pair_weights, down_weights],
        [((8 * CAP + TILE, width), F32)]
        + [((8 * CAP + TILE, width), BF16)] * 3
        + [((slots, 3 * hidden), BF16)],
    )
    passed = relay(shares[2], "y")
    terms = call(
        weight_kernel,
        place,
        [shares[4]] + blocks,
        [((3, half, width), kind) for kind in (F32, BF16) for _ in range(4)],
        [pltpu.VMEM((2, 4, slots, width), BF16)],
    )
    keeps, sends = terms[0:4], terms[4:8]
    moved = [swap(send, "core") for send in sends]
    near, back = halfway(passed, shares[1], shares[3])
    near, back, *moved = lax.optimization_barrier((near, back, *moved))
    arrived = [shift(near, "y", -1), shift(back, "y", 1)]

    def both_cores(i):
        return keeps[i] + moved[i].astype(F32)

    passed = relay(both_cores(2).astype(BF16), "x")
    near, back = halfway(passed, both_cores(1), both_cores(3))
    far_sums = [shift(near, "x", -1), shift(back, "x", 1)]
    totals = call(total_kernel, place, [shares[0]] + arrived, [((unit, width), BF16)] * 4)
    returned = [totals[0]] + [shift(totals[k], "expert", -k) for k in (1, 2, 3)]
    layer_output, token_grad, prob_grad = call(
        owner_kernel,
        place,
        [small, placing] + returned,
        [((rows, width), BF16), ((rows, width), BF16), ((8, rows), F32)],
    )
    weight_total = both_cores(0)
    for block in far_sums:
        weight_total = weight_total + block.astype(F32)
    weight_total = weight_total.astype(BF16).reshape(2, 3 * half // 2, width)
    parts = [turn(weight_total[n]) for n in range(2)]
    *parts, layer_output = lax.optimization_barrier((*parts, layer_output))
    weight_grad = jnp.concatenate([part.astype(F32) for part in parts])
    weight_grad = weight_grad.reshape(stacked_weights.shape)
    return layer_output, token_grad, prob_grad[0:2].T, weight_grad


def solution(mesh):
    split = Mesh(
        mesh.devices.reshape(4, 2, 4, 4, 2), ("x", "core", "expert", "y", "zl")
    )
    rows = P(("x", "core", "expert"), ("y", "zl"))
    pairs = P(("x", "core", "expert"), None)
    weights = P("expert", None, ("y", "zl"), ("x", "core"))
    return jax.shard_map(
        body,
        mesh=split,
        in_specs=(rows, pairs, pairs, weights, rows),
        out_specs=(rows, rows, pairs, weights),
        check_vma=False,
    )
```

```python
import functools

import functools

import jax
import jax.numpy as jnp
from jax import lax
from jax.experimental import pallas as pl
from jax.experimental.pallas import tpu as pltpu
from jax.sharding import Mesh, PartitionSpec as P

F32 = jnp.float32
BF16 = jnp.bfloat16
CAP = 80
TILE = 16
PARAMS = pltpu.CompilerParams(vmem_limit_bytes=48 * 1024 * 1024)


def nn(a, b):
    return lax.dot_general(a, b, (((1,), (0,)), ((), ())), preferred_element_type=F32)


def nt(a, b):
    return lax.dot_general(a, b, (((1,), (1,)), ((), ())), preferred_element_type=F32)


def tn(a, b):
    return lax.dot_general(a, b, (((0,), (0,)), ((), ())), preferred_element_type=F32)


def call(kernel, place, args, outs, scratch=(), spaces=None):
    whole = pl.BlockSpec(memory_space=pltpu.VMEM)
    return list(pl.pallas_call(
        kernel,
        out_shape=[jax.ShapeDtypeStruct(shape, kind) for shape, kind in outs],
        in_specs=[pl.BlockSpec(memory_space=pltpu.SMEM)] + (spaces or [whole] * len(args)),
        out_specs=[whole] * len(outs),
        scratch_shapes=list(scratch),
        compiler_params=PARAMS,
    )(place, *args))


def expert_rows(place, ids, k):
    expert = lax.rem(place[0] + k, 4).astype(F32)
    return ids[0:1, :] == expert, ids[1:2, :] == expert


def slots_kernel(place, small, wide, placing, *outs):
    ids, probs = small.at[0:2], small.at[2:4]
    width = wide.shape[1] // 2
    rows = ids.shape[1]
    before = (
        lax.broadcasted_iota(jnp.int32, (rows, rows), 0)
        < lax.broadcasted_iota(jnp.int32, (rows, rows), 1)
    ).astype(BF16)
    slot = lax.broadcasted_iota(jnp.int32, (CAP, rows), 0)
    scales = []
    for k in range(4):
        one, two = expert_rows(place, ids, k)
        named = jnp.logical_or(one, two)
        marks = jnp.broadcast_to(named, (8, rows)).astype(F32)
        position = nn(marks.astype(BF16), before)[0:1, :].astype(jnp.int32)
        weight = jnp.where(one, probs[0:1, :], probs[1:2, :])
        chosen = jnp.logical_and(
            jnp.broadcast_to(marks[0:1, :] > 0.5, (CAP, rows)),
            slot == jnp.broadcast_to(position, (CAP, rows)),
        )
        placing[k * CAP : (k + 1) * CAP, :] = chosen.astype(F32).astype(BF16)
        scales.append(jnp.sum(jnp.where(chosen, weight, 0.0), axis=1, keepdims=True))
    for k in range(4):
        hot = placing[k * CAP : (k + 1) * CAP, :]
        outs[k][0:CAP, :] = nn(hot, wide[:, 0:width]).astype(BF16)
        outs[k][CAP : 2 * CAP, :] = (scales[k] * nn(hot, wide[:, width:])).astype(BF16)


def fetch(own, other, joined, sems, names, place):
    half, width = own[0].shape[1:]
    copies = []
    for block in range(4):
        spot = lax.rem(place[2] - place[1] + block + 4, 4)
        columns = pl.ds(pl.multiple_of(spot * width, width), width)
        for n, m in enumerate(names):
            for h, source in enumerate((own[block], other[block])):
                copies.append(
                    pltpu.make_async_copy(
                        source.at[m],
                        joined.at[pl.ds((2 * n + h) * half, half), columns],
                        sems.at[block, n, h],
                    )
                )
    for copy in copies:
        copy.start()
    return copies


def take_rows(target, source, second):
    for k in range(4):
        first = (2 * k + second) * CAP
        target[k * CAP : (k + 1) * CAP, :] = source[first : first + CAP, :]


def early_kernel(place, *refs):
    rows, own, other = refs[0:3], refs[3:7], refs[7:11]
    pair, down, pair_weights, down_weights, wide, pair_sems, down_sems = refs[11:18]
    width = rows[0].shape[1]
    copies = fetch(own, other, pair_weights, pair_sems, (0, 1), place)
    more = fetch(own, other, down_weights, down_sems, (2,), place)
    for second in range(2):
        for n in range(3):
            take_rows(wide.at[second, :, pl.ds(n * width, width)], rows[n], second)
    for second, out, weights in ((0, pair, pair_weights), (1, down, down_weights)):
        for copy in more if second else copies:
            copy.wait()
        low = nt(wide[second, :, 0 : 2 * width], weights[:, 0 : 2 * width])
        out[...] = low + nt(wide[second, :, 2 * width :], weights[:, 3 * width :])


def late_kernel(second, place, early, rows, weights, out, chosen):
    width = rows.shape[1]
    take_rows(chosen, rows, second)
    total = early[...] + nt(chosen[...], weights[:, 2 * width : 3 * width])
    out[...] = total.astype(BF16)


def pieces(values):
    high = values.astype(BF16)
    rest = values - high.astype(F32)
    middle = rest.astype(BF16)
    low = (rest - middle.astype(F32)).astype(BF16)
    return high, middle, low


def marked_rows(row, first):
    spot = lax.broadcasted_iota(jnp.int32, (TILE, row.shape[1]), 0)
    total = jnp.zeros(spot.shape, F32)
    for n, part in enumerate(pieces(row)):
        total += jnp.where(spot == first + n, part.astype(F32), 0.0)
    return total


def store_shares(outs, order, hidden, marks, pair_weights, down_weights):
    width, step, unit = hidden.shape[1] // 3, outs[0].shape[1], 2 * CAP
    for out, j in zip(outs, order):
        columns = slice(j * step, (j + 1) * step)
        first = nn(hidden[:, 2 * width :], down_weights[:, columns]).astype(out.dtype)
        second = nn(hidden[:, 0 : 2 * width], pair_weights[:, columns]).astype(out.dtype)
        for k in range(4):
            start, rows = k * unit, slice(k * CAP, (k + 1) * CAP)
            out[start : start + CAP, :] = first[rows, :]
            out[start + CAP : start + 2 * CAP, :] = second[rows, :]
        out[4 * unit :, :] = jnp.zeros((TILE, step), out.dtype)
        out[4 * unit :, 0:128] = marks.astype(out.dtype)


def rest_kernel(place, hidden, marks, pair_weights, down_weights, *outs):
    store_shares(outs, (1, 3, 0), hidden, marks[...], pair_weights, down_weights)


def share_kernel(
    place, pair, pair_far, down, down_far, pair_weights, down_weights, across, hidden, mark_rows
):
    width = down.shape[1]

    def both(near, far, n):
        columns = slice(n * width, (n + 1) * width)
        return near[:, columns].astype(F32) + far[:, columns].astype(F32)

    gate, up, grad = both(pair, pair_far, 0), both(pair, pair_far, 1), both(down, down_far, 0)
    sigmoid = 1.0 / (1.0 + jnp.exp(-gate))
    swish = gate * sigmoid
    act = (swish * up).astype(BF16)
    hidden[:, 2 * width :] = act
    hidden[:, 0:width] = (grad * up * sigmoid * (1.0 + gate * (1.0 - sigmoid))).astype(BF16)
    hidden[:, width : 2 * width] = (grad * swish).astype(BF16)
    share = jnp.sum(act.astype(F32) * grad, axis=1, keepdims=True)
    shape = (CAP, 128)
    same = lax.broadcasted_iota(jnp.int32, shape, 0) == lax.broadcasted_iota(jnp.int32, shape, 1)
    marks = jnp.zeros((TILE, 128), F32)
    for k in range(4):
        row = jnp.sum(
            jnp.where(same, share[k * CAP : (k + 1) * CAP, :], 0.0), axis=0, keepdims=True
        )
        marks += marked_rows(row, 3 * k)
    mark_rows[...] = marks
    store_shares((across,), (2,), hidden, marks, pair_weights, down_weights)


def total_kernel(place, own, one, three, *outs):
    unit = 2 * CAP

    def total(span, columns):
        value = own[span, columns] + one[span, columns].astype(F32)
        return value + three[span, columns].astype(F32)

    marks = total(slice(4 * unit, 4 * unit + TILE), slice(0, 128))
    width = own.shape[1]
    for k in range(4):
        outs[k][0:unit, :] = total(slice(k * unit, (k + 1) * unit), slice(0, width)).astype(BF16)
        row = jnp.sum(marks[3 * k : 3 * k + 3, :], axis=0, keepdims=True)
        outs[k][unit:, :] = jnp.zeros((TILE, width), BF16)
        outs[k][unit:, 0:128] = marked_rows(row, 0).astype(BF16)


def weight_kernel(place, joined, *refs):
    rows, keeps, sends, chosen = refs[0:4], refs[4:8], refs[8:12], refs[12]
    half = keeps[0].shape[1]
    for j in range(4):
        spot = lax.rem(place[1] - place[2] + j + 4, 4)
        for second in range(2):
            take_rows(chosen.at[second, spot], rows[j], second)
    for i in (2, 1, 3, 0):
        for m in range(3):
            columns = slice(2 * m * half, 2 * (m + 1) * half)
            total = tn(joined[:, columns], chosen[1 if m == 2 else 0, i])
            keeps[i][m] = total[0:half, :]
            sends[i][m] = total[half:, :].astype(BF16)


def column(row):
    rows = row.shape[1]
    shape = (rows, rows)
    same = lax.broadcasted_iota(jnp.int32, shape, 0) == lax.broadcasted_iota(jnp.int32, shape, 1)
    return jnp.sum(jnp.where(same, row, 0.0), axis=1, keepdims=True)


def owner_kernel(place, small, placing, *refs):
    ids, probs = small.at[0:2], small.at[2:4]
    blocks, layer, token, prob = refs[0:4], *refs[4:7]
    total = jnp.zeros(layer.shape, F32)
    grads = jnp.zeros(token.shape, F32)
    shares = [jnp.zeros((1, ids.shape[1]), F32) for _ in range(2)]
    for k in range(4):
        one, two = expert_rows(place, ids, k)
        hot = placing[k * CAP : (k + 1) * CAP, :]
        weight = jnp.where(one, probs[0:1, :], 0.0) + jnp.where(two, probs[1:2, :], 0.0)
        total += column(weight) * tn(hot, blocks[k][0:CAP, :])
        grads += tn(hot, blocks[k][CAP : 2 * CAP, :])
        found = nn(blocks[k][2 * CAP :, 0:128][:, 0:CAP], hot)
        share = jnp.sum(found, axis=0, keepdims=True)
        shares[0] += jnp.where(one, share, 0.0)
        shares[1] += jnp.where(two, share, 0.0)
    layer[...] = total.astype(BF16)
    token[...] = grads.astype(BF16)
    prob[...] = jnp.zeros(prob.shape, F32)
    for n in range(2):
        prob[n : n + 1, :] = shares[n] / probs[n : n + 1, :]


def shift(value, axis, step):
    return lax.ppermute(value, axis, [(i, (i + step) % 4) for i in range(4)])


def relay(value, axis):
    steps = [(c, i, (i + (3 if c else 1)) % 4) for c in range(2) for i in range(4)]
    if axis == "x":
        return lax.ppermute(value, ("x", "core"), [(2 * i + c, 2 * j + c) for c, i, j in steps])
    return lax.ppermute(value, ("core", axis), [(4 * c + i, 4 * c + j) for c, i, j in steps])


def swap(value, axis):
    return lax.ppermute(value, axis, [(0, 1), (1, 0)])


def turn(value):
    return lax.ppermute(value, ("core", "zl"), [(2 * c + z, 2 * z + c) for c in range(2) for z in range(2)])


def body(tokens, expert_ids, gate_probs, stacked_weights, out_grad):
    rows, width = tokens.shape
    half = stacked_weights.shape[2]
    hidden = 2 * half
    slots = 4 * CAP
    place = jnp.stack(
        [lax.axis_index(name) for name in ("expert", "x", "y", "zl", "core")]
    ).astype(jnp.int32)
    small = jnp.concatenate([expert_ids.T.astype(F32), gate_probs.T])
    wide = jnp.concatenate([tokens, out_grad], axis=1)
    vmem = pl.BlockSpec(memory_space=pltpu.VMEM)
    hbm = pl.BlockSpec(memory_space=pl.ANY)

    placing, *blocks = call(
        slots_kernel,
        place,
        [small, wide],
        [((slots, rows), BF16)] + [((2 * CAP, width), BF16)] * 4,
    )

    blocks = [blocks[0]] + [shift(blocks[k], "expert", k) for k in (1, 2, 3)]
    own, blocks[0] = lax.optimization_barrier((stacked_weights[0], blocks[0]))
    turned = lax.ppermute(own, ("core", "zl"), [(1, 2), (2, 1)])
    own = jnp.where(place[4] == place[3], own, turned)
    first = lax.axis_index("core") == 0
    near, back = shift(own, "x", 1), shift(own, "x", 3)
    own = [own, near, relay(jnp.where(first, near, back), "x"), back]
    blocks = [jnp.concatenate(blocks, axis=0)]
    near, back = shift(blocks[0], "y", 1), shift(blocks[0], "y", 3)
    own[0], own[1], own[3], near, back = lax.optimization_barrier(
        (own[0], own[1], own[3], near, back)
    )
    other = [swap(block, "core") for block in own]
    blocks += [near, relay(jnp.where(first, near, back), "y"), back]

    early_pair, early_down, pair_weights, down_weights = call(
        early_kernel,
        place,
        [blocks[0], blocks[1], blocks[3]] + own + other,
        [((slots, 2 * hidden), F32), ((slots, hidden), F32)]
        + [((2 * hidden, 4 * width), BF16), ((hidden, 4 * width), BF16)],
        [
            pltpu.VMEM((2, slots, 3 * width), BF16),
            pltpu.SemaphoreType.DMA((4, 2, 2)),
            pltpu.SemaphoreType.DMA((4, 1, 2)),
        ],
        [vmem] * 3 + [hbm] * 8,
    )

    def late(second, early, weights):
        return call(
            functools.partial(late_kernel, second),
            place,
            [early, blocks[2], weights],
            [(early.shape, BF16)],
            [pltpu.VMEM((slots, width), BF16)],
        )[0]

    pair = late(0, early_pair, pair_weights)
    pair_far = swap(pair, "zl")
    down = late(1, early_down, down_weights)
    down_far = swap(down, "zl")

    def halfway(passed, near, back):
        passed = passed.astype(F32)
        near = (near + jnp.where(first, 0.0, passed)).astype(BF16)
        return near, (back + jnp.where(first, passed, 0.0)).astype(BF16)

    unit = 2 * CAP + TILE
    tall = (8 * CAP + TILE, width)
    across, grads, marks = call(
        share_kernel,
        place,
        [pair, pair_far, down, down_far, pair_weights, down_weights],
        [(tall, BF16), ((slots, 3 * hidden), BF16), ((TILE, 128), F32)],
    )
    passed = relay(across, "y")
    near, back, mine = call(
        rest_kernel,
        place,
        [grads, marks, pair_weights, down_weights],
        [(tall, BF16), (tall, BF16), (tall, F32)],
    )
    terms = call(
        weight_kernel,
        place,
        [grads] + blocks,
        [((3, half, width), kind) for kind in (F32, BF16) for _ in range(4)],
        [pltpu.VMEM((2, 4, slots, width), BF16)],
    )
    keeps, sends = terms[0:4], terms[4:8]
    moved = [swap(send, "core") for send in sends]
    near, back = halfway(passed, near, back)
    near, back, *moved = lax.optimization_barrier((near, back, *moved))
    arrived = [shift(near, "y", -1), shift(back, "y", 1)]

    def both_cores(i):
        return keeps[i] + moved[i].astype(F32)

    passed = relay(both_cores(2).astype(BF16), "x")
    near, back = halfway(passed, both_cores(1), both_cores(3))
    far_sums = [shift(near, "x", -1), shift(back, "x", 1)]
    totals = call(total_kernel, place, [mine] + arrived, [((unit, width), BF16)] * 4)
    returned = [totals[0]] + [shift(totals[k], "expert", -k) for k in (1, 2, 3)]
    layer_output, token_grad, prob_grad = call(
        owner_kernel,
        place,
        [small, placing] + returned,
        [((rows, width), BF16), ((rows, width), BF16), ((8, rows), F32)],
    )
    weight_total = both_cores(0)
    for block in far_sums:
        weight_total = weight_total + block.astype(F32)
    weight_total = weight_total.astype(BF16).reshape(2, 3 * half // 2, width)
    parts = [turn(weight_total[n]) for n in range(2)]
    *parts, layer_output = lax.optimization_barrier((*parts, layer_output))
    weight_grad = jnp.concatenate([part.astype(F32) for part in parts])
    weight_grad = weight_grad.reshape(stacked_weights.shape)
    return layer_output, token_grad, prob_grad[0:2].T, weight_grad


def solution(mesh):
    split = Mesh(
        mesh.devices.reshape(4, 2, 4, 4, 2), ("x", "core", "expert", "y", "zl")
    )
    rows = P(("x", "core", "expert"), ("y", "zl"))
    pairs = P(("x", "core", "expert"), None)
    weights = P("expert", None, ("y", "zl"), ("x", "core"))
    return jax.shard_map(
        body,
        mesh=split,
        in_specs=(rows, pairs, pairs, weights, rows),
        out_specs=(rows, rows, pairs, weights),
        check_vma=False,
    )
```

```python
import functools

import functools

import jax
import jax.numpy as jnp
from jax import lax
from jax.experimental import pallas as pl
from jax.experimental.pallas import tpu as pltpu
from jax.sharding import Mesh, PartitionSpec as P

F32 = jnp.float32
BF16 = jnp.bfloat16
CAP = 80
TILE = 16
PARAMS = pltpu.CompilerParams(vmem_limit_bytes=48 * 1024 * 1024)


def nn(a, b):
    return lax.dot_general(a, b, (((1,), (0,)), ((), ())), preferred_element_type=F32)


def nt(a, b):
    return lax.dot_general(a, b, (((1,), (1,)), ((), ())), preferred_element_type=F32)


def tn(a, b):
    return lax.dot_general(a, b, (((0,), (0,)), ((), ())), preferred_element_type=F32)


def call(kernel, place, args, outs, scratch=(), spaces=None):
    whole = pl.BlockSpec(memory_space=pltpu.VMEM)
    return list(pl.pallas_call(
        kernel,
        out_shape=[jax.ShapeDtypeStruct(shape, kind) for shape, kind in outs],
        in_specs=[pl.BlockSpec(memory_space=pltpu.SMEM)] + (spaces or [whole] * len(args)),
        out_specs=[whole] * len(outs),
        scratch_shapes=list(scratch),
        compiler_params=PARAMS,
    )(place, *args))


def expert_rows(place, ids, k):
    expert = lax.rem(place[0] + k, 4).astype(F32)
    return ids[0:1, :] == expert, ids[1:2, :] == expert


def slots_kernel(place, small, wide, placing, *outs):
    ids, probs = small.at[0:2], small.at[2:4]
    width = wide.shape[1] // 2
    rows = ids.shape[1]
    before = (
        lax.broadcasted_iota(jnp.int32, (rows, rows), 0)
        < lax.broadcasted_iota(jnp.int32, (rows, rows), 1)
    ).astype(BF16)
    slot = lax.broadcasted_iota(jnp.int32, (CAP, rows), 0)
    scales = []
    for k in range(4):
        one, two = expert_rows(place, ids, k)
        named = jnp.logical_or(one, two)
        marks = jnp.broadcast_to(named, (8, rows)).astype(F32)
        position = nn(marks.astype(BF16), before)[0:1, :].astype(jnp.int32)
        weight = jnp.where(one, probs[0:1, :], probs[1:2, :])
        chosen = jnp.logical_and(
            jnp.broadcast_to(marks[0:1, :] > 0.5, (CAP, rows)),
            slot == jnp.broadcast_to(position, (CAP, rows)),
        )
        placing[k * CAP : (k + 1) * CAP, :] = chosen.astype(F32).astype(BF16)
        scales.append(jnp.sum(jnp.where(chosen, weight, 0.0), axis=1, keepdims=True))
    for k in range(4):
        hot = placing[k * CAP : (k + 1) * CAP, :]
        outs[k][0:CAP, :] = nn(hot, wide[:, 0:width]).astype(BF16)
        outs[k][CAP : 2 * CAP, :] = (scales[k] * nn(hot, wide[:, width:])).astype(BF16)


def fetch(own, other, joined, sems, names, place):
    half, width = own[0].shape[1:]
    copies = []
    for block in range(4):
        spot = lax.rem(place[2] - place[1] + block + 4, 4)
        columns = pl.ds(pl.multiple_of(spot * width, width), width)
        for n, m in enumerate(names):
            for h, source in enumerate((own[block], other[block])):
                copies.append(
                    pltpu.make_async_copy(
                        source.at[m],
                        joined.at[pl.ds((2 * n + h) * half, half), columns],
                        sems.at[block, n, h],
                    )
                )
    for copy in copies:
        copy.start()
    return copies


def take_rows(target, source, second):
    for k in range(4):
        first = (2 * k + second) * CAP
        target[k * CAP : (k + 1) * CAP, :] = source[first : first + CAP, :]


def project_kernel(names, second, place, *refs):
    rows, own, other = refs[0:4], refs[4:8], refs[8:12]
    out, joined, wide, sems = refs[12:16]
    width = rows[0].shape[1]
    copies = fetch(own, other, joined, sems, names, place)
    for j in range(4):
        take_rows(wide.at[:, pl.ds(j * width, width)], rows[j], second)
    for copy in copies:
        copy.wait()
    out[...] = nt(wide[...], joined[...]).astype(BF16)


def pieces(values):
    high = values.astype(BF16)
    rest = values - high.astype(F32)
    middle = rest.astype(BF16)
    low = (rest - middle.astype(F32)).astype(BF16)
    return high, middle, low


def marked_rows(row, first):
    spot = lax.broadcasted_iota(jnp.int32, (TILE, row.shape[1]), 0)
    total = jnp.zeros(spot.shape, F32)
    for n, part in enumerate(pieces(row)):
        total += jnp.where(spot == first + n, part.astype(F32), 0.0)
    return total


def share_kernel(place, pair, pair_far, down, down_far, pair_weights, down_weights, *refs):
    outs, hidden = refs[0:4], refs[4]
    width, step = down.shape[1], outs[0].shape[1]

    def both(near, far, n):
        columns = slice(n * width, (n + 1) * width)
        return near[:, columns].astype(F32) + far[:, columns].astype(F32)

    gate, up, grad = both(pair, pair_far, 0), both(pair, pair_far, 1), both(down, down_far, 0)
    sigmoid = 1.0 / (1.0 + jnp.exp(-gate))
    swish = gate * sigmoid
    act = (swish * up).astype(BF16)
    hidden[:, 2 * width :] = act
    hidden[:, 0:width] = (grad * up * sigmoid * (1.0 + gate * (1.0 - sigmoid))).astype(BF16)
    hidden[:, width : 2 * width] = (grad * swish).astype(BF16)
    share = jnp.sum(act.astype(F32) * grad, axis=1, keepdims=True)
    shape = (CAP, 128)
    same = lax.broadcasted_iota(jnp.int32, shape, 0) == lax.broadcasted_iota(jnp.int32, shape, 1)
    marks = jnp.zeros((TILE, 128), F32)
    for k in range(4):
        row = jnp.sum(
            jnp.where(same, share[k * CAP : (k + 1) * CAP, :], 0.0), axis=0, keepdims=True
        )
        marks += marked_rows(row, 3 * k)
    unit = 2 * CAP
    for j in (2, 1, 3, 0):
        kind = outs[j].dtype
        columns = slice(j * step, (j + 1) * step)
        out = nn(hidden[:, 2 * width :], down_weights[:, columns])
        back = nn(hidden[:, 0 : 2 * width], pair_weights[:, columns])
        for k in range(4):
            start, rows = k * unit, slice(k * CAP, (k + 1) * CAP)
            outs[j][start : start + CAP, :] = out[rows, :].astype(kind)
            outs[j][start + CAP : start + 2 * CAP, :] = back[rows, :].astype(kind)
        outs[j][4 * unit :, :] = jnp.zeros((TILE, step), kind)
        outs[j][4 * unit :, 0:128] = marks.astype(kind)


def total_kernel(place, own, one, three, *outs):
    unit = 2 * CAP

    def total(span, columns):
        value = own[span, columns] + one[span, columns].astype(F32)
        return value + three[span, columns].astype(F32)

    marks = total(slice(4 * unit, 4 * unit + TILE), slice(0, 128))
    width = own.shape[1]
    for k in range(4):
        outs[k][0:unit, :] = total(slice(k * unit, (k + 1) * unit), slice(0, width)).astype(BF16)
        row = jnp.sum(marks[3 * k : 3 * k + 3, :], axis=0, keepdims=True)
        outs[k][unit:, :] = jnp.zeros((TILE, width), BF16)
        outs[k][unit:, 0:128] = marked_rows(row, 0).astype(BF16)


def weight_kernel(place, joined, *refs):
    rows, keeps, sends, chosen = refs[0:4], refs[4:8], refs[8:12], refs[12]
    half = keeps[0].shape[1]
    for j in range(4):
        spot = lax.rem(place[1] - place[2] + j + 4, 4)
        for second in range(2):
            take_rows(chosen.at[second, spot], rows[j], second)
    for i in (2, 1, 3, 0):
        for m in range(3):
            columns = slice(2 * m * half, 2 * (m + 1) * half)
            total = tn(joined[:, columns], chosen[1 if m == 2 else 0, i])
            keeps[i][m] = total[0:half, :]
            sends[i][m] = total[half:, :].astype(BF16)


def column(row):
    rows = row.shape[1]
    shape = (rows, rows)
    same = lax.broadcasted_iota(jnp.int32, shape, 0) == lax.broadcasted_iota(jnp.int32, shape, 1)
    return jnp.sum(jnp.where(same, row, 0.0), axis=1, keepdims=True)


def owner_kernel(place, small, placing, *refs):
    ids, probs = small.at[0:2], small.at[2:4]
    blocks, layer, token, prob = refs[0:4], *refs[4:7]
    total = jnp.zeros(layer.shape, F32)
    grads = jnp.zeros(token.shape, F32)
    shares = [jnp.zeros((1, ids.shape[1]), F32) for _ in range(2)]
    for k in range(4):
        one, two = expert_rows(place, ids, k)
        hot = placing[k * CAP : (k + 1) * CAP, :]
        weight = jnp.where(one, probs[0:1, :], 0.0) + jnp.where(two, probs[1:2, :], 0.0)
        total += column(weight) * tn(hot, blocks[k][0:CAP, :])
        grads += tn(hot, blocks[k][CAP : 2 * CAP, :])
        found = nn(blocks[k][2 * CAP :, 0:128][:, 0:CAP], hot)
        share = jnp.sum(found, axis=0, keepdims=True)
        shares[0] += jnp.where(one, share, 0.0)
        shares[1] += jnp.where(two, share, 0.0)
    layer[...] = total.astype(BF16)
    token[...] = grads.astype(BF16)
    prob[...] = jnp.zeros(prob.shape, F32)
    for n in range(2):
        prob[n : n + 1, :] = shares[n] / probs[n : n + 1, :]


def shift(value, axis, step):
    return lax.ppermute(value, axis, [(i, (i + step) % 4) for i in range(4)])


def relay(value, axis):
    steps = [(c, i, (i + (3 if c else 1)) % 4) for c in range(2) for i in range(4)]
    if axis == "x":
        return lax.ppermute(value, ("x", "core"), [(2 * i + c, 2 * j + c) for c, i, j in steps])
    return lax.ppermute(value, ("core", axis), [(4 * c + i, 4 * c + j) for c, i, j in steps])


def swap(value, axis):
    return lax.ppermute(value, axis, [(0, 1), (1, 0)])


def turn(value):
    return lax.ppermute(value, ("core", "zl"), [(2 * c + z, 2 * z + c) for c in range(2) for z in range(2)])


def body(tokens, expert_ids, gate_probs, stacked_weights, out_grad):
    rows, width = tokens.shape
    half = stacked_weights.shape[2]
    hidden = 2 * half
    slots = 4 * CAP
    place = jnp.stack(
        [lax.axis_index(name) for name in ("expert", "x", "y", "zl", "core")]
    ).astype(jnp.int32)
    small = jnp.pad(expert_ids.T.astype(F32), ((0, 2), (0, 0))) + jnp.pad(
        gate_probs.T, ((2, 0), (0, 0))
    )
    wide = jnp.concatenate([tokens, out_grad], axis=1)
    vmem = pl.BlockSpec(memory_space=pltpu.VMEM)
    hbm = pl.BlockSpec(memory_space=pl.ANY)

    placing, *blocks = call(
        slots_kernel,
        place,
        [small, wide],
        [((slots, rows), BF16)] + [((2 * CAP, width), BF16)] * 4,
    )

    blocks = [blocks[0]] + [shift(blocks[k], "expert", k) for k in (1, 2, 3)]
    own = stacked_weights[0]
    turned = lax.ppermute(own, ("core", "zl"), [(1, 2), (2, 1)])
    own = jnp.where(place[4] == place[3], own, turned)
    first = lax.axis_index("core") == 0
    near, back = shift(own, "x", 1), shift(own, "x", 3)
    own = [own, near, relay(jnp.where(first, near, back), "x"), back]
    blocks = [jnp.concatenate(blocks, axis=0)]
    near, back = shift(blocks[0], "y", 1), shift(blocks[0], "y", 3)
    own[0], own[1], own[3], near, back = lax.optimization_barrier(
        (own[0], own[1], own[3], near, back)
    )
    other = [swap(block, "core") for block in own]
    blocks += [near, relay(jnp.where(first, near, back), "y"), back]

    def project(names, second):
        tall = len(names) * hidden
        return call(
            functools.partial(project_kernel, names, second),
            place,
            blocks + own + other,
            [((slots, tall), BF16), ((tall, 4 * width), BF16)],
            [pltpu.VMEM((slots, 4 * width), BF16), pltpu.SemaphoreType.DMA((4, 2, 2))],
            [vmem] * 4 + [hbm] * 8,
        )

    pair, pair_weights = project((0, 1), 0)
    pair_far = swap(pair, "zl")
    down, down_weights = project((2,), 1)
    down_far = swap(down, "zl")

    def halfway(passed, near, back):
        passed = passed.astype(F32)
        near = (near + jnp.where(first, 0.0, passed)).astype(BF16)
        return near, (back + jnp.where(first, passed, 0.0)).astype(BF16)

    unit = 2 * CAP + TILE
    shares = call(
        share_kernel,
        place,
        [pair, pair_far, down, down_far, pair_weights, down_weights],
        [((8 * CAP + TILE, width), F32)]
        + [((8 * CAP + TILE, width), BF16)] * 3
        + [((slots, 3 * hidden), BF16)],
    )
    passed = relay(shares[2], "y")
    terms = call(
        weight_kernel,
        place,
        [shares[4]] + blocks,
        [((3, half, width), kind) for kind in (F32, BF16) for _ in range(4)],
        [pltpu.VMEM((2, 4, slots, width), BF16)],
    )
    keeps, sends = terms[0:4], terms[4:8]
    moved = [swap(send, "core") for send in sends]
    near, back = halfway(passed, shares[1], shares[3])
    near, back, *moved = lax.optimization_barrier((near, back, *moved))
    arrived = [shift(near, "y", -1), shift(back, "y", 1)]

    def both_cores(i):
        return keeps[i] + moved[i].astype(F32)

    passed = relay(both_cores(2).astype(BF16), "x")
    near, back = halfway(passed, both_cores(1), both_cores(3))
    far_sums = [shift(near, "x", -1), shift(back, "x", 1)]
    totals = call(total_kernel, place, [shares[0]] + arrived, [((unit, width), BF16)] * 4)
    returned = [totals[0]] + [shift(totals[k], "expert", -k) for k in (1, 2, 3)]
    layer_output, token_grad, prob_grad = call(
        owner_kernel,
        place,
        [small, placing] + returned,
        [((rows, width), BF16), ((rows, width), BF16), ((8, rows), F32)],
    )
    weight_total = both_cores(0)
    for block in far_sums:
        weight_total = weight_total + block.astype(F32)
    weight_total = weight_total.astype(BF16).reshape(2, 3 * half // 2, width)
    parts = [turn(weight_total[n]) for n in range(2)]
    *parts, layer_output = lax.optimization_barrier((*parts, layer_output))
    weight_grad = jnp.concatenate([part.astype(F32) for part in parts])
    weight_grad = weight_grad.reshape(stacked_weights.shape)
    return layer_output, token_grad, prob_grad[0:2].T, weight_grad


def solution(mesh):
    split = Mesh(
        mesh.devices.reshape(4, 2, 4, 4, 2), ("x", "core", "expert", "y", "zl")
    )
    rows = P(("x", "core", "expert"), ("y", "zl"))
    pairs = P(("x", "core", "expert"), None)
    weights = P("expert", None, ("y", "zl"), ("x", "core"))
    return jax.shard_map(
        body,
        mesh=split,
        in_specs=(rows, pairs, pairs, weights, rows),
        out_specs=(rows, rows, pairs, weights),
        check_vma=False,
    )
```

```python
import functools

import functools

import jax
import jax.numpy as jnp
from jax import lax
from jax.experimental import pallas as pl
from jax.experimental.pallas import tpu as pltpu
from jax.sharding import Mesh, PartitionSpec as P

F32 = jnp.float32
BF16 = jnp.bfloat16
CAP = 80
TILE = 16
PARAMS = pltpu.CompilerParams(vmem_limit_bytes=48 * 1024 * 1024)


def nn(a, b):
    return lax.dot_general(a, b, (((1,), (0,)), ((), ())), preferred_element_type=F32)


def nt(a, b):
    return lax.dot_general(a, b, (((1,), (1,)), ((), ())), preferred_element_type=F32)


def tn(a, b):
    return lax.dot_general(a, b, (((0,), (0,)), ((), ())), preferred_element_type=F32)


def call(kernel, place, args, outs, scratch=(), spaces=None):
    whole = pl.BlockSpec(memory_space=pltpu.VMEM)
    return list(pl.pallas_call(
        kernel,
        out_shape=[jax.ShapeDtypeStruct(shape, kind) for shape, kind in outs],
        in_specs=[pl.BlockSpec(memory_space=pltpu.SMEM)] + (spaces or [whole] * len(args)),
        out_specs=[whole] * len(outs),
        scratch_shapes=list(scratch),
        compiler_params=PARAMS,
    )(place, *args))


def expert_rows(place, ids, k):
    expert = lax.rem(place[0] + k, 4).astype(F32)
    return ids[0:1, :] == expert, ids[1:2, :] == expert


def slots_kernel(place, small, wide, placing, *outs):
    ids, probs = small.at[0:2], small.at[2:4]
    width = wide.shape[1] // 2
    rows = ids.shape[1]
    before = (
        lax.broadcasted_iota(jnp.int32, (rows, rows), 0)
        < lax.broadcasted_iota(jnp.int32, (rows, rows), 1)
    ).astype(BF16)
    slot = lax.broadcasted_iota(jnp.int32, (CAP, rows), 0)
    scales = []
    for k in range(4):
        one, two = expert_rows(place, ids, k)
        named = jnp.logical_or(one, two)
        marks = jnp.broadcast_to(named, (8, rows)).astype(F32)
        position = nn(marks.astype(BF16), before)[0:1, :].astype(jnp.int32)
        weight = jnp.where(one, probs[0:1, :], probs[1:2, :])
        chosen = jnp.logical_and(
            jnp.broadcast_to(marks[0:1, :] > 0.5, (CAP, rows)),
            slot == jnp.broadcast_to(position, (CAP, rows)),
        )
        placing[k * CAP : (k + 1) * CAP, :] = chosen.astype(F32).astype(BF16)
        scales.append(jnp.sum(jnp.where(chosen, weight, 0.0), axis=1, keepdims=True))
    for k in range(4):
        hot = placing[k * CAP : (k + 1) * CAP, :]
        outs[k][0:CAP, :] = nn(hot, wide[:, 0:width]).astype(BF16)
        outs[k][CAP : 2 * CAP, :] = (scales[k] * nn(hot, wide[:, width:])).astype(BF16)


def fetch(own, other, joined, sems, names, place):
    half, width = own[0].shape[1:]
    copies = []
    for block in range(4):
        spot = lax.rem(place[2] - place[1] + block + 4, 4)
        columns = pl.ds(pl.multiple_of(spot * width, width), width)
        for n, m in enumerate(names):
            for h, source in enumerate((own[block], other[block])):
                copies.append(
                    pltpu.make_async_copy(
                        source.at[m],
                        joined.at[pl.ds((2 * n + h) * half, half), columns],
                        sems.at[block, n, h],
                    )
                )
    for copy in copies:
        copy.start()
    return copies


def take_rows(target, source, second):
    for k in range(4):
        first = (2 * k + second) * CAP
        target[k * CAP : (k + 1) * CAP, :] = source[first : first + CAP, :]


def project_kernel(names, second, place, *refs):
    rows, own, other = refs[0:4], refs[4:8], refs[8:12]
    out, joined, wide, sems = refs[12:16]
    width = rows[0].shape[1]
    copies = fetch(own, other, joined, sems, names, place)
    for j in range(4):
        take_rows(wide.at[:, pl.ds(j * width, width)], rows[j], second)
    for copy in copies:
        copy.wait()
    out[...] = nt(wide[...], joined[...]).astype(BF16)


def pieces(values):
    high = values.astype(BF16)
    rest = values - high.astype(F32)
    middle = rest.astype(BF16)
    low = (rest - middle.astype(F32)).astype(BF16)
    return high, middle, low


def marked_rows(row, first):
    spot = lax.broadcasted_iota(jnp.int32, (TILE, row.shape[1]), 0)
    total = jnp.zeros(spot.shape, F32)
    for n, part in enumerate(pieces(row)):
        total += jnp.where(spot == first + n, part.astype(F32), 0.0)
    return total


def share_kernel(place, pair, pair_far, down, down_far, pair_weights, down_weights, *refs):
    outs, hidden = refs[0:4], refs[4]
    width, step = down.shape[1], outs[0].shape[1]

    def both(near, far, n):
        columns = slice(n * width, (n + 1) * width)
        return near[:, columns].astype(F32) + far[:, columns].astype(F32)

    gate, up, grad = both(pair, pair_far, 0), both(pair, pair_far, 1), both(down, down_far, 0)
    sigmoid = 1.0 / (1.0 + jnp.exp(-gate))
    swish = gate * sigmoid
    act = (swish * up).astype(BF16)
    hidden[:, 2 * width :] = act
    hidden[:, 0:width] = (grad * up * sigmoid * (1.0 + gate * (1.0 - sigmoid))).astype(BF16)
    hidden[:, width : 2 * width] = (grad * swish).astype(BF16)
    share = jnp.sum(act.astype(F32) * grad, axis=1, keepdims=True)
    shape = (CAP, 128)
    same = lax.broadcasted_iota(jnp.int32, shape, 0) == lax.broadcasted_iota(jnp.int32, shape, 1)
    marks = jnp.zeros((TILE, 128), F32)
    for k in range(4):
        row = jnp.sum(
            jnp.where(same, share[k * CAP : (k + 1) * CAP, :], 0.0), axis=0, keepdims=True
        )
        marks += marked_rows(row, 3 * k)
    unit = 2 * CAP
    for j in (2, 1, 3, 0):
        kind = outs[j].dtype
        columns = slice(j * step, (j + 1) * step)
        out = nn(hidden[:, 2 * width :], down_weights[:, columns])
        back = nn(hidden[:, 0 : 2 * width], pair_weights[:, columns])
        for k in range(4):
            start, rows = k * unit, slice(k * CAP, (k + 1) * CAP)
            outs[j][start : start + CAP, :] = out[rows, :].astype(kind)
            outs[j][start + CAP : start + 2 * CAP, :] = back[rows, :].astype(kind)
        outs[j][4 * unit :, :] = jnp.zeros((TILE, step), kind)
        outs[j][4 * unit :, 0:128] = marks.astype(kind)


def total_kernel(place, own, one, three, *outs):
    unit = 2 * CAP

    def total(span, columns):
        value = own[span, columns] + one[span, columns].astype(F32)
        return value + three[span, columns].astype(F32)

    marks = total(slice(4 * unit, 4 * unit + TILE), slice(0, 128))
    width = own.shape[1]
    for k in range(4):
        outs[k][0:unit, :] = total(slice(k * unit, (k + 1) * unit), slice(0, width)).astype(BF16)
        row = jnp.sum(marks[3 * k : 3 * k + 3, :], axis=0, keepdims=True)
        outs[k][unit:, :] = jnp.zeros((TILE, width), BF16)
        outs[k][unit:, 0:128] = marked_rows(row, 0).astype(BF16)


def weight_kernel(place, joined, *refs):
    rows, keeps, sends, chosen = refs[0:4], refs[4:8], refs[8:12], refs[12]
    half = keeps[0].shape[1]
    for j in range(4):
        spot = lax.rem(place[1] - place[2] + j + 4, 4)
        for second in range(2):
            take_rows(chosen.at[second, spot], rows[j], second)
    for i in (2, 1, 3, 0):
        for m in range(3):
            columns = slice(2 * m * half, 2 * (m + 1) * half)
            total = tn(joined[:, columns], chosen[1 if m == 2 else 0, i])
            keeps[i][m] = total[0:half, :]
            sends[i][m] = total[half:, :].astype(BF16)


def column(row):
    rows = row.shape[1]
    shape = (rows, rows)
    same = lax.broadcasted_iota(jnp.int32, shape, 0) == lax.broadcasted_iota(jnp.int32, shape, 1)
    return jnp.sum(jnp.where(same, row, 0.0), axis=1, keepdims=True)


def owner_kernel(place, small, placing, *refs):
    ids, probs = small.at[0:2], small.at[2:4]
    blocks, layer, token, prob = refs[0:4], *refs[4:7]
    total = jnp.zeros(layer.shape, F32)
    grads = jnp.zeros(token.shape, F32)
    shares = [jnp.zeros((1, ids.shape[1]), F32) for _ in range(2)]
    for k in range(4):
        one, two = expert_rows(place, ids, k)
        hot = placing[k * CAP : (k + 1) * CAP, :]
        weight = jnp.where(one, probs[0:1, :], 0.0) + jnp.where(two, probs[1:2, :], 0.0)
        total += column(weight) * tn(hot, blocks[k][0:CAP, :])
        grads += tn(hot, blocks[k][CAP : 2 * CAP, :])
        found = nn(blocks[k][2 * CAP :, 0:128][:, 0:CAP], hot)
        share = jnp.sum(found, axis=0, keepdims=True)
        shares[0] += jnp.where(one, share, 0.0)
        shares[1] += jnp.where(two, share, 0.0)
    layer[...] = total.astype(BF16)
    token[...] = grads.astype(BF16)
    prob[...] = jnp.zeros(prob.shape, F32)
    for n in range(2):
        prob[n : n + 1, :] = shares[n] / probs[n : n + 1, :]


def shift(value, axis, step):
    return lax.ppermute(value, axis, [(i, (i + step) % 4) for i in range(4)])


def relay(value, axis):
    steps = [(c, i, (i + (3 if c else 1)) % 4) for c in range(2) for i in range(4)]
    if axis == "x":
        return lax.ppermute(value, ("x", "core"), [(2 * i + c, 2 * j + c) for c, i, j in steps])
    return lax.ppermute(value, ("core", axis), [(4 * c + i, 4 * c + j) for c, i, j in steps])


def swap(value, axis):
    return lax.ppermute(value, axis, [(0, 1), (1, 0)])


def turn(value):
    return lax.ppermute(value, ("core", "zl"), [(1, 2), (2, 1)])


def home(value, step):
    places = [(x, c, z) for x in range(4) for c in range(2) for z in range(2)]
    perm = [(4 * x + 2 * c + z, 4 * ((x + step) % 4) + 2 * z + c) for x, c, z in places]
    return lax.ppermute(value, ("x", "core", "zl"), perm)


def body(tokens, expert_ids, gate_probs, stacked_weights, out_grad):
    rows, width = tokens.shape
    half = stacked_weights.shape[2]
    hidden = 2 * half
    slots = 4 * CAP
    place = jnp.stack(
        [lax.axis_index(name) for name in ("expert", "x", "y", "zl", "core")]
    ).astype(jnp.int32)
    small = jnp.pad(expert_ids.T.astype(F32), ((0, 2), (0, 0))) + jnp.pad(
        gate_probs.T, ((2, 0), (0, 0))
    )
    wide = jnp.concatenate([tokens, out_grad], axis=1)
    vmem = pl.BlockSpec(memory_space=pltpu.VMEM)
    hbm = pl.BlockSpec(memory_space=pl.ANY)

    placing, *blocks = call(
        slots_kernel,
        place,
        [small, wide],
        [((slots, rows), BF16)] + [((2 * CAP, width), BF16)] * 4,
    )

    blocks = [blocks[0]] + [shift(blocks[k], "expert", k) for k in (1, 2, 3)]
    own = stacked_weights[0]
    turned = turn(own)
    own = jnp.where(place[4] == place[3], own, turned)
    first = lax.axis_index("core") == 0
    near, back = shift(own, "x", 1), shift(own, "x", 3)
    own = [own, near, relay(jnp.where(first, near, back), "x"), back]
    blocks = [jnp.concatenate(blocks, axis=0)]
    near, back = shift(blocks[0], "y", 1), shift(blocks[0], "y", 3)
    own[0], own[1], own[3], near, back = lax.optimization_barrier(
        (own[0], own[1], own[3], near, back)
    )
    other = [swap(block, "core") for block in own]
    blocks += [near, relay(jnp.where(first, near, back), "y"), back]

    def project(names, second):
        tall = len(names) * hidden
        return call(
            functools.partial(project_kernel, names, second),
            place,
            blocks + own + other,
            [((slots, tall), BF16), ((tall, 4 * width), BF16)],
            [pltpu.VMEM((slots, 4 * width), BF16), pltpu.SemaphoreType.DMA((4, 2, 2))],
            [vmem] * 4 + [hbm] * 8,
        )

    pair, pair_weights = project((0, 1), 0)
    pair_far = swap(pair, "zl")
    down, down_weights = project((2,), 1)
    down_far = swap(down, "zl")

    def halfway(passed, near, back):
        passed = passed.astype(F32)
        near = (near + jnp.where(first, 0.0, passed)).astype(BF16)
        return near, (back + jnp.where(first, passed, 0.0)).astype(BF16)

    unit = 2 * CAP + TILE
    shares = call(
        share_kernel,
        place,
        [pair, pair_far, down, down_far, pair_weights, down_weights],
        [((8 * CAP + TILE, width), F32)]
        + [((8 * CAP + TILE, width), BF16)] * 3
        + [((slots, 3 * hidden), BF16)],
    )
    passed = relay(shares[2], "y")
    terms = call(
        weight_kernel,
        place,
        [shares[4]] + blocks,
        [((3, half, width), kind) for kind in (F32, BF16) for _ in range(4)],
        [pltpu.VMEM((2, 4, slots, width), BF16)],
    )
    keeps, sends = terms[0:4], terms[4:8]
    moved = [swap(send, "core") for send in sends]
    near, back = halfway(passed, shares[1], shares[3])
    near, back, *moved = lax.optimization_barrier((near, back, *moved))
    arrived = [shift(near, "y", -1), shift(back, "y", 1)]

    def both_cores(i):
        return keeps[i] + moved[i].astype(F32)

    passed = relay(both_cores(2).astype(BF16), "x")
    near, back = halfway(passed, both_cores(1), both_cores(3))
    far_sums = [home(near, -1), home(back, 1)]
    mine_sum = both_cores(0)
    turned_sum = turn(mine_sum.astype(BF16))
    turned_sum, *arrived = lax.optimization_barrier((turned_sum, *arrived))
    totals = call(total_kernel, place, [shares[0]] + arrived, [((unit, width), BF16)] * 4)
    returned = [totals[0]] + [shift(totals[k], "expert", -k) for k in (1, 2, 3)]
    layer_output, token_grad, prob_grad = call(
        owner_kernel,
        place,
        [small, placing] + returned,
        [((rows, width), BF16), ((rows, width), BF16), ((8, rows), F32)],
    )
    weight_total = jnp.where(place[4] == place[3], mine_sum, turned_sum.astype(F32))
    for block in far_sums:
        weight_total = weight_total + block.astype(F32)
    weight_grad = weight_total[None]
    return layer_output, token_grad, prob_grad[0:2].T, weight_grad


def solution(mesh):
    split = Mesh(
        mesh.devices.reshape(4, 2, 4, 4, 2), ("x", "core", "expert", "y", "zl")
    )
    rows = P(("x", "core", "expert"), ("y", "zl"))
    pairs = P(("x", "core", "expert"), None)
    weights = P("expert", None, ("y", "zl"), ("x", "core"))
    return jax.shard_map(
        body,
        mesh=split,
        in_specs=(rows, pairs, pairs, weights, rows),
        out_specs=(rows, rows, pairs, weights),
        check_vma=False,
    )
```

```python
import functools

import functools

import jax
import jax.numpy as jnp
from jax import lax
from jax.experimental import pallas as pl
from jax.experimental.pallas import tpu as pltpu
from jax.sharding import Mesh, PartitionSpec as P

F32 = jnp.float32
BF16 = jnp.bfloat16
CAP = 80
TILE = 16
PARAMS = pltpu.CompilerParams(vmem_limit_bytes=48 * 1024 * 1024)


def nn(a, b):
    return lax.dot_general(a, b, (((1,), (0,)), ((), ())), preferred_element_type=F32)


def nt(a, b):
    return lax.dot_general(a, b, (((1,), (1,)), ((), ())), preferred_element_type=F32)


def tn(a, b):
    return lax.dot_general(a, b, (((0,), (0,)), ((), ())), preferred_element_type=F32)


def call(kernel, place, args, outs, scratch=(), spaces=None):
    whole = pl.BlockSpec(memory_space=pltpu.VMEM)
    return list(pl.pallas_call(
        kernel,
        out_shape=[jax.ShapeDtypeStruct(shape, kind) for shape, kind in outs],
        in_specs=[pl.BlockSpec(memory_space=pltpu.SMEM)] + (spaces or [whole] * len(args)),
        out_specs=[whole] * len(outs),
        scratch_shapes=list(scratch),
        compiler_params=PARAMS,
    )(place, *args))


def expert_rows(place, ids, k):
    expert = lax.rem(place[0] + k, 4).astype(F32)
    return ids[0:1, :] == expert, ids[1:2, :] == expert


def slots_kernel(place, small, wide, placing, *outs):
    ids, probs = small.at[0:2], small.at[2:4]
    width = wide.shape[1] // 2
    rows = ids.shape[1]
    before = (
        lax.broadcasted_iota(jnp.int32, (rows, rows), 0)
        < lax.broadcasted_iota(jnp.int32, (rows, rows), 1)
    ).astype(BF16)
    slot = lax.broadcasted_iota(jnp.int32, (CAP, rows), 0)
    scales = []
    for k in range(4):
        one, two = expert_rows(place, ids, k)
        named = jnp.logical_or(one, two)
        marks = jnp.broadcast_to(named, (8, rows)).astype(F32)
        position = nn(marks.astype(BF16), before)[0:1, :].astype(jnp.int32)
        weight = jnp.where(one, probs[0:1, :], probs[1:2, :])
        chosen = jnp.logical_and(
            jnp.broadcast_to(marks[0:1, :] > 0.5, (CAP, rows)),
            slot == jnp.broadcast_to(position, (CAP, rows)),
        )
        placing[k * CAP : (k + 1) * CAP, :] = chosen.astype(F32).astype(BF16)
        scales.append(jnp.sum(jnp.where(chosen, weight, 0.0), axis=1, keepdims=True))
    for k in range(4):
        hot = placing[k * CAP : (k + 1) * CAP, :]
        outs[k][0:CAP, :] = nn(hot, wide[:, 0:width]).astype(BF16)
        outs[k][CAP : 2 * CAP, :] = (scales[k] * nn(hot, wide[:, width:])).astype(BF16)


def fetch(own, other, joined, sems, names, place):
    half, width = own[0].shape[1:]
    copies = []
    for block in range(4):
        spot = lax.rem(place[2] - place[1] + block + 4, 4)
        columns = pl.ds(pl.multiple_of(spot * width, width), width)
        for n, m in enumerate(names):
            for h, source in enumerate((own[block], other[block])):
                copies.append(
                    pltpu.make_async_copy(
                        source.at[m],
                        joined.at[pl.ds((2 * n + h) * half, half), columns],
                        sems.at[block, n, h],
                    )
                )
    for copy in copies:
        copy.start()
    return copies


def take_rows(target, source, second):
    for k in range(4):
        first = (2 * k + second) * CAP
        target[k * CAP : (k + 1) * CAP, :] = source[first : first + CAP, :]


def project_kernel(names, second, place, *refs):
    rows, own, other = refs[0:4], refs[4:8], refs[8:12]
    out, joined, wide, sems = refs[12:16]
    width = rows[0].shape[1]
    copies = fetch(own, other, joined, sems, names, place)
    for j in range(4):
        take_rows(wide.at[:, pl.ds(j * width, width)], rows[j], second)
    late = 2 * len(copies) // 4
    for copy in copies[:late]:
        copy.wait()
    total = jnp.zeros(out.shape, F32)
    for block in range(4):
        if block == 2:
            for copy in copies[late:]:
                copy.wait()
        spot = lax.rem(place[2] - place[1] + block + 4, 4)
        columns = pl.ds(pl.multiple_of(spot * width, width), width)
        total += nt(wide[:, columns], joined[:, columns])
    out[...] = total.astype(BF16)


def pieces(values):
    high = values.astype(BF16)
    rest = values - high.astype(F32)
    middle = rest.astype(BF16)
    low = (rest - middle.astype(F32)).astype(BF16)
    return high, middle, low


def marked_rows(row, first):
    spot = lax.broadcasted_iota(jnp.int32, (TILE, row.shape[1]), 0)
    total = jnp.zeros(spot.shape, F32)
    for n, part in enumerate(pieces(row)):
        total += jnp.where(spot == first + n, part.astype(F32), 0.0)
    return total


def share_kernel(place, pair, pair_far, down, down_far, pair_weights, down_weights, *refs):
    outs, hidden = refs[0:4], refs[4]
    width, step = down.shape[1], outs[0].shape[1]

    def both(near, far, n):
        columns = slice(n * width, (n + 1) * width)
        return near[:, columns].astype(F32) + far[:, columns].astype(F32)

    gate, up, grad = both(pair, pair_far, 0), both(pair, pair_far, 1), both(down, down_far, 0)
    sigmoid = 1.0 / (1.0 + jnp.exp(-gate))
    swish = gate * sigmoid
    act = (swish * up).astype(BF16)
    hidden[:, 2 * width :] = act
    hidden[:, 0:width] = (grad * up * sigmoid * (1.0 + gate * (1.0 - sigmoid))).astype(BF16)
    hidden[:, width : 2 * width] = (grad * swish).astype(BF16)
    share = jnp.sum(act.astype(F32) * grad, axis=1, keepdims=True)
    shape = (CAP, 128)
    same = lax.broadcasted_iota(jnp.int32, shape, 0) == lax.broadcasted_iota(jnp.int32, shape, 1)
    marks = jnp.zeros((TILE, 128), F32)
    for k in range(4):
        row = jnp.sum(
            jnp.where(same, share[k * CAP : (k + 1) * CAP, :], 0.0), axis=0, keepdims=True
        )
        marks += marked_rows(row, 3 * k)
    unit = 2 * CAP
    for j in (2, 1, 3, 0):
        kind = outs[j].dtype
        columns = slice(j * step, (j + 1) * step)
        out = nn(hidden[:, 2 * width :], down_weights[:, columns])
        back = nn(hidden[:, 0 : 2 * width], pair_weights[:, columns])
        for k in range(4):
            start, rows = k * unit, slice(k * CAP, (k + 1) * CAP)
            outs[j][start : start + CAP, :] = out[rows, :].astype(kind)
            outs[j][start + CAP : start + 2 * CAP, :] = back[rows, :].astype(kind)
        outs[j][4 * unit :, :] = jnp.zeros((TILE, step), kind)
        outs[j][4 * unit :, 0:128] = marks.astype(kind)


def total_kernel(place, own, one, three, *outs):
    unit = 2 * CAP

    def total(span, columns):
        value = own[span, columns] + one[span, columns].astype(F32)
        return value + three[span, columns].astype(F32)

    marks = total(slice(4 * unit, 4 * unit + TILE), slice(0, 128))
    width = own.shape[1]
    for k in range(4):
        outs[k][0:unit, :] = total(slice(k * unit, (k + 1) * unit), slice(0, width)).astype(BF16)
        row = jnp.sum(marks[3 * k : 3 * k + 3, :], axis=0, keepdims=True)
        outs[k][unit:, :] = jnp.zeros((TILE, width), BF16)
        outs[k][unit:, 0:128] = marked_rows(row, 0).astype(BF16)


def weight_kernel(place, joined, *refs):
    rows, keeps, sends, chosen = refs[0:4], refs[4:8], refs[8:12], refs[12]
    half = keeps[0].shape[1]
    for j in range(4):
        spot = lax.rem(place[1] - place[2] + j + 4, 4)
        for second in range(2):
            take_rows(chosen.at[second, spot], rows[j], second)
    for i in (2, 1, 3, 0):
        for m in range(3):
            columns = slice(2 * m * half, 2 * (m + 1) * half)
            total = tn(joined[:, columns], chosen[1 if m == 2 else 0, i])
            keeps[i][m] = total[0:half, :].astype(BF16)
            sends[i][m] = total[half:, :].astype(BF16)


def column(row):
    rows = row.shape[1]
    shape = (rows, rows)
    same = lax.broadcasted_iota(jnp.int32, shape, 0) == lax.broadcasted_iota(jnp.int32, shape, 1)
    return jnp.sum(jnp.where(same, row, 0.0), axis=1, keepdims=True)


def owner_kernel(place, small, placing, *refs):
    ids, probs = small.at[0:2], small.at[2:4]
    blocks, layer, token, prob = refs[0:4], *refs[4:7]
    total = jnp.zeros(layer.shape, F32)
    grads = jnp.zeros(token.shape, F32)
    shares = [jnp.zeros((1, ids.shape[1]), F32) for _ in range(2)]
    for k in range(4):
        one, two = expert_rows(place, ids, k)
        hot = placing[k * CAP : (k + 1) * CAP, :]
        weight = jnp.where(one, probs[0:1, :], 0.0) + jnp.where(two, probs[1:2, :], 0.0)
        total += column(weight) * tn(hot, blocks[k][0:CAP, :])
        grads += tn(hot, blocks[k][CAP : 2 * CAP, :])
        found = nn(blocks[k][2 * CAP :, 0:128][:, 0:CAP], hot)
        share = jnp.sum(found, axis=0, keepdims=True)
        shares[0] += jnp.where(one, share, 0.0)
        shares[1] += jnp.where(two, share, 0.0)
    layer[...] = total.astype(BF16)
    token[...] = grads.astype(BF16)
    prob[...] = jnp.zeros(prob.shape, F32)
    for n in range(2):
        prob[n : n + 1, :] = shares[n] / probs[n : n + 1, :]


def shift(value, axis, step):
    return lax.ppermute(value, axis, [(i, (i + step) % 4) for i in range(4)])


def relay(value, axis):
    steps = [(c, i, (i + (3 if c else 1)) % 4) for c in range(2) for i in range(4)]
    if axis == "x":
        return lax.ppermute(value, ("x", "core"), [(2 * i + c, 2 * j + c) for c, i, j in steps])
    return lax.ppermute(value, ("core", axis), [(4 * c + i, 4 * c + j) for c, i, j in steps])


def swap(value, axis):
    return lax.ppermute(value, axis, [(0, 1), (1, 0)])


def turn(value):
    return lax.ppermute(value, ("core", "zl"), [(2 * c + z, 2 * z + c) for c in range(2) for z in range(2)])


def body(tokens, expert_ids, gate_probs, stacked_weights, out_grad):
    rows, width = tokens.shape
    half = stacked_weights.shape[2]
    hidden = 2 * half
    slots = 4 * CAP
    place = jnp.stack(
        [lax.axis_index(name) for name in ("expert", "x", "y", "zl", "core")]
    ).astype(jnp.int32)
    small = jnp.concatenate([expert_ids.T.astype(F32), gate_probs.T])
    wide = jnp.concatenate([tokens, out_grad], axis=1)
    vmem = pl.BlockSpec(memory_space=pltpu.VMEM)
    hbm = pl.BlockSpec(memory_space=pl.ANY)

    placing, *blocks = call(
        slots_kernel,
        place,
        [small, wide],
        [((slots, rows), BF16)] + [((2 * CAP, width), BF16)] * 4,
    )

    blocks = [blocks[0]] + [shift(blocks[k], "expert", k) for k in (1, 2, 3)]
    own, blocks[0] = lax.optimization_barrier((stacked_weights[0], blocks[0]))
    turned = lax.ppermute(own, ("core", "zl"), [(1, 2), (2, 1)])
    own = jnp.where(place[4] == place[3], own, turned)
    first = lax.axis_index("core") == 0
    near, back = shift(own, "x", 1), shift(own, "x", 3)
    own = [own, near, relay(jnp.where(first, near, back), "x"), back]
    blocks = [jnp.concatenate(blocks, axis=0)]
    near, back = shift(blocks[0], "y", 1), shift(blocks[0], "y", 3)
    own[0], own[1], own[3], near, back = lax.optimization_barrier(
        (own[0], own[1], own[3], near, back)
    )
    other = [swap(block, "core") for block in own]
    blocks += [near, relay(jnp.where(first, near, back), "y"), back]

    def project(names, second):
        tall = len(names) * hidden
        return call(
            functools.partial(project_kernel, names, second),
            place,
            blocks + own + other,
            [((slots, tall), BF16), ((tall, 4 * width), BF16)],
            [pltpu.VMEM((slots, 4 * width), BF16), pltpu.SemaphoreType.DMA((4, 2, 2))],
            [vmem] * 4 + [hbm] * 8,
        )

    pair, pair_weights = project((0, 1), 0)
    pair_far = swap(pair, "zl")
    down, down_weights = project((2,), 1)
    down_far = swap(down, "zl")

    def halfway(passed, near, back):
        passed = passed.astype(F32)
        near = (near + jnp.where(first, 0.0, passed)).astype(BF16)
        return near, (back + jnp.where(first, passed, 0.0)).astype(BF16)

    unit = 2 * CAP + TILE
    shares = call(
        share_kernel,
        place,
        [pair, pair_far, down, down_far, pair_weights, down_weights],
        [((8 * CAP + TILE, width), F32)]
        + [((8 * CAP + TILE, width), BF16)] * 3
        + [((slots, 3 * hidden), BF16)],
    )
    passed = relay(shares[2], "y")
    terms = call(
        weight_kernel,
        place,
        [shares[4]] + blocks,
        [((3, half, width), BF16)] * 8,
        [pltpu.VMEM((2, 4, slots, width), BF16)],
    )
    keeps, sends = terms[0:4], terms[4:8]
    moved = [swap(send, "core") for send in sends]
    near, back = halfway(passed, shares[1], shares[3])
    near, back, *moved = lax.optimization_barrier((near, back, *moved))
    arrived = [shift(near, "y", -1), shift(back, "y", 1)]

    def both_cores(i):
        return keeps[i].astype(F32) + moved[i].astype(F32)

    passed = relay(both_cores(2).astype(BF16), "x")
    near, back = halfway(passed, both_cores(1), both_cores(3))
    far_sums = [shift(near, "x", -1), shift(back, "x", 1)]
    totals = call(total_kernel, place, [shares[0]] + arrived, [((unit, width), BF16)] * 4)
    returned = [totals[0]] + [shift(totals[k], "expert", -k) for k in (1, 2, 3)]
    layer_output, token_grad, prob_grad = call(
        owner_kernel,
        place,
        [small, placing] + returned,
        [((rows, width), BF16), ((rows, width), BF16), ((8, rows), F32)],
    )
    weight_total = both_cores(0)
    for block in far_sums:
        weight_total = weight_total + block.astype(F32)
    weight_total = weight_total.astype(BF16).reshape(2, 3 * half // 2, width)
    parts = [turn(weight_total[n]) for n in range(2)]
    *parts, layer_output = lax.optimization_barrier((*parts, layer_output))
    weight_grad = jnp.concatenate([part.astype(F32) for part in parts])
    weight_grad = weight_grad.reshape(stacked_weights.shape)
    return layer_output, token_grad, prob_grad[0:2].T, weight_grad


def solution(mesh):
    split = Mesh(
        mesh.devices.reshape(4, 2, 4, 4, 2), ("x", "core", "expert", "y", "zl")
    )
    rows = P(("x", "core", "expert"), ("y", "zl"))
    pairs = P(("x", "core", "expert"), None)
    weights = P("expert", None, ("y", "zl"), ("x", "core"))
    return jax.shard_map(
        body,
        mesh=split,
        in_specs=(rows, pairs, pairs, weights, rows),
        out_specs=(rows, rows, pairs, weights),
        check_vma=False,
    )
```

```python
import functools

import functools

import jax
import jax.numpy as jnp
from jax import lax
from jax.experimental import pallas as pl
from jax.experimental.pallas import tpu as pltpu
from jax.sharding import Mesh, PartitionSpec as P

F32 = jnp.float32
BF16 = jnp.bfloat16
CAP = 80
TILE = 16
PARAMS = pltpu.CompilerParams(vmem_limit_bytes=48 * 1024 * 1024)


def nn(a, b):
    return lax.dot_general(a, b, (((1,), (0,)), ((), ())), preferred_element_type=F32)


def nt(a, b):
    return lax.dot_general(a, b, (((1,), (1,)), ((), ())), preferred_element_type=F32)


def tn(a, b):
    return lax.dot_general(a, b, (((0,), (0,)), ((), ())), preferred_element_type=F32)


def call(kernel, place, args, outs, scratch=(), spaces=None):
    whole = pl.BlockSpec(memory_space=pltpu.VMEM)
    return list(pl.pallas_call(
        kernel,
        out_shape=[jax.ShapeDtypeStruct(shape, kind) for shape, kind in outs],
        in_specs=[pl.BlockSpec(memory_space=pltpu.SMEM)] + (spaces or [whole] * len(args)),
        out_specs=[whole] * len(outs),
        scratch_shapes=list(scratch),
        compiler_params=PARAMS,
    )(place, *args))


def expert_rows(place, ids, k):
    expert = lax.rem(place[0] + k, 4).astype(F32)
    return ids[0:1, :] == expert, ids[1:2, :] == expert


def slots_kernel(place, small, wide, placing, *outs):
    ids, probs = small.at[0:2], small.at[2:4]
    width = wide.shape[1] // 2
    rows = ids.shape[1]
    before = (
        lax.broadcasted_iota(jnp.int32, (rows, rows), 0)
        < lax.broadcasted_iota(jnp.int32, (rows, rows), 1)
    ).astype(BF16)
    slot = lax.broadcasted_iota(jnp.int32, (CAP, rows), 0)
    scales = []
    for k in range(4):
        one, two = expert_rows(place, ids, k)
        named = jnp.logical_or(one, two)
        marks = jnp.broadcast_to(named, (8, rows)).astype(F32)
        position = nn(marks.astype(BF16), before)[0:1, :].astype(jnp.int32)
        weight = jnp.where(one, probs[0:1, :], probs[1:2, :])
        chosen = jnp.logical_and(
            jnp.broadcast_to(marks[0:1, :] > 0.5, (CAP, rows)),
            slot == jnp.broadcast_to(position, (CAP, rows)),
        )
        placing[k * CAP : (k + 1) * CAP, :] = chosen.astype(F32).astype(BF16)
        scales.append(jnp.sum(jnp.where(chosen, weight, 0.0), axis=1, keepdims=True))
    for k in range(4):
        hot = placing[k * CAP : (k + 1) * CAP, :]
        outs[k][0:CAP, :] = nn(hot, wide[:, 0:width]).astype(BF16)
        outs[k][CAP : 2 * CAP, :] = (scales[k] * nn(hot, wide[:, width:])).astype(BF16)


def fetch(own, other, joined, sems, names, place):
    half, width = own[0].shape[1:]
    copies = []
    for block in range(4):
        spot = lax.rem(place[2] - place[1] + block + 4, 4)
        columns = pl.ds(pl.multiple_of(spot * width, width), width)
        for n, m in enumerate(names):
            for h, source in enumerate((own[block], other[block])):
                copies.append(
                    pltpu.make_async_copy(
                        source.at[m],
                        joined.at[pl.ds((2 * n + h) * half, half), columns],
                        sems.at[block, n, h],
                    )
                )
    for copy in copies:
        copy.start()
    return copies


def take_rows(target, source, second):
    for k in range(4):
        first = (2 * k + second) * CAP
        target[k * CAP : (k + 1) * CAP, :] = source[first : first + CAP, :]


def project_kernel(names, second, place, *refs):
    rows, own, other = refs[0:4], refs[4:8], refs[8:12]
    out, joined, wide, sems = refs[12:16]
    width = rows[0].shape[1]
    copies = fetch(own, other, joined, sems, names, place)
    for j in range(4):
        take_rows(wide.at[:, pl.ds(j * width, width)], rows[j], second)
    for copy in copies:
        copy.wait()
    out[...] = nt(wide[...], joined[...]).astype(BF16)


def pieces(values):
    high = values.astype(BF16)
    rest = values - high.astype(F32)
    middle = rest.astype(BF16)
    low = (rest - middle.astype(F32)).astype(BF16)
    return high, middle, low


def marked_rows(row, first):
    spot = lax.broadcasted_iota(jnp.int32, (TILE, row.shape[1]), 0)
    total = jnp.zeros(spot.shape, F32)
    for n, part in enumerate(pieces(row)):
        total += jnp.where(spot == first + n, part.astype(F32), 0.0)
    return total


def share_kernel(place, pair, pair_far, down, down_far, pair_weights, down_weights, *refs):
    outs, hidden = refs[0:4], refs[4]
    width, step = down.shape[1], outs[0].shape[1]

    def both(near, far, n):
        columns = slice(n * width, (n + 1) * width)
        return near[:, columns].astype(F32) + far[:, columns].astype(F32)

    gate, up, grad = both(pair, pair_far, 0), both(pair, pair_far, 1), both(down, down_far, 0)
    sigmoid = 1.0 / (1.0 + jnp.exp(-gate))
    swish = gate * sigmoid
    act = (swish * up).astype(BF16)
    hidden[:, 2 * width :] = act
    hidden[:, 0:width] = (grad * up * sigmoid * (1.0 + gate * (1.0 - sigmoid))).astype(BF16)
    hidden[:, width : 2 * width] = (grad * swish).astype(BF16)
    share = jnp.sum(act.astype(F32) * grad, axis=1, keepdims=True)
    shape = (CAP, 128)
    same = lax.broadcasted_iota(jnp.int32, shape, 0) == lax.broadcasted_iota(jnp.int32, shape, 1)
    marks = jnp.zeros((TILE, 128), F32)
    for k in range(4):
        row = jnp.sum(
            jnp.where(same, share[k * CAP : (k + 1) * CAP, :], 0.0), axis=0, keepdims=True
        )
        marks += marked_rows(row, 3 * k)
    unit = 2 * CAP
    for j in (2, 1, 3, 0):
        kind = outs[j].dtype
        columns = slice(j * step, (j + 1) * step)
        out = nn(hidden[:, 2 * width :], down_weights[:, columns])
        back = nn(hidden[:, 0 : 2 * width], pair_weights[:, columns])
        for k in range(4):
            start, rows = k * unit, slice(k * CAP, (k + 1) * CAP)
            outs[j][start : start + CAP, :] = out[rows, :].astype(kind)
            outs[j][start + CAP : start + 2 * CAP, :] = back[rows, :].astype(kind)
        outs[j][4 * unit :, :] = jnp.zeros((TILE, step), kind)
        outs[j][4 * unit :, 0:128] = marks.astype(kind)


def total_kernel(place, own, one, three, *outs):
    unit = 2 * CAP

    def total(span, columns):
        value = own[span, columns] + one[span, columns].astype(F32)
        return value + three[span, columns].astype(F32)

    marks = total(slice(4 * unit, 4 * unit + TILE), slice(0, 128))
    width = own.shape[1]
    for k in range(4):
        outs[k][0:unit, :] = total(slice(k * unit, (k + 1) * unit), slice(0, width)).astype(BF16)
        row = jnp.sum(marks[3 * k : 3 * k + 3, :], axis=0, keepdims=True)
        outs[k][unit:, :] = jnp.zeros((TILE, width), BF16)
        outs[k][unit:, 0:128] = marked_rows(row, 0).astype(BF16)


def weight_kernel(place, joined, *refs):
    rows, keeps, sends, chosen = refs[0:4], refs[4:8], refs[8:12], refs[12]
    half = keeps[0].shape[1]
    for j in range(4):
        spot = lax.rem(place[1] - place[2] + j + 4, 4)
        for second in range(2):
            take_rows(chosen.at[second, spot], rows[j], second)
    for i in (2, 1, 3, 0):
        for m in range(3):
            columns = slice(2 * m * half, 2 * (m + 1) * half)
            total = tn(joined[:, columns], chosen[1 if m == 2 else 0, i])
            keeps[i][m] = total[0:half, :].astype(BF16)
            sends[i][m] = total[half:, :].astype(BF16)


def column(row):
    rows = row.shape[1]
    shape = (rows, rows)
    same = lax.broadcasted_iota(jnp.int32, shape, 0) == lax.broadcasted_iota(jnp.int32, shape, 1)
    return jnp.sum(jnp.where(same, row, 0.0), axis=1, keepdims=True)


def owner_kernel(place, small, placing, *refs):
    ids, probs = small.at[0:2], small.at[2:4]
    blocks, layer, token, prob = refs[0:4], *refs[4:7]
    total = jnp.zeros(layer.shape, F32)
    grads = jnp.zeros(token.shape, F32)
    shares = [jnp.zeros((1, ids.shape[1]), F32) for _ in range(2)]
    for k in range(4):
        one, two = expert_rows(place, ids, k)
        hot = placing[k * CAP : (k + 1) * CAP, :]
        weight = jnp.where(one, probs[0:1, :], 0.0) + jnp.where(two, probs[1:2, :], 0.0)
        total += column(weight) * tn(hot, blocks[k][0:CAP, :])
        grads += tn(hot, blocks[k][CAP : 2 * CAP, :])
        found = nn(blocks[k][2 * CAP :, 0:128][:, 0:CAP], hot)
        share = jnp.sum(found, axis=0, keepdims=True)
        shares[0] += jnp.where(one, share, 0.0)
        shares[1] += jnp.where(two, share, 0.0)
    layer[...] = total.astype(BF16)
    token[...] = grads.astype(BF16)
    prob[...] = jnp.zeros(prob.shape, F32)
    for n in range(2):
        prob[n : n + 1, :] = shares[n] / probs[n : n + 1, :]


def shift(value, axis, step):
    return lax.ppermute(value, axis, [(i, (i + step) % 4) for i in range(4)])


def relay(value, axis):
    steps = [(c, i, (i + (3 if c else 1)) % 4) for c in range(2) for i in range(4)]
    if axis == "x":
        return lax.ppermute(value, ("x", "core"), [(2 * i + c, 2 * j + c) for c, i, j in steps])
    return lax.ppermute(value, ("core", axis), [(4 * c + i, 4 * c + j) for c, i, j in steps])


def swap(value, axis):
    return lax.ppermute(value, axis, [(0, 1), (1, 0)])


def turn(value):
    return lax.ppermute(value, ("core", "zl"), [(2 * c + z, 2 * z + c) for c in range(2) for z in range(2)])


def body(tokens, expert_ids, gate_probs, stacked_weights, out_grad):
    rows, width = tokens.shape
    half = stacked_weights.shape[2]
    hidden = 2 * half
    slots = 4 * CAP
    place = jnp.stack(
        [lax.axis_index(name) for name in ("expert", "x", "y", "zl", "core")]
    ).astype(jnp.int32)
    small = jnp.concatenate([expert_ids.T.astype(F32), gate_probs.T])
    wide = jnp.concatenate([tokens, out_grad], axis=1)
    vmem = pl.BlockSpec(memory_space=pltpu.VMEM)
    hbm = pl.BlockSpec(memory_space=pl.ANY)

    placing, *blocks = call(
        slots_kernel,
        place,
        [small, wide],
        [((slots, rows), BF16)] + [((2 * CAP, width), BF16)] * 4,
    )

    blocks = [blocks[0]] + [shift(blocks[k], "expert", k) for k in (1, 2, 3)]
    own, blocks[0] = lax.optimization_barrier((stacked_weights[0], blocks[0]))
    turned = lax.ppermute(own, ("core", "zl"), [(1, 2), (2, 1)])
    own = jnp.where(place[4] == place[3], own, turned)
    first = lax.axis_index("core") == 0
    near, back = shift(own, "x", 1), shift(own, "x", 3)
    own = [own, near, relay(jnp.where(first, near, back), "x"), back]
    blocks = [jnp.concatenate(blocks, axis=0)]
    near, back = shift(blocks[0], "y", 1), shift(blocks[0], "y", 3)
    own[0], own[1], own[3], near, back = lax.optimization_barrier(
        (own[0], own[1], own[3], near, back)
    )
    other = [swap(block, "core") for block in own]
    blocks += [near, relay(jnp.where(first, near, back), "y"), back]

    def project(names, second):
        tall = len(names) * hidden
        return call(
            functools.partial(project_kernel, names, second),
            place,
            blocks + own + other,
            [((slots, tall), BF16), ((tall, 4 * width), BF16)],
            [pltpu.VMEM((slots, 4 * width), BF16), pltpu.SemaphoreType.DMA((4, 2, 2))],
            [vmem] * 4 + [hbm] * 8,
        )

    pair, pair_weights = project((0, 1), 0)
    pair_far = swap(pair, "zl")
    down, down_weights = project((2,), 1)
    down_far = swap(down, "zl")

    def halfway(passed, near, back):
        passed = passed.astype(F32)
        near = (near + jnp.where(first, 0.0, passed)).astype(BF16)
        return near, (back + jnp.where(first, passed, 0.0)).astype(BF16)

    unit = 2 * CAP + TILE
    shares = call(
        share_kernel,
        place,
        [pair, pair_far, down, down_far, pair_weights, down_weights],
        [((8 * CAP + TILE, width), F32)]
        + [((8 * CAP + TILE, width), BF16)] * 3
        + [((slots, 3 * hidden), BF16)],
    )
    passed = relay(shares[2], "y")
    terms = call(
        weight_kernel,
        place,
        [shares[4]] + blocks,
        [((3, half, width), BF16)] * 8,
        [pltpu.VMEM((2, 4, slots, width), BF16)],
    )
    keeps, sends = terms[0:4], terms[4:8]
    moved = [swap(send, "core") for send in sends]
    near, back = halfway(passed, shares[1], shares[3])
    near, back, *moved = lax.optimization_barrier((near, back, *moved))
    arrived = [shift(near, "y", -1), shift(back, "y", 1)]

    def both_cores(i):
        return keeps[i].astype(F32) + moved[i].astype(F32)

    passed = relay(both_cores(2).astype(BF16), "x")
    near, back = halfway(passed, both_cores(1), both_cores(3))
    far_sums = [shift(near, "x", -1), shift(back, "x", 1)]
    totals = call(total_kernel, place, [shares[0]] + arrived, [((unit, width), BF16)] * 4)
    returned = [totals[0]] + [shift(totals[k], "expert", -k) for k in (1, 2, 3)]
    weight_total = both_cores(0)
    for block in far_sums:
        weight_total = weight_total + block.astype(F32)
    weight_total = weight_total.astype(BF16)
    weight_total, *returned[1:] = lax.optimization_barrier((weight_total, *returned[1:]))
    layer_output, token_grad, prob_grad = call(
        owner_kernel,
        place,
        [small, placing] + returned,
        [((rows, width), BF16), ((rows, width), BF16), ((8, rows), F32)],
    )
    weight_grad = turn(weight_total).astype(F32)[None]
    return layer_output, token_grad, prob_grad[0:2].T, weight_grad


def solution(mesh):
    split = Mesh(
        mesh.devices.reshape(4, 2, 4, 4, 2), ("x", "core", "expert", "y", "zl")
    )
    rows = P(("x", "core", "expert"), ("y", "zl"))
    pairs = P(("x", "core", "expert"), None)
    weights = P("expert", None, ("y", "zl"), ("x", "core"))
    return jax.shard_map(
        body,
        mesh=split,
        in_specs=(rows, pairs, pairs, weights, rows),
        out_specs=(rows, rows, pairs, weights),
        check_vma=False,
    )
```

```python
import functools

import functools

import jax
import jax.numpy as jnp
from jax import lax
from jax.experimental import pallas as pl
from jax.experimental.pallas import tpu as pltpu
from jax.sharding import Mesh, PartitionSpec as P

F32 = jnp.float32
BF16 = jnp.bfloat16
CAP = 80
TILE = 16
PARAMS = pltpu.CompilerParams(vmem_limit_bytes=48 * 1024 * 1024)


def nn(a, b):
    return lax.dot_general(a, b, (((1,), (0,)), ((), ())), preferred_element_type=F32)


def nt(a, b):
    return lax.dot_general(a, b, (((1,), (1,)), ((), ())), preferred_element_type=F32)


def tn(a, b):
    return lax.dot_general(a, b, (((0,), (0,)), ((), ())), preferred_element_type=F32)


def call(kernel, place, args, outs, scratch=(), spaces=None):
    whole = pl.BlockSpec(memory_space=pltpu.VMEM)
    return list(pl.pallas_call(
        kernel,
        out_shape=[jax.ShapeDtypeStruct(shape, kind) for shape, kind in outs],
        in_specs=[pl.BlockSpec(memory_space=pltpu.SMEM)] + (spaces or [whole] * len(args)),
        out_specs=[whole] * len(outs),
        scratch_shapes=list(scratch),
        compiler_params=PARAMS,
    )(place, *args))


def expert_rows(place, ids, k):
    expert = lax.rem(place[0] + k, 4).astype(F32)
    return ids[0:1, :] == expert, ids[1:2, :] == expert


def slots_kernel(place, small, wide, placing, *outs):
    ids, probs = small.at[0:2], small.at[2:4]
    width = wide.shape[1] // 2
    rows = ids.shape[1]
    before = (
        lax.broadcasted_iota(jnp.int32, (rows, rows), 0)
        < lax.broadcasted_iota(jnp.int32, (rows, rows), 1)
    ).astype(BF16)
    slot = lax.broadcasted_iota(jnp.int32, (CAP, rows), 0)
    scales = []
    for k in range(4):
        one, two = expert_rows(place, ids, k)
        named = jnp.logical_or(one, two)
        marks = jnp.broadcast_to(named, (8, rows)).astype(F32)
        position = nn(marks.astype(BF16), before)[0:1, :].astype(jnp.int32)
        weight = jnp.where(one, probs[0:1, :], probs[1:2, :])
        chosen = jnp.logical_and(
            jnp.broadcast_to(marks[0:1, :] > 0.5, (CAP, rows)),
            slot == jnp.broadcast_to(position, (CAP, rows)),
        )
        placing[k * CAP : (k + 1) * CAP, :] = chosen.astype(F32).astype(BF16)
        scales.append(jnp.sum(jnp.where(chosen, weight, 0.0), axis=1, keepdims=True))
    for k in range(4):
        hot = placing[k * CAP : (k + 1) * CAP, :]
        outs[k][0:CAP, :] = nn(hot, wide[:, 0:width]).astype(BF16)
        outs[k][CAP : 2 * CAP, :] = (scales[k] * nn(hot, wide[:, width:])).astype(BF16)


def fetch(own, other, joined, sems, names, place):
    half, width = own[0].shape[1:]
    copies = []
    for block in range(4):
        spot = lax.rem(block + (1 - 2 * place[4]) * (place[2] - place[1]) + 8, 4)
        columns = pl.ds(pl.multiple_of(spot * width, width), width)
        for n, m in enumerate(names):
            for h, source in enumerate((own[block], other[block])):
                copies.append(
                    pltpu.make_async_copy(
                        source.at[m],
                        joined.at[pl.ds((2 * n + h) * half, half), columns],
                        sems.at[block, n, h],
                    )
                )
    for copy in copies:
        copy.start()
    return copies


def take_rows(target, source, second):
    for k in range(4):
        first = (2 * k + second) * CAP
        target[k * CAP : (k + 1) * CAP, :] = source[first : first + CAP, :]


def project_kernel(names, second, place, *refs):
    rows, own, other = refs[0:4], refs[4:8], refs[8:12]
    out, joined, wide, sems = refs[12:16]
    width = rows[0].shape[1]
    copies = fetch(own, other, joined, sems, names, place)
    for j in range(4):
        take_rows(wide.at[:, pl.ds(j * width, width)], rows[j], second)
    for copy in copies:
        copy.wait()
    out[...] = nt(wide[...], joined[...]).astype(BF16)


def pieces(values):
    high = values.astype(BF16)
    rest = values - high.astype(F32)
    middle = rest.astype(BF16)
    low = (rest - middle.astype(F32)).astype(BF16)
    return high, middle, low


def marked_rows(row, first):
    spot = lax.broadcasted_iota(jnp.int32, (TILE, row.shape[1]), 0)
    total = jnp.zeros(spot.shape, F32)
    for n, part in enumerate(pieces(row)):
        total += jnp.where(spot == first + n, part.astype(F32), 0.0)
    return total


def share_kernel(place, pair, pair_far, down, down_far, pair_weights, down_weights, *refs):
    outs, hidden = refs[0:4], refs[4]
    width, step = down.shape[1], outs[0].shape[1]

    def both(near, far, n):
        columns = slice(n * width, (n + 1) * width)
        return near[:, columns].astype(F32) + far[:, columns].astype(F32)

    gate, up, grad = both(pair, pair_far, 0), both(pair, pair_far, 1), both(down, down_far, 0)
    sigmoid = 1.0 / (1.0 + jnp.exp(-gate))
    swish = gate * sigmoid
    act = (swish * up).astype(BF16)
    hidden[:, 2 * width :] = act
    hidden[:, 0:width] = (grad * up * sigmoid * (1.0 + gate * (1.0 - sigmoid))).astype(BF16)
    hidden[:, width : 2 * width] = (grad * swish).astype(BF16)
    share = jnp.sum(act.astype(F32) * grad, axis=1, keepdims=True)
    shape = (CAP, 128)
    same = lax.broadcasted_iota(jnp.int32, shape, 0) == lax.broadcasted_iota(jnp.int32, shape, 1)
    marks = jnp.zeros((TILE, 128), F32)
    for k in range(4):
        row = jnp.sum(
            jnp.where(same, share[k * CAP : (k + 1) * CAP, :], 0.0), axis=0, keepdims=True
        )
        marks += marked_rows(row, 3 * k)
    unit = 2 * CAP
    for j in (2, 1, 3, 0):
        kind = outs[j].dtype
        columns = slice(j * step, (j + 1) * step)
        out = nn(hidden[:, 2 * width :], down_weights[:, columns])
        back = nn(hidden[:, 0 : 2 * width], pair_weights[:, columns])
        for k in range(4):
            start, rows = k * unit, slice(k * CAP, (k + 1) * CAP)
            outs[j][start : start + CAP, :] = out[rows, :].astype(kind)
            outs[j][start + CAP : start + 2 * CAP, :] = back[rows, :].astype(kind)
        outs[j][4 * unit :, :] = jnp.zeros((TILE, step), kind)
        outs[j][4 * unit :, 0:128] = marks.astype(kind)


def total_kernel(place, own, one, three, *outs):
    unit = 2 * CAP

    def total(span, columns):
        value = own[span, columns] + one[span, columns].astype(F32)
        return value + three[span, columns].astype(F32)

    marks = total(slice(4 * unit, 4 * unit + TILE), slice(0, 128))
    width = own.shape[1]
    for k in range(4):
        outs[k][0:unit, :] = total(slice(k * unit, (k + 1) * unit), slice(0, width)).astype(BF16)
        row = jnp.sum(marks[3 * k : 3 * k + 3, :], axis=0, keepdims=True)
        outs[k][unit:, :] = jnp.zeros((TILE, width), BF16)
        outs[k][unit:, 0:128] = marked_rows(row, 0).astype(BF16)


def weight_kernel(place, joined, *refs):
    rows, keeps, sends, chosen = refs[0:4], refs[4:8], refs[8:12], refs[12]
    half = keeps[0].shape[1]
    for j in range(4):
        spot = lax.rem(j + (1 - 2 * place[4]) * (place[1] - place[2]) + 8, 4)
        for second in range(2):
            take_rows(chosen.at[second, spot], rows[j], second)
    for i in (2, 1, 3, 0):
        for m in range(3):
            columns = slice(2 * m * half, 2 * (m + 1) * half)
            total = tn(joined[:, columns], chosen[1 if m == 2 else 0, i])
            keeps[i][m] = total[0:half, :].astype(BF16)
            sends[i][m] = total[half:, :].astype(BF16)


def column(row):
    rows = row.shape[1]
    shape = (rows, rows)
    same = lax.broadcasted_iota(jnp.int32, shape, 0) == lax.broadcasted_iota(jnp.int32, shape, 1)
    return jnp.sum(jnp.where(same, row, 0.0), axis=1, keepdims=True)


def owner_kernel(place, small, placing, *refs):
    ids, probs = small.at[0:2], small.at[2:4]
    blocks, layer, token, prob = refs[0:4], *refs[4:7]
    total = jnp.zeros(layer.shape, F32)
    grads = jnp.zeros(token.shape, F32)
    shares = [jnp.zeros((1, ids.shape[1]), F32) for _ in range(2)]
    for k in range(4):
        one, two = expert_rows(place, ids, k)
        hot = placing[k * CAP : (k + 1) * CAP, :]
        weight = jnp.where(one, probs[0:1, :], 0.0) + jnp.where(two, probs[1:2, :], 0.0)
        total += column(weight) * tn(hot, blocks[k][0:CAP, :])
        grads += tn(hot, blocks[k][CAP : 2 * CAP, :])
        found = nn(blocks[k][2 * CAP :, 0:128][:, 0:CAP], hot)
        share = jnp.sum(found, axis=0, keepdims=True)
        shares[0] += jnp.where(one, share, 0.0)
        shares[1] += jnp.where(two, share, 0.0)
    layer[...] = total.astype(BF16)
    token[...] = grads.astype(BF16)
    prob[...] = jnp.zeros(prob.shape, F32)
    for n in range(2):
        prob[n : n + 1, :] = shares[n] / probs[n : n + 1, :]


def shift(value, axis, step):
    return lax.ppermute(value, axis, [(i, (i + step) % 4) for i in range(4)])


def relay(value, axis, sign=1):
    steps = [(c, i, (i + (-sign if c else sign)) % 4) for c in range(2) for i in range(4)]
    if axis == "x":
        return lax.ppermute(value, ("x", "core"), [(2 * i + c, 2 * j + c) for c, i, j in steps])
    return lax.ppermute(value, ("core", axis), [(4 * c + i, 4 * c + j) for c, i, j in steps])


def swap(value, axis):
    return lax.ppermute(value, axis, [(0, 1), (1, 0)])


def turn(value):
    return lax.ppermute(value, ("core", "zl"), [(2 * c + z, 2 * z + c) for c in range(2) for z in range(2)])


def body(tokens, expert_ids, gate_probs, stacked_weights, out_grad):
    rows, width = tokens.shape
    half = stacked_weights.shape[2]
    hidden = 2 * half
    slots = 4 * CAP
    place = jnp.stack(
        [lax.axis_index(name) for name in ("expert", "x", "y", "zl", "core")]
    ).astype(jnp.int32)
    small = jnp.concatenate([expert_ids.T.astype(F32), gate_probs.T])
    wide = jnp.concatenate([tokens, out_grad], axis=1)
    vmem = pl.BlockSpec(memory_space=pltpu.VMEM)
    hbm = pl.BlockSpec(memory_space=pl.ANY)

    placing, *blocks = call(
        slots_kernel,
        place,
        [small, wide],
        [((slots, rows), BF16)] + [((2 * CAP, width), BF16)] * 4,
    )

    blocks = [blocks[0]] + [shift(blocks[k], "expert", k) for k in (1, 2, 3)]
    own, blocks[0] = lax.optimization_barrier((stacked_weights[0], blocks[0]))
    turned = lax.ppermute(own, ("core", "zl"), [(1, 2), (2, 1)])
    own = jnp.where(place[4] == place[3], own, turned)
    near, back = relay(own, "x"), relay(own, "x", -1)
    own = [own, near, relay(near, "x"), back]
    blocks = [jnp.concatenate(blocks, axis=0)]
    near, back = relay(blocks[0], "y"), relay(blocks[0], "y", -1)
    own[0], own[1], own[3], near, back = lax.optimization_barrier(
        (own[0], own[1], own[3], near, back)
    )
    other = [swap(own[(4 - i) % 4], "core") for i in range(4)]
    blocks += [near, relay(near, "y"), back]

    def project(names, second):
        tall = len(names) * hidden
        return call(
            functools.partial(project_kernel, names, second),
            place,
            blocks + own + other,
            [((slots, tall), BF16), ((tall, 4 * width), BF16)],
            [pltpu.VMEM((slots, 4 * width), BF16), pltpu.SemaphoreType.DMA((4, 2, 2))],
            [vmem] * 4 + [hbm] * 8,
        )

    pair, pair_weights = project((0, 1), 0)
    pair_far = swap(pair, "zl")
    down, down_weights = project((2,), 1)
    down_far = swap(down, "zl")

    def halfway(passed, near, back):
        passed, near = lax.optimization_barrier((passed, near))
        return near.astype(BF16), (back + passed.astype(F32)).astype(BF16)

    unit = 2 * CAP + TILE
    shares = call(
        share_kernel,
        place,
        [pair, pair_far, down, down_far, pair_weights, down_weights],
        [((8 * CAP + TILE, width), F32)]
        + [((8 * CAP + TILE, width), BF16)] * 3
        + [((slots, 3 * hidden), BF16)],
    )
    passed = relay(shares[2], "y")
    terms = call(
        weight_kernel,
        place,
        [shares[4]] + blocks,
        [((3, half, width), BF16)] * 8,
        [pltpu.VMEM((2, 4, slots, width), BF16)],
    )
    keeps, sends = terms[0:4], terms[4:8]
    moved = [swap(sends[(4 - i) % 4], "core") for i in range(4)]
    near, back = halfway(passed, shares[1], shares[3])
    near, back, *moved = lax.optimization_barrier((near, back, *moved))
    arrived = [relay(near, "y", -1), relay(back, "y")]

    def both_cores(i):
        return keeps[i].astype(F32) + moved[i].astype(F32)

    passed = relay(both_cores(2).astype(BF16), "x")
    near, back = halfway(passed, both_cores(1), both_cores(3))
    far_sums = [relay(near, "x", -1), relay(back, "x")]
    totals = call(total_kernel, place, [shares[0]] + arrived, [((unit, width), BF16)] * 4)
    returned = [totals[0]] + [shift(totals[k], "expert", -k) for k in (1, 2, 3)]
    layer_output, token_grad, prob_grad = call(
        owner_kernel,
        place,
        [small, placing] + returned,
        [((rows, width), BF16), ((rows, width), BF16), ((8, rows), F32)],
    )
    weight_total = both_cores(0)
    for block in far_sums:
        weight_total = weight_total + block.astype(F32)
    weight_total = weight_total.astype(BF16).reshape(2, 3 * half // 2, width)
    parts = [turn(weight_total[n]) for n in range(2)]
    *parts, layer_output = lax.optimization_barrier((*parts, layer_output))
    weight_grad = jnp.concatenate([part.astype(F32) for part in parts])
    weight_grad = weight_grad.reshape(stacked_weights.shape)
    return layer_output, token_grad, prob_grad[0:2].T, weight_grad


def solution(mesh):
    split = Mesh(
        mesh.devices.reshape(4, 2, 4, 4, 2), ("x", "core", "expert", "y", "zl")
    )
    rows = P(("x", "core", "expert"), ("y", "zl"))
    pairs = P(("x", "core", "expert"), None)
    weights = P("expert", None, ("y", "zl"), ("x", "core"))
    return jax.shard_map(
        body,
        mesh=split,
        in_specs=(rows, pairs, pairs, weights, rows),
        out_specs=(rows, rows, pairs, weights),
        check_vma=False,
    )
```

```python
import functools

import functools

import jax
import jax.numpy as jnp
from jax import lax
from jax.experimental import pallas as pl
from jax.experimental.pallas import tpu as pltpu
from jax.sharding import Mesh, PartitionSpec as P

F32 = jnp.float32
BF16 = jnp.bfloat16
CAP = 80
TILE = 16
PARAMS = pltpu.CompilerParams(vmem_limit_bytes=48 * 1024 * 1024)


def nn(a, b):
    return lax.dot_general(a, b, (((1,), (0,)), ((), ())), preferred_element_type=F32)


def nt(a, b):
    return lax.dot_general(a, b, (((1,), (1,)), ((), ())), preferred_element_type=F32)


def tn(a, b):
    return lax.dot_general(a, b, (((0,), (0,)), ((), ())), preferred_element_type=F32)


def call(kernel, place, args, outs, scratch=(), spaces=None):
    whole = pl.BlockSpec(memory_space=pltpu.VMEM)
    return list(pl.pallas_call(
        kernel,
        out_shape=[jax.ShapeDtypeStruct(shape, kind) for shape, kind in outs],
        in_specs=[pl.BlockSpec(memory_space=pltpu.SMEM)] + (spaces or [whole] * len(args)),
        out_specs=[whole] * len(outs),
        scratch_shapes=list(scratch),
        compiler_params=PARAMS,
    )(place, *args))


def expert_rows(place, ids, k):
    expert = lax.rem(place[0] + k, 4).astype(F32)
    return ids[0:1, :] == expert, ids[1:2, :] == expert


def slots_kernel(place, small, wide, placing, *outs):
    ids, probs = small.at[0:2], small.at[2:4]
    width = wide.shape[1] // 2
    rows = ids.shape[1]
    before = (
        lax.broadcasted_iota(jnp.int32, (rows, rows), 0)
        < lax.broadcasted_iota(jnp.int32, (rows, rows), 1)
    ).astype(BF16)
    slot = lax.broadcasted_iota(jnp.int32, (CAP, rows), 0)
    scales = []
    for k in range(4):
        one, two = expert_rows(place, ids, k)
        named = jnp.logical_or(one, two)
        marks = jnp.broadcast_to(named, (8, rows)).astype(F32)
        position = nn(marks.astype(BF16), before)[0:1, :].astype(jnp.int32)
        weight = jnp.where(one, probs[0:1, :], probs[1:2, :])
        chosen = jnp.logical_and(
            jnp.broadcast_to(marks[0:1, :] > 0.5, (CAP, rows)),
            slot == jnp.broadcast_to(position, (CAP, rows)),
        )
        placing[k * CAP : (k + 1) * CAP, :] = chosen.astype(F32).astype(BF16)
        scales.append(jnp.sum(jnp.where(chosen, weight, 0.0), axis=1, keepdims=True))
    for k in range(4):
        hot = placing[k * CAP : (k + 1) * CAP, :]
        outs[k][0:CAP, :] = nn(hot, wide[:, 0:width]).astype(BF16)
        outs[k][CAP : 2 * CAP, :] = (scales[k] * nn(hot, wide[:, width:])).astype(BF16)


def fetch(own, other, joined, sems, names, place):
    half, width = own[0].shape[1:]
    copies = []
    for block in range(4):
        spot = lax.rem(block + (1 - 2 * place[4]) * (place[2] - place[1]) + 8, 4)
        columns = pl.ds(pl.multiple_of(spot * width, width), width)
        for n, m in enumerate(names):
            for h, source in enumerate((own[block], other[block])):
                copies.append(
                    pltpu.make_async_copy(
                        source.at[m],
                        joined.at[pl.ds((2 * n + h) * half, half), columns],
                        sems.at[block, n, h],
                    )
                )
    for copy in copies:
        copy.start()
    return copies


def take_rows(target, source, second):
    for k in range(4):
        first = (2 * k + second) * CAP
        target[k * CAP : (k + 1) * CAP, :] = source[first : first + CAP, :]


def project_kernel(names, second, place, *refs):
    rows, own, other = refs[0:4], refs[4:8], refs[8:12]
    out, joined, wide, sems = refs[12:16]
    width = rows[0].shape[1]
    copies = fetch(own, other, joined, sems, names, place)
    for j in range(4):
        take_rows(wide.at[:, pl.ds(j * width, width)], rows[j], second)
    for copy in copies:
        copy.wait()
    out[...] = nt(wide[...], joined[...]).astype(BF16)


def pieces(values):
    high = values.astype(BF16)
    rest = values - high.astype(F32)
    middle = rest.astype(BF16)
    low = (rest - middle.astype(F32)).astype(BF16)
    return high, middle, low


def marked_rows(row, first):
    spot = lax.broadcasted_iota(jnp.int32, (TILE, row.shape[1]), 0)
    total = jnp.zeros(spot.shape, F32)
    for n, part in enumerate(pieces(row)):
        total += jnp.where(spot == first + n, part.astype(F32), 0.0)
    return total


def share_kernel(place, pair, pair_far, down, down_far, pair_weights, down_weights, *refs):
    outs, hidden = refs[0:4], refs[4]
    width, step = down.shape[1], outs[0].shape[1]

    def both(near, far, n):
        columns = slice(n * width, (n + 1) * width)
        return near[:, columns].astype(F32) + far[:, columns].astype(F32)

    gate, up, grad = both(pair, pair_far, 0), both(pair, pair_far, 1), both(down, down_far, 0)
    sigmoid = 1.0 / (1.0 + jnp.exp(-gate))
    swish = gate * sigmoid
    act = (swish * up).astype(BF16)
    hidden[:, 2 * width :] = act
    hidden[:, 0:width] = (grad * up * sigmoid * (1.0 + gate * (1.0 - sigmoid))).astype(BF16)
    hidden[:, width : 2 * width] = (grad * swish).astype(BF16)
    share = jnp.sum(act.astype(F32) * grad, axis=1, keepdims=True)
    shape = (CAP, 128)
    same = lax.broadcasted_iota(jnp.int32, shape, 0) == lax.broadcasted_iota(jnp.int32, shape, 1)
    marks = jnp.zeros((TILE, 128), F32)
    for k in range(4):
        row = jnp.sum(
            jnp.where(same, share[k * CAP : (k + 1) * CAP, :], 0.0), axis=0, keepdims=True
        )
        marks += marked_rows(row, 3 * k)
    unit = 2 * CAP
    for j in (2, 1, 3, 0):
        kind = outs[j].dtype
        columns = slice(j * step, (j + 1) * step)
        out = nn(hidden[:, 2 * width :], down_weights[:, columns])
        back = nn(hidden[:, 0 : 2 * width], pair_weights[:, columns])
        for k in range(4):
            start, rows = k * unit, slice(k * CAP, (k + 1) * CAP)
            outs[j][start : start + CAP, :] = out[rows, :].astype(kind)
            outs[j][start + CAP : start + 2 * CAP, :] = back[rows, :].astype(kind)
        outs[j][4 * unit :, :] = jnp.zeros((TILE, step), kind)
        outs[j][4 * unit :, 0:128] = marks.astype(kind)


def total_kernel(place, own, one, three, *outs):
    unit = 2 * CAP

    def total(span, columns):
        value = own[span, columns] + one[span, columns].astype(F32)
        return value + three[span, columns].astype(F32)

    marks = total(slice(4 * unit, 4 * unit + TILE), slice(0, 128))
    width = own.shape[1]
    for k in range(4):
        outs[k][0:unit, :] = total(slice(k * unit, (k + 1) * unit), slice(0, width)).astype(BF16)
        row = jnp.sum(marks[3 * k : 3 * k + 3, :], axis=0, keepdims=True)
        outs[k][unit:, :] = jnp.zeros((TILE, width), BF16)
        outs[k][unit:, 0:128] = marked_rows(row, 0).astype(BF16)


def weight_kernel(place, joined, *refs):
    rows, keeps, sends, chosen = refs[0:4], refs[4:8], refs[8:12], refs[12]
    half = keeps[0].shape[1]
    for j in range(4):
        spot = lax.rem(j + (1 - 2 * place[4]) * (place[1] - place[2]) + 8, 4)
        for second in range(2):
            take_rows(chosen.at[second, spot], rows[j], second)
    for i in (2, 1, 3, 0):
        for m in range(3):
            columns = slice(2 * m * half, 2 * (m + 1) * half)
            total = tn(joined[:, columns], chosen[1 if m == 2 else 0, i])
            keeps[i][m] = total[0:half, :].astype(BF16)
            sends[i][m] = total[half:, :].astype(BF16)


def column(row):
    rows = row.shape[1]
    shape = (rows, rows)
    same = lax.broadcasted_iota(jnp.int32, shape, 0) == lax.broadcasted_iota(jnp.int32, shape, 1)
    return jnp.sum(jnp.where(same, row, 0.0), axis=1, keepdims=True)


def owner_kernel(place, small, placing, *refs):
    ids, probs = small.at[0:2], small.at[2:4]
    blocks, layer, token, prob = refs[0:4], *refs[4:7]
    total = jnp.zeros(layer.shape, F32)
    grads = jnp.zeros(token.shape, F32)
    shares = [jnp.zeros((1, ids.shape[1]), F32) for _ in range(2)]
    for k in range(4):
        one, two = expert_rows(place, ids, k)
        hot = placing[k * CAP : (k + 1) * CAP, :]
        weight = jnp.where(one, probs[0:1, :], 0.0) + jnp.where(two, probs[1:2, :], 0.0)
        total += column(weight) * tn(hot, blocks[k][0:CAP, :])
        grads += tn(hot, blocks[k][CAP : 2 * CAP, :])
        found = nn(blocks[k][2 * CAP :, 0:128][:, 0:CAP], hot)
        share = jnp.sum(found, axis=0, keepdims=True)
        shares[0] += jnp.where(one, share, 0.0)
        shares[1] += jnp.where(two, share, 0.0)
    layer[...] = total.astype(BF16)
    token[...] = grads.astype(BF16)
    prob[...] = jnp.zeros(prob.shape, F32)
    for n in range(2):
        prob[n : n + 1, :] = shares[n] / probs[n : n + 1, :]


def shift(value, axis, step):
    return lax.ppermute(value, axis, [(i, (i + step) % 4) for i in range(4)])


def relay(value, axis, sign=1):
    steps = [(c, i, (i + (-sign if c else sign)) % 4) for c in range(2) for i in range(4)]
    if axis == "x":
        return lax.ppermute(value, ("x", "core"), [(2 * i + c, 2 * j + c) for c, i, j in steps])
    return lax.ppermute(value, ("core", axis), [(4 * c + i, 4 * c + j) for c, i, j in steps])


def swap(value, axis):
    return lax.ppermute(value, axis, [(0, 1), (1, 0)])


def turn(value):
    return lax.ppermute(value, ("core", "zl"), [(2 * c + z, 2 * z + c) for c in range(2) for z in range(2)])


def body(tokens, expert_ids, gate_probs, stacked_weights, out_grad):
    rows, width = tokens.shape
    half = stacked_weights.shape[2]
    hidden = 2 * half
    slots = 4 * CAP
    place = jnp.stack(
        [lax.axis_index(name) for name in ("expert", "x", "y", "zl", "core")]
    ).astype(jnp.int32)
    small = jnp.concatenate([expert_ids.T.astype(F32), gate_probs.T])
    wide = jnp.concatenate([tokens, out_grad], axis=1)
    vmem = pl.BlockSpec(memory_space=pltpu.VMEM)
    hbm = pl.BlockSpec(memory_space=pl.ANY)

    placing, *blocks = call(
        slots_kernel,
        place,
        [small, wide],
        [((slots, rows), BF16)] + [((2 * CAP, width), BF16)] * 4,
    )

    blocks = [blocks[0]] + [shift(blocks[k], "expert", k) for k in (1, 2, 3)]
    own = stacked_weights[0]
    turned = lax.ppermute(own, ("core", "zl"), [(1, 2), (2, 1)])
    own = jnp.where(place[4] == place[3], own, turned)
    near, back = relay(own, "x"), relay(own, "x", -1)
    own = [own, near, relay(near, "x"), back]
    blocks = [jnp.concatenate(blocks, axis=0)]
    near, back = relay(blocks[0], "y"), relay(blocks[0], "y", -1)
    own[0], own[1], own[3], near, back = lax.optimization_barrier(
        (own[0], own[1], own[3], near, back)
    )
    other = [swap(own[(4 - i) % 4], "core") for i in range(4)]
    blocks += [near, relay(near, "y"), back]

    def project(names, second):
        tall = len(names) * hidden
        return call(
            functools.partial(project_kernel, names, second),
            place,
            blocks + own + other,
            [((slots, tall), BF16), ((tall, 4 * width), BF16)],
            [pltpu.VMEM((slots, 4 * width), BF16), pltpu.SemaphoreType.DMA((4, 2, 2))],
            [vmem] * 4 + [hbm] * 8,
        )

    pair, pair_weights = project((0, 1), 0)
    pair_far = swap(pair, "zl")
    down, down_weights = project((2,), 1)
    down_far = swap(down, "zl")

    def halfway(passed, near, back):
        passed, near = lax.optimization_barrier((passed, near))
        return near.astype(BF16), (back + passed.astype(F32)).astype(BF16)

    unit = 2 * CAP + TILE
    shares = call(
        share_kernel,
        place,
        [pair, pair_far, down, down_far, pair_weights, down_weights],
        [((8 * CAP + TILE, width), F32)]
        + [((8 * CAP + TILE, width), BF16)] * 3
        + [((slots, 3 * hidden), BF16)],
    )
    passed = relay(shares[2], "y")
    terms = call(
        weight_kernel,
        place,
        [shares[4]] + blocks,
        [((3, half, width), BF16)] * 8,
        [pltpu.VMEM((2, 4, slots, width), BF16)],
    )
    keeps, sends = terms[0:4], terms[4:8]
    moved = [swap(sends[(4 - i) % 4], "core") for i in range(4)]
    near, back = halfway(passed, shares[1], shares[3])
    near, back, *moved = lax.optimization_barrier((near, back, *moved))
    arrived = [relay(near, "y", -1), relay(back, "y")]

    def both_cores(i):
        return keeps[i].astype(F32) + moved[i].astype(F32)

    passed = relay(both_cores(2).astype(BF16), "x")
    near, back = halfway(passed, both_cores(1), both_cores(3))
    far_sums = [relay(near, "x", -1), relay(back, "x")]
    totals = call(total_kernel, place, [shares[0]] + arrived, [((unit, width), BF16)] * 4)
    returned = [totals[0]] + [shift(totals[k], "expert", -k) for k in (1, 2, 3)]
    layer_output, token_grad, prob_grad = call(
        owner_kernel,
        place,
        [small, placing] + returned,
        [((rows, width), BF16), ((rows, width), BF16), ((8, rows), F32)],
    )
    weight_total = both_cores(0)
    for block in far_sums:
        weight_total = weight_total + block.astype(F32)
    weight_total = weight_total.astype(BF16).reshape(2, 3 * half // 2, width)
    parts = [turn(weight_total[n]) for n in range(2)]
    *parts, layer_output = lax.optimization_barrier((*parts, layer_output))
    weight_grad = jnp.concatenate([part.astype(F32) for part in parts])
    weight_grad = weight_grad.reshape(stacked_weights.shape)
    return layer_output, token_grad, prob_grad[0:2].T, weight_grad


def solution(mesh):
    split = Mesh(
        mesh.devices.reshape(4, 2, 4, 4, 2), ("x", "core", "expert", "y", "zl")
    )
    rows = P(("x", "core", "expert"), ("y", "zl"))
    pairs = P(("x", "core", "expert"), None)
    weights = P("expert", None, ("y", "zl"), ("x", "core"))
    return jax.shard_map(
        body,
        mesh=split,
        in_specs=(rows, pairs, pairs, weights, rows),
        out_specs=(rows, rows, pairs, weights),
        check_vma=False,
    )
```

```python
import functools

import functools

import jax
import jax.numpy as jnp
from jax import lax
from jax.experimental import pallas as pl
from jax.experimental.pallas import tpu as pltpu
from jax.sharding import Mesh, PartitionSpec as P

F32 = jnp.float32
BF16 = jnp.bfloat16
CAP = 80
TILE = 16
PARAMS = pltpu.CompilerParams(vmem_limit_bytes=48 * 1024 * 1024)


def nn(a, b):
    return lax.dot_general(a, b, (((1,), (0,)), ((), ())), preferred_element_type=F32)


def nt(a, b):
    return lax.dot_general(a, b, (((1,), (1,)), ((), ())), preferred_element_type=F32)


def tn(a, b):
    return lax.dot_general(a, b, (((0,), (0,)), ((), ())), preferred_element_type=F32)


def call(kernel, place, args, outs, scratch=(), spaces=None):
    whole = pl.BlockSpec(memory_space=pltpu.VMEM)
    return list(pl.pallas_call(
        kernel,
        out_shape=[jax.ShapeDtypeStruct(shape, kind) for shape, kind in outs],
        in_specs=[pl.BlockSpec(memory_space=pltpu.SMEM)] + (spaces or [whole] * len(args)),
        out_specs=[whole] * len(outs),
        scratch_shapes=list(scratch),
        compiler_params=PARAMS,
    )(place, *args))


def expert_rows(place, ids, k):
    expert = lax.rem(place[0] + k, 4).astype(F32)
    return ids[0:1, :] == expert, ids[1:2, :] == expert


def slots_kernel(place, small, wide, placing, *outs):
    ids, probs = small.at[0:2], small.at[2:4]
    width = wide.shape[1] // 2
    rows = ids.shape[1]
    before = (
        lax.broadcasted_iota(jnp.int32, (rows, rows), 0)
        < lax.broadcasted_iota(jnp.int32, (rows, rows), 1)
    ).astype(BF16)
    slot = lax.broadcasted_iota(jnp.int32, (CAP, rows), 0)
    scales = []
    for k in range(4):
        one, two = expert_rows(place, ids, k)
        named = jnp.logical_or(one, two)
        marks = jnp.broadcast_to(named, (8, rows)).astype(F32)
        position = nn(marks.astype(BF16), before)[0:1, :].astype(jnp.int32)
        weight = jnp.where(one, probs[0:1, :], probs[1:2, :])
        chosen = jnp.logical_and(
            jnp.broadcast_to(marks[0:1, :] > 0.5, (CAP, rows)),
            slot == jnp.broadcast_to(position, (CAP, rows)),
        )
        placing[k * CAP : (k + 1) * CAP, :] = chosen.astype(F32).astype(BF16)
        scales.append(jnp.sum(jnp.where(chosen, weight, 0.0), axis=1, keepdims=True))
    for k in range(4):
        hot = placing[k * CAP : (k + 1) * CAP, :]
        outs[k][0:CAP, :] = nn(hot, wide[:, 0:width]).astype(BF16)
        outs[k][CAP : 2 * CAP, :] = (scales[k] * nn(hot, wide[:, width:])).astype(BF16)


def fetch(own, other, joined, sems, names, place):
    half, width = own[0].shape[1:]
    copies = []
    for block in range(4):
        spot = lax.rem(block + (1 - 2 * place[4]) * (place[2] - place[1]) + 8, 4)
        columns = pl.ds(pl.multiple_of(spot * width, width), width)
        for n, m in enumerate(names):
            for h, source in enumerate((own[block], other[block])):
                copies.append(
                    pltpu.make_async_copy(
                        source.at[m],
                        joined.at[pl.ds((2 * n + h) * half, half), columns],
                        sems.at[block, n, h],
                    )
                )
    for copy in copies:
        copy.start()
    return copies


def take_rows(target, source, second):
    for k in range(4):
        first = (2 * k + second) * CAP
        target[k * CAP : (k + 1) * CAP, :] = source[first : first + CAP, :]


def project_kernel(names, second, place, *refs):
    rows, own, other = refs[0:4], refs[4:8], refs[8:12]
    out, joined, wide, sems = refs[12:16]
    width = rows[0].shape[1]
    copies = fetch(own, other, joined, sems, names, place)
    for j in range(4):
        take_rows(wide.at[:, pl.ds(j * width, width)], rows[j], second)
    for copy in copies:
        copy.wait()
    out[...] = nt(wide[...], joined[...]).astype(BF16)


def pieces(values):
    high = values.astype(BF16)
    rest = values - high.astype(F32)
    middle = rest.astype(BF16)
    low = (rest - middle.astype(F32)).astype(BF16)
    return high, middle, low


def marked_rows(row, first):
    spot = lax.broadcasted_iota(jnp.int32, (TILE, row.shape[1]), 0)
    total = jnp.zeros(spot.shape, F32)
    for n, part in enumerate(pieces(row)):
        total += jnp.where(spot == first + n, part.astype(F32), 0.0)
    return total


def share_kernel(place, pair, pair_far, down, down_far, pair_weights, down_weights, *refs):
    outs, hidden = refs[0:4], refs[4]
    width, step = down.shape[1], outs[0].shape[1]

    def both(near, far, n):
        columns = slice(n * width, (n + 1) * width)
        return near[:, columns].astype(F32) + far[:, columns].astype(F32)

    gate, up, grad = both(pair, pair_far, 0), both(pair, pair_far, 1), both(down, down_far, 0)
    sigmoid = 1.0 / (1.0 + jnp.exp(-gate))
    swish = gate * sigmoid
    act = (swish * up).astype(BF16)
    hidden[:, 2 * width :] = act
    hidden[:, 0:width] = (grad * up * sigmoid * (1.0 + gate * (1.0 - sigmoid))).astype(BF16)
    hidden[:, width : 2 * width] = (grad * swish).astype(BF16)
    share = jnp.sum(act.astype(F32) * grad, axis=1, keepdims=True)
    shape = (CAP, 128)
    same = lax.broadcasted_iota(jnp.int32, shape, 0) == lax.broadcasted_iota(jnp.int32, shape, 1)
    marks = jnp.zeros((TILE, 128), F32)
    for k in range(4):
        row = jnp.sum(
            jnp.where(same, share[k * CAP : (k + 1) * CAP, :], 0.0), axis=0, keepdims=True
        )
        marks += marked_rows(row, 3 * k)
    unit = 2 * CAP
    for j in (2, 1, 3, 0):
        kind = outs[j].dtype
        columns = slice(j * step, (j + 1) * step)
        out = nn(hidden[:, 2 * width :], down_weights[:, columns])
        back = nn(hidden[:, 0 : 2 * width], pair_weights[:, columns])
        for k in range(4):
            start, rows = k * unit, slice(k * CAP, (k + 1) * CAP)
            outs[j][start : start + CAP, :] = out[rows, :].astype(kind)
            outs[j][start + CAP : start + 2 * CAP, :] = back[rows, :].astype(kind)
        outs[j][4 * unit :, :] = jnp.zeros((TILE, step), kind)
        outs[j][4 * unit :, 0:128] = marks.astype(kind)


def total_kernel(place, own, one, three, *outs):
    unit = 2 * CAP

    def total(span, columns):
        value = own[span, columns] + one[span, columns].astype(F32)
        return value + three[span, columns].astype(F32)

    marks = total(slice(4 * unit, 4 * unit + TILE), slice(0, 128))
    width = own.shape[1]
    for k in range(4):
        outs[k][0:unit, :] = total(slice(k * unit, (k + 1) * unit), slice(0, width)).astype(BF16)
        row = jnp.sum(marks[3 * k : 3 * k + 3, :], axis=0, keepdims=True)
        outs[k][unit:, :] = jnp.zeros((TILE, width), BF16)
        outs[k][unit:, 0:128] = marked_rows(row, 0).astype(BF16)


def weight_kernel(place, joined, *refs):
    rows, keeps, sends, chosen = refs[0:4], refs[4:8], refs[8:12], refs[12]
    half = keeps[0].shape[1]
    for j in range(4):
        spot = lax.rem(j + (1 - 2 * place[4]) * (place[1] - place[2]) + 8, 4)
        for second in range(2):
            take_rows(chosen.at[second, spot], rows[j], second)
    for i in (2, 1, 3, 0):
        for m in range(3):
            columns = slice(2 * m * half, 2 * (m + 1) * half)
            total = tn(joined[:, columns], chosen[1 if m == 2 else 0, i])
            keeps[i][m] = total[0:half, :].astype(BF16)
            sends[i][m] = total[half:, :].astype(BF16)


def column(row):
    rows = row.shape[1]
    shape = (rows, rows)
    same = lax.broadcasted_iota(jnp.int32, shape, 0) == lax.broadcasted_iota(jnp.int32, shape, 1)
    return jnp.sum(jnp.where(same, row, 0.0), axis=1, keepdims=True)


def owner_kernel(place, small, placing, *refs):
    ids, probs = small.at[0:2], small.at[2:4]
    blocks, layer, token, prob = refs[0:4], *refs[4:7]
    total = jnp.zeros(layer.shape, F32)
    grads = jnp.zeros(token.shape, F32)
    shares = [jnp.zeros((1, ids.shape[1]), F32) for _ in range(2)]
    for k in range(4):
        one, two = expert_rows(place, ids, k)
        hot = placing[k * CAP : (k + 1) * CAP, :]
        weight = jnp.where(one, probs[0:1, :], 0.0) + jnp.where(two, probs[1:2, :], 0.0)
        total += column(weight) * tn(hot, blocks[k][0:CAP, :])
        grads += tn(hot, blocks[k][CAP : 2 * CAP, :])
        found = nn(blocks[k][2 * CAP :, 0:128][:, 0:CAP], hot)
        share = jnp.sum(found, axis=0, keepdims=True)
        shares[0] += jnp.where(one, share, 0.0)
        shares[1] += jnp.where(two, share, 0.0)
    layer[...] = total.astype(BF16)
    token[...] = grads.astype(BF16)
    prob[...] = jnp.zeros(prob.shape, F32)
    for n in range(2):
        prob[n : n + 1, :] = shares[n] / probs[n : n + 1, :]


def shift(value, axis, step):
    return lax.ppermute(value, axis, [(i, (i + step) % 4) for i in range(4)])


def relay(value, axis, sign=1):
    steps = [(c, i, (i + (-sign if c else sign)) % 4) for c in range(2) for i in range(4)]
    if axis == "x":
        return lax.ppermute(value, ("x", "core"), [(2 * i + c, 2 * j + c) for c, i, j in steps])
    return lax.ppermute(value, ("core", axis), [(4 * c + i, 4 * c + j) for c, i, j in steps])


def swap(value, axis):
    return lax.ppermute(value, axis, [(0, 1), (1, 0)])


def turn(value):
    return lax.ppermute(value, ("core", "zl"), [(2 * c + z, 2 * z + c) for c in range(2) for z in range(2)])


def body(tokens, expert_ids, gate_probs, stacked_weights, out_grad):
    rows, width = tokens.shape
    half = stacked_weights.shape[2]
    hidden = 2 * half
    slots = 4 * CAP
    place = jnp.stack(
        [lax.axis_index(name) for name in ("expert", "x", "y", "zl", "core")]
    ).astype(jnp.int32)
    small = jnp.concatenate([expert_ids.T.astype(F32), gate_probs.T])
    wide = jnp.concatenate([tokens, out_grad], axis=1)
    vmem = pl.BlockSpec(memory_space=pltpu.VMEM)
    hbm = pl.BlockSpec(memory_space=pl.ANY)

    placing, *blocks = call(
        slots_kernel,
        place,
        [small, wide],
        [((slots, rows), BF16)] + [((2 * CAP, width), BF16)] * 4,
    )

    blocks = [blocks[0]] + [shift(blocks[k], "expert", k) for k in (1, 2, 3)]
    own, blocks[0] = lax.optimization_barrier((stacked_weights[0], blocks[0]))
    turned = lax.ppermute(own, ("core", "zl"), [(1, 2), (2, 1)])
    own = jnp.where(place[4] == place[3], own, turned)
    near, back = relay(own, "x"), relay(own, "x", -1)
    own = [own, near, relay(near, "x"), back]
    blocks = [jnp.concatenate(blocks, axis=0)]
    near, back = relay(blocks[0], "y"), relay(blocks[0], "y", -1)
    own[0], own[1], own[3], near, back = lax.optimization_barrier(
        (own[0], own[1], own[3], near, back)
    )
    other = [swap(own[(4 - i) % 4], "core") for i in range(4)]
    blocks += [near, relay(near, "y"), back]

    def project(names, second):
        tall = len(names) * hidden
        return call(
            functools.partial(project_kernel, names, second),
            place,
            blocks + own + other,
            [((slots, tall), BF16), ((tall, 4 * width), BF16)],
            [pltpu.VMEM((slots, 4 * width), BF16), pltpu.SemaphoreType.DMA((4, 2, 2))],
            [vmem] * 4 + [hbm] * 8,
        )

    pair, pair_weights = project((0, 1), 0)
    pair_far = swap(pair, "zl")
    down, down_weights = project((2,), 1)
    down_far = swap(down, "zl")

    def halfway(passed, near, back):
        passed, near = lax.optimization_barrier((passed, near))
        return near.astype(BF16), (back + passed.astype(F32)).astype(BF16)

    unit = 2 * CAP + TILE
    shares = call(
        share_kernel,
        place,
        [pair, pair_far, down, down_far, pair_weights, down_weights],
        [((8 * CAP + TILE, width), F32)]
        + [((8 * CAP + TILE, width), BF16)] * 3
        + [((slots, 3 * hidden), BF16)],
    )
    passed = relay(shares[2], "y")
    terms = call(
        weight_kernel,
        place,
        [shares[4]] + blocks,
        [((3, half, width), BF16)] * 8,
        [pltpu.VMEM((2, 4, slots, width), BF16)],
    )
    keeps, sends = terms[0:4], terms[4:8]
    moved = [swap(sends[(4 - i) % 4], "core") for i in range(4)]
    near, back = halfway(passed, shares[1], shares[3])
    near, back, *moved = lax.optimization_barrier((near, back, *moved))
    arrived = [relay(near, "y", -1), relay(back, "y")]

    def both_cores(i):
        return keeps[i].astype(F32) + moved[i].astype(F32)

    passed = relay(both_cores(2).astype(BF16), "x")
    near = both_cores(1).astype(BF16)
    back = (both_cores(3) + passed.astype(F32)).astype(BF16)
    far_sums = [relay(near, "x", -1), relay(back, "x")]
    totals = call(total_kernel, place, [shares[0]] + arrived, [((unit, width), BF16)] * 4)
    returned = [totals[0]] + [shift(totals[k], "expert", -k) for k in (1, 2, 3)]
    layer_output, token_grad, prob_grad = call(
        owner_kernel,
        place,
        [small, placing] + returned,
        [((rows, width), BF16), ((rows, width), BF16), ((8, rows), F32)],
    )
    weight_total = both_cores(0)
    for block in far_sums:
        weight_total = weight_total + block.astype(F32)
    weight_total = weight_total.astype(BF16).reshape(2, 3 * half // 2, width)
    parts = [turn(weight_total[n]) for n in range(2)]
    *parts, layer_output = lax.optimization_barrier((*parts, layer_output))
    weight_grad = jnp.concatenate([part.astype(F32) for part in parts])
    weight_grad = weight_grad.reshape(stacked_weights.shape)
    return layer_output, token_grad, prob_grad[0:2].T, weight_grad


def solution(mesh):
    split = Mesh(
        mesh.devices.reshape(4, 2, 4, 4, 2), ("x", "core", "expert", "y", "zl")
    )
    rows = P(("x", "core", "expert"), ("y", "zl"))
    pairs = P(("x", "core", "expert"), None)
    weights = P("expert", None, ("y", "zl"), ("x", "core"))
    return jax.shard_map(
        body,
        mesh=split,
        in_specs=(rows, pairs, pairs, weights, rows),
        out_specs=(rows, rows, pairs, weights),
        check_vma=False,
    )
```
